32 devices in a mesh: fsdp: 8 (over z, y), dp: 4 (over x, core).
Axes of the slice: x: 2, y: 2, z: 4, core: 2. Of those that a mesh axis runs over, the one named last changes fastest.
Arguments:
- tokens: bfloat16 [65536, 384], P(('fsdp', 'dp')), may hold values from -6 to 6
- cotangent: bfloat16 [65536, 384], P(('fsdp', 'dp')), may hold values from -6 to 6
- size_group: int32 [256], replicated, may hold values from 0 to 2
- assignment: int32 [256], replicated, may hold values from 0 to 31, as said below
- ln1_gain: bfloat16 [384], P('fsdp'), may hold values from 0.5 to 1.5
- ln1_bias: bfloat16 [384], P('fsdp'), may hold values from -2 to 2
- w_qkv: bfloat16 [442368], P('fsdp'), may hold values from -0.4375 to 0.4375
- q_bias: bfloat16 [384], P('fsdp'), may hold values from -3 to 3
- v_bias: bfloat16 [384], P('fsdp'), may hold values from -3 to 3
- w_proj: bfloat16 [147456], P('fsdp'), may hold values from -1.25 to 1.25
- proj_bias: bfloat16 [384], P('fsdp'), may hold values from -2 to 2
- ln2_gain: bfloat16 [384], P('fsdp'), may hold values from 0.5 to 1.5
- ln2_bias: bfloat16 [384], P('fsdp'), may hold values from -2 to 2
- w_up: bfloat16 [589824], P('fsdp'), may hold values from -0.3125 to 0.3125
- up_bias: bfloat16 [1536], P('fsdp'), may hold values from -3 to 3
- w_down: bfloat16 [589824], P('fsdp'), may hold values from -0.21875 to 0.21875
- down_bias: bfloat16 [384], P('fsdp'), may hold values from -2 to 2
Outputs:
- layer_out: bfloat16 [65536, 384], P(('fsdp', 'dp'))
- input_grad: bfloat16 [65536, 384], P(('fsdp', 'dp'))
- grad_ln1_gain: float32 [384], P('fsdp')
- grad_ln1_bias: float32 [384], P('fsdp')
- grad_w_qkv: float32 [442368], P('fsdp')
- grad_q_bias: float32 [384], P('fsdp')
- grad_v_bias: float32 [384], P('fsdp')
- grad_w_proj: float32 [147456], P('fsdp')
- grad_proj_bias: float32 [384], P('fsdp')
- grad_ln2_gain: float32 [384], P('fsdp')
- grad_ln2_bias: float32 [384], P('fsdp')
- grad_w_up: float32 [589824], P('fsdp')
- grad_up_bias: float32 [1536], P('fsdp')
- grad_w_down: float32 [589824], P('fsdp')
- grad_down_bias: float32 [384], P('fsdp')
The draws below stay inside these ranges and needn't reach their ends.
Inputs may be any that keep to these rules, and one draw needn't show every extreme that they name: `assignment`: every device receives exactly 8 images whose tokens number at most 2048, and some device holds exactly 2048; a device's rows of tokens and cotangent hold its images in increasing image order from its first row, then unused rows.
All inputs are finite; a program needn't handle non-finite values.
Results may differ from the reference program's by a relative error of at most 0.014.
The reference program's roundings to bfloat16 on the way count: a program that leaves them out, or rounds other values in their place, can miss the bound.
Values may be sent and summed in bfloat16 or wider, within the bound.
No kernel may reach another device: no remote copies, remote signals or barrier semaphores. Data moves between devices by JAX's collectives and lax.ppermute only.
A program may use at most 256 MiB of HBM per device.

```python
import math
from functools import partial
import jax
import jax.numpy as jnp
from jax import lax

D = 384
HEADS = 4
HEAD_DIM = 96
FF = 1536
LEN_S = 196
LEN_M = 256
LEN_L = 400
GROUPS_DEV = 2
IMG_DEV = 8
CAP = 2048
IMAGES = 256
ROWS = 65536
N_FSDP = 8
N_DP = 4


def image_layout(key):
    patterns = jnp.array([[2, 0, 0, 0], [1, 1, 1, 1], [1, 1, 1, 0], [1, 1, 0, 0], [1, 0, 0, 0], [0, 0, 0, 0]], dtype=jnp.int32)
    devices = IMAGES // IMG_DEV
    quads = IMAGES // 4
    key_pattern, key_device, key_order = jax.random.split(key, 3)
    chosen = jax.random.randint(key_pattern, (quads,), 0, 6)
    owners = jnp.arange(quads, dtype=jnp.int32) // GROUPS_DEV
    filled = jax.random.randint(key_device, (), 0, devices)
    chosen = jnp.where(owners == filled, 1, chosen)
    slot_group = jnp.take(patterns, chosen, axis=0).reshape(-1)
    slot_owner = jnp.repeat(owners, 4)
    shuffled = jax.random.permutation(key_order, quads * 4)
    group_ids = jnp.zeros(quads * 4, jnp.int32).at[shuffled].set(slot_group)
    owner_ids = jnp.zeros(quads * 4, jnp.int32).at[shuffled].set(slot_owner)
    return (group_ids, owner_ids)


def draw_size_group(key, part):
    return image_layout(key)[0]


def draw_assignment(key, part):
    return image_layout(key)[1]


def shard_levels(key, shape, cuts, low, high):
    factor_of = 1.0
    for axis_at, blocks in cuts:
        steps = jax.random.uniform(jax.random.fold_in(jax.random.fold_in(key, 6), axis_at), (blocks,), jnp.float32, low / len(cuts), high / len(cuts))
        factor_of = factor_of * jnp.repeat(jnp.exp(steps), shape[axis_at] // blocks).reshape((-1,) + (1,) * (len(shape) - 1 - axis_at))
    return factor_of


def gaussian(stream_key, shape, scale, bound, shards=(), held_as=jnp.bfloat16):
    level = shard_levels(stream_key, shape, shards, -0.22, 0.18) if shards else 1.0
    result = jax.random.normal(stream_key, shape, jnp.float32) * scale * level
    return jnp.minimum(jnp.maximum(result, -bound), bound).astype(held_as)


def setup_inputs(seed: int = 0) -> dict:
    arg_keys = jax.random.split(jax.random.key(seed), 18)
    tokens = gaussian(arg_keys[0], (ROWS, D), 1.0, 6.0, ((0, 32),))
    cotangent = gaussian(arg_keys[1], (ROWS, D), 1.0, 6.0, ((0, 32),))
    size_group = draw_size_group(jax.random.fold_in(arg_keys[17], 71), 0)
    assignment = draw_assignment(jax.random.fold_in(arg_keys[17], 71), 0)
    ln1_gain = jnp.clip(1.0 + 0.1 * jax.random.normal(arg_keys[4], (D,), jnp.float32), 0.5, 1.5).astype(jnp.bfloat16)
    ln1_bias = gaussian(arg_keys[5], (D,), 0.3, 2.0, ((0, 8),))
    w_qkv = gaussian(arg_keys[6], (3 * D * D,), (D // 2) ** -0.5, 0.4375, ((0, 8),))
    q_bias = gaussian(arg_keys[7], (D,), 0.5, 3.0, ((0, 8),))
    v_bias = gaussian(arg_keys[8], (D,), 0.5, 3.0, ((0, 8),))
    w_proj = gaussian(arg_keys[9], (D * D,), (D // 16) ** -0.5, 1.25, ((0, 8),))
    proj_bias = gaussian(arg_keys[10], (D,), 0.3, 2.0, ((0, 8),))
    ln2_gain = jnp.clip(1.0 + 0.1 * jax.random.normal(arg_keys[11], (D,), jnp.float32), 0.5, 1.5).astype(jnp.bfloat16)
    ln2_bias = gaussian(arg_keys[12], (D,), 0.3, 2.0, ((0, 8),))
    w_up = gaussian(arg_keys[13], (D * FF,), D ** -0.5, 0.3125, ((0, 8),))
    up_bias = gaussian(arg_keys[14], (FF,), 0.5, 3.0, ((0, 8),))
    w_down = gaussian(arg_keys[15], (FF * D,), (FF // 2) ** -0.5, 0.21875, ((0, 8),))
    down_bias = gaussian(arg_keys[16], (D,), 0.3, 2.0, ((0, 8),))
    return dict(tokens=tokens, cotangent=cotangent, size_group=size_group, assignment=assignment, ln1_gain=ln1_gain, ln1_bias=ln1_bias, w_qkv=w_qkv, q_bias=q_bias, v_bias=v_bias, w_proj=w_proj, proj_bias=proj_bias, ln2_gain=ln2_gain, ln2_bias=ln2_bias, w_up=w_up, up_bias=up_bias, w_down=w_down, down_bias=down_bias)


@jax.custom_vjp
def low(v):
    return lax.optimization_barrier(v.astype(jnp.bfloat16)).astype(jnp.float32)

@jax.custom_vjp
def low_back(v):
    return v

def low_keep(v):
    return (low(v), None)

def low_pass(kept, grad):
    return (grad,)

def back_keep(v):
    return (v, None)

def back_low(kept, grad):
    return (low(grad),)
low.defvjp(low_keep, low_pass)
low_back.defvjp(back_keep, back_low)

def row_layout(size_group, assignment, device, rows_cap):
    lengths = jnp.where(size_group == 0, LEN_S, jnp.where(size_group == 1, LEN_M, LEN_L)).astype(jnp.int32)
    owned_mask = (assignment == device).astype(jnp.int32)
    image_ends = jnp.cumsum(lengths * owned_mask).astype(jnp.int32)
    positions = jnp.arange(rows_cap, dtype=jnp.int32)
    finished = (image_ends[None, :] <= positions[:, None]) & (owned_mask[None, :] == 1)
    segment = lax.optimization_barrier(jnp.sum(finished.astype(jnp.int32), axis=1)).astype(jnp.int32)
    valid_rows = (positions < image_ends[-1]).astype(jnp.float32)
    return (segment, valid_rows)

def highest(former, latter):
    return jnp.dot(former, latter, precision=lax.Precision.HIGHEST, preferred_element_type=jnp.float32)

def normalize(values, gain, shift):
    center = values - lax.optimization_barrier(jnp.mean(values, axis=-1, keepdims=True))
    variance = lax.optimization_barrier(jnp.mean(center * center, axis=-1, keepdims=True))
    return center * lax.rsqrt(variance + 1e-06) * gain + shift

def attend(packed):
    qkv_rows, segment = packed
    score_scale = 1.0 / math.sqrt(HEAD_DIM)
    queries = qkv_rows[:, :D].reshape(-1, HEADS, HEAD_DIM)
    keys_all = qkv_rows[:, D:2 * D].reshape(-1, HEADS, HEAD_DIM)
    values_all = qkv_rows[:, 2 * D:].reshape(-1, HEADS, HEAD_DIM)
    scores = jnp.einsum('qhd,khd->hqk', queries, keys_all, precision=lax.Precision.HIGHEST) * score_scale
    same_image = segment[:, None] == segment[None, :]
    scores = low_back(jnp.where(same_image[None], scores, -1e+30))
    probs_low = low(jax.nn.softmax(scores, axis=-1))
    mixed_rows = jnp.einsum('hqk,khd->qhd', probs_low, values_all, precision=lax.Precision.HIGHEST)
    return mixed_rows.reshape(-1, D)

def forward(rows_in, weights, segments, valid_rows):
    ln1_gain, ln1_bias, w_qkv, q_bias, v_bias, w_proj, proj_bias, ln2_gain, ln2_bias, w_up, up_bias, w_down, down_bias = weights
    normed = low(normalize(rows_in, ln1_gain, ln1_bias))
    bias_full = jnp.concatenate([q_bias, jnp.zeros_like(q_bias), v_bias])
    qkv_rows = low(low_back(highest(normed, w_qkv.reshape(D, 3 * D))) + bias_full)
    mixed_rows = lax.map(jax.checkpoint(attend), (qkv_rows.reshape(N_FSDP * N_DP, CAP, 3 * D), segments))
    attn_rows = low(low_back(mixed_rows.reshape(-1, D)))
    residual = rows_in + low_back(highest(attn_rows, w_proj.reshape(D, D))) + proj_bias
    normed_two = low(normalize(residual, ln2_gain, ln2_bias))
    preact = low_back(highest(normed_two, w_up.reshape(D, FF))) + up_bias
    active = low(jax.nn.gelu(preact, approximate=False))
    output = residual + low_back(highest(active, w_down.reshape(FF, D))) + down_bias
    return output * valid_rows[:, None]

def reference(tokens, cotangent, size_group, assignment, ln1_gain, ln1_bias, w_qkv, q_bias, v_bias, w_proj, proj_bias, ln2_gain, ln2_bias, w_up, up_bias, w_down, down_bias):

    def layout_of(device):
        return row_layout(size_group, assignment, device, CAP)
    segments, valid_rows = lax.map(layout_of, jnp.arange(N_FSDP * N_DP, dtype=jnp.int32))
    valid_rows = valid_rows.reshape(-1)
    weights = tuple((item.astype(jnp.float32) for item in (ln1_gain, ln1_bias, w_qkv, q_bias, v_bias, w_proj, proj_bias, ln2_gain, ln2_bias, w_up, up_bias, w_down, down_bias)))
    lifted = tokens.astype(jnp.float32)
    output, pullback = jax.vjp(partial(forward, segments=segments, valid_rows=valid_rows), lifted, weights)
    grad_rows, grad_weights = pullback(cotangent.astype(jnp.float32))
    grad_ln1_gain, grad_ln1_bias, grad_w_qkv, grad_q_bias, grad_v_bias, grad_w_proj, grad_proj_bias, grad_ln2_gain, grad_ln2_bias, grad_w_up, grad_up_bias, grad_w_down, grad_down_bias = grad_weights
    return (output.astype(jnp.bfloat16), grad_rows.astype(jnp.bfloat16), grad_ln1_gain, grad_ln1_bias, grad_w_qkv, grad_q_bias, grad_v_bias, grad_w_proj, grad_proj_bias, grad_ln2_gain, grad_ln2_bias, grad_w_up, grad_up_bias, grad_w_down, grad_down_bias)
```

```python
from functools import partial
import math

import jax
import jax.numpy as jnp
from jax import lax
from jax.experimental import pallas as pl
from jax.experimental.pallas import tpu as pltpu
from jax.sharding import PartitionSpec as P

HEAD_DIM = 96
HEAD_PAD = 128
LENS = (196, 256, 400)
SLOT = 400
ROW_PAD = 32
VEC = 128
SCALE = 1.0 / math.sqrt(HEAD_DIM)
EXP_SCALE = SCALE * math.log2(math.e)
VMEM_LIMIT = 56 * 1024 * 1024
F32 = jnp.float32
BF16 = jnp.bfloat16


def dot_nn(a, b):
    return lax.dot_general(a, b, (((1,), (0,)), ((), ())), preferred_element_type=F32)


def dot_nt(a, b):
    return lax.dot_general(a, b, (((1,), (1,)), ((), ())), preferred_element_type=F32)


def dot_tn(a, b):
    return lax.dot_general(a, b, (((0,), (0,)), ((), ())), preferred_element_type=F32)


def pad_heads(values):
    rows, cols = values.shape
    gap = jnp.zeros((rows, HEAD_PAD - HEAD_DIM), values.dtype)
    parts = []
    for h in range(cols // HEAD_DIM):
        parts += [values[:, h * HEAD_DIM : (h + 1) * HEAD_DIM], gap]
    return jnp.concatenate(parts, axis=1)


def unpad_heads(values):
    rows, cols = values.shape
    return jnp.concatenate(
        [values[:, h * HEAD_PAD : h * HEAD_PAD + HEAD_DIM] for h in range(cols // HEAD_PAD)], axis=1
    )


def row_norm(x):
    center = x - jnp.mean(x, axis=-1, keepdims=True)
    inverse = lax.rsqrt(jnp.mean(center * center, axis=-1, keepdims=True) + 1e-6)
    return center * inverse, inverse


def row_norm_back(e, xhat, inverse):
    return inverse * (
        e - jnp.mean(e, axis=-1, keepdims=True) - xhat * jnp.mean(e * xhat, axis=-1, keepdims=True)
    )


def load_rows(ref, start, count):
    base = pl.multiple_of((start // 8) * 8, 8)
    window = ref[pl.ds(base, count + 8), :]
    moved = pltpu.roll(window, count + 4, 0)
    return jnp.where(start % 8 == 0, window, moved)[:count]


def store_rows(ref, start, length, values, cols):
    count = -(-length // 8) * 8
    base = pl.multiple_of((start // 8) * 8, 8)
    window = jnp.concatenate([values[:count], jnp.zeros((8, values.shape[1]), values.dtype)], axis=0)
    window = jnp.where(start % 8 == 0, window, pltpu.roll(window, 4, 0))
    row = lax.broadcasted_iota(jnp.int32, window.shape, 0) - start % 8
    held = ref[pl.ds(base, count + 8), cols]
    ref[pl.ds(base, count + 8), cols] = jnp.where((row >= 0) & (row < length), window, held)


def by_group(group, work):
    for g, length in enumerate(LENS):
        pl.when(group == g)(partial(work, length, -(-length // 16) * 16))


def attn_fwd_kernel(meta, tok, w1, attn, qkv, lse, wpad, tok32, out32, bias, *, heads):
    i = pl.program_id(0)
    rows, width = tok.shape
    hp = heads * HEAD_PAD

    @pl.when(i == 0)
    def _():
        tok32[:rows] = tok[...].astype(F32)
        tok32[rows:] = jnp.zeros((tok32.shape[0] - rows, width), F32)
        out32[...] = jnp.zeros(out32.shape, F32)
        wpad[...] = pad_heads(w1[:, : 3 * width].astype(F32)).astype(BF16)
        vec = w1[:, 3 * width :].astype(F32).T
        bias[0:1, :width] = vec[0:1]
        bias[1:2, :width] = vec[1:2]
        bias[2:3, :] = jnp.concatenate(
            [pad_heads(vec[2:3]), jnp.zeros((1, hp), F32), pad_heads(vec[3:4])], axis=1
        )

    start = meta[i]

    def work(length, padded):
        x = load_rows(tok32, start, padded)
        xhat, _ = row_norm(x)
        normed = (xhat * bias[0:1, :width] + bias[1:2, :width]).astype(BF16)
        qkv[0, :padded, :] = (dot_nn(normed, wpad[...]) + bias[2:3, :]).astype(BF16)
        for h in range(heads):
            at = h * HEAD_PAD
            q = qkv[0, :padded, at : at + HEAD_PAD]
            k = qkv[0, :padded, hp + at : hp + at + HEAD_PAD]
            v = qkv[0, :padded, 2 * hp + at : 2 * hp + at + HEAD_PAD]
            s = dot_nt(k, q)
            if length < padded:
                key = lax.broadcasted_iota(jnp.int32, s.shape, 0)
                s = jnp.where(key < length, s, -1e30)
            top = jnp.max(s, axis=0, keepdims=True)
            e = jnp.exp2((s - top) * EXP_SCALE)
            total = jnp.sum(e, axis=0, keepdims=True)
            p = (e * (1.0 / total)).astype(BF16)
            lse[0, h : h + 1, :padded] = top * EXP_SCALE + jnp.log2(total)
            o = dot_tn(p, v)
            store_rows(out32, start, length, o, pl.ds(at, HEAD_PAD))

    by_group(meta[8 + i], work)

    @pl.when(i == pl.num_programs(0) - 1)
    def _():
        attn[...] = out32[:rows].astype(BF16)


def attn_fwd(meta, tokens, w1):
    rows, width = tokens.shape
    heads = width // HEAD_DIM
    hp = heads * HEAD_PAD
    slots = (meta.shape[0] - 1) // 2
    return pl.pallas_call(
        partial(attn_fwd_kernel, heads=heads),
        grid_spec=pltpu.PrefetchScalarGridSpec(
            num_scalar_prefetch=1,
            grid=(slots,),
            in_specs=[
                pl.BlockSpec((rows, width), lambda i, m: (0, 0)),
                pl.BlockSpec(w1.shape, lambda i, m: (0, 0)),
            ],
            out_specs=[
                pl.BlockSpec((rows, hp), lambda i, m: (0, 0)),
                pl.BlockSpec((1, SLOT, 3 * hp), lambda i, m: (i, 0, 0)),
                pl.BlockSpec((1, 8, 512), lambda i, m: (i, 0, 0)),
                pl.BlockSpec((width, 3 * hp), lambda i, m: (0, 0)),
            ],
            scratch_shapes=[
                pltpu.VMEM((rows + ROW_PAD, width), F32),
                pltpu.VMEM((rows + ROW_PAD, hp), F32),
                pltpu.VMEM((8, 3 * hp), F32),
            ],
        ),
        out_shape=[
            jax.ShapeDtypeStruct((rows, hp), BF16),
            jax.ShapeDtypeStruct((slots, SLOT, 3 * hp), BF16),
            jax.ShapeDtypeStruct((slots, 8, 512), F32),
            jax.ShapeDtypeStruct((width, 3 * hp), BF16),
        ],
        compiler_params=pltpu.CompilerParams(vmem_limit_bytes=VMEM_LIMIT),
        name="attn_fwd",
    )(meta, tokens, w1)


INV_SQRT2 = 1.0 / math.sqrt(2.0)
ERF = (0.254829592, -0.284496736, 1.421413741, -1.453152027, 1.061405429)
ERF_T = 0.3275911


def gelu_pair(u):
    tail = 1.0 / (1.0 + (ERF_T * INV_SQRT2) * jnp.abs(u))
    poly = ERF[4] * tail + ERF[3]
    for c in (ERF[2], ERF[1], ERF[0]):
        poly = poly * tail + c
    bell = jnp.exp2((u * u) * (-0.5 * math.log2(math.e)))
    half = (0.5 * tail) * poly * bell
    cdf = jnp.where(u >= 0, 1.0 - half, half)
    return u * cdf, cdf + u * (bell * (1.0 / math.sqrt(2.0 * math.pi)))


def mlp_kernel(
    meta, tok, cot, attn, w2, out, dx1, dattn, grads, wproj, rowvec, gd, gu, gp, gsum, *, heads, chunk
):
    i = pl.program_id(0)
    rows, width = tok.shape
    hp = heads * HEAD_PAD
    hidden = 4 * width

    @pl.when(i == 0)
    def _():
        proj = w2[:, :width]
        wproj[...] = jnp.zeros(wproj.shape, BF16)
        for h in range(heads):
            wproj[h * HEAD_PAD : h * HEAD_PAD + HEAD_DIM] = proj[h * HEAD_DIM : (h + 1) * HEAD_DIM]
        vec = w2[:, width + 2 * hidden :].astype(F32).T
        for r in range(4):
            rowvec[r : r + 1, :width] = vec[r : r + 1]
            rowvec[4:5, r * width : (r + 1) * width] = vec[4 + r : 5 + r]
        gd[...] = jnp.zeros(gd.shape, F32)
        gu[...] = jnp.zeros(gu.shape, F32)
        gp[...] = jnp.zeros(gp.shape, F32)
        gsum[...] = jnp.zeros(gsum.shape, F32)

    proj_bias, gain, shift, down_bias = [rowvec[r : r + 1, :width] for r in range(4)]
    row = lax.broadcasted_iota(jnp.int32, (rows, 1), 0) + i * rows
    valid = (row < meta[16]).astype(F32)
    attn_rows = attn[...]
    x1 = tok[...].astype(F32) + dot_nn(attn_rows, wproj[...]) + proj_bias
    xhat, inverse = row_norm(x1)
    normed = (xhat * gain + shift).astype(BF16)
    dy = cot[...].astype(F32) * valid
    dyb = dy.astype(BF16)
    y = x1 + down_bias
    dn = jnp.zeros((rows, width), F32)
    for c in range(hidden // chunk):
        at = c * chunk
        up = w2[:, width + at : width + at + chunk]
        pre = dot_nn(normed, up) + rowvec[4:5, at : at + chunk]
        act, slope = gelu_pair(pre)
        actb = act.astype(BF16)
        if chunk <= width:
            blk, off = divmod(at, width)
            base = width + hidden + blk * width
            down = w2[off : off + chunk, base : base + width]
            y = y + dot_nn(actb, down)
            dact = dot_nt(dyb, down)
        dpre = dact * slope
        dpreb = dpre.astype(BF16)
        gd[at : at + chunk, :] += dot_tn(actb, dyb)
        gu[:, at : at + chunk] += dot_tn(normed, dpreb)
        gsum[4:5, at : at + chunk] += jnp.sum(dpre, axis=0, keepdims=True)
        dn = dn + dot_nt(dpreb, up)
    out[...] = (y * valid).astype(BF16)
    dx = dy + row_norm_back(dn * gain, xhat, inverse)
    dx1[...] = dx
    dxb = dx.astype(BF16)
    gp[...] += dot_tn(attn_rows, dxb)
    dattn[...] = dot_nt(dxb, wproj[...]).astype(BF16)
    gsum[0:1, :width] += jnp.sum(dx, axis=0, keepdims=True)
    gsum[1:2, :width] += jnp.sum(dn * xhat, axis=0, keepdims=True)
    gsum[2:3, :width] += jnp.sum(dn, axis=0, keepdims=True)
    gsum[3:4, :width] += jnp.sum(dy, axis=0, keepdims=True)

    @pl.when(i == pl.num_programs(0) - 1)
    def _():
        for h in range(heads):
            grads[h * HEAD_DIM : (h + 1) * HEAD_DIM, :width] = gp[
                h * HEAD_PAD : h * HEAD_PAD + HEAD_DIM
            ].astype(BF16)
        grads[:, width : width + hidden] = gu[...].astype(BF16)
        for c in range(4):
            base = width + hidden + c * width
            grads[:, base : base + width] = gd[c * width : (c + 1) * width].astype(BF16)
        vec = jnp.concatenate(
            [gsum[0:4, :width]]
            + [gsum[4:5, c * width : (c + 1) * width] for c in range(4)]
            + [jnp.zeros((120, width), F32)],
            axis=0,
        )
        grads[:, width + 2 * hidden :] = vec.T.astype(BF16)


def mlp(meta, tokens, cotangent, attn, w2, block=256, chunk=384):
    rows, width = tokens.shape
    heads = width // HEAD_DIM
    hp = heads * HEAD_PAD
    hidden = 4 * width
    by_row = lambda cols: pl.BlockSpec((block, cols), lambda i, m: (i, 0))
    return pl.pallas_call(
        partial(mlp_kernel, heads=heads, chunk=chunk),
        grid_spec=pltpu.PrefetchScalarGridSpec(
            num_scalar_prefetch=1,
            grid=(rows // block,),
            in_specs=[
                by_row(width),
                by_row(width),
                by_row(hp),
                pl.BlockSpec(w2.shape, lambda i, m: (0, 0)),
            ],
            out_specs=[
                by_row(width),
                by_row(width),
                by_row(hp),
                pl.BlockSpec(w2.shape, lambda i, m: (0, 0)),
            ],
            scratch_shapes=[
                pltpu.VMEM((hp, width), BF16),
                pltpu.VMEM((8, hidden), F32),
                pltpu.VMEM((hidden, width), F32),
                pltpu.VMEM((width, hidden), F32),
                pltpu.VMEM((hp, width), F32),
                pltpu.VMEM((8, hidden), F32),
            ],
        ),
        out_shape=[
            jax.ShapeDtypeStruct((rows, width), BF16),
            jax.ShapeDtypeStruct((rows, width), F32),
            jax.ShapeDtypeStruct((rows, hp), BF16),
            jax.ShapeDtypeStruct(w2.shape, BF16),
        ],
        compiler_params=pltpu.CompilerParams(vmem_limit_bytes=VMEM_LIMIT),
        name="mlp",
    )(meta, tokens, cotangent, attn, w2)


def attn_bwd_kernel(
    meta, tok, qkv, lse, dattn, dx1, wpad, w1, din, grads, tok32, da32, gw, gsum, dq, bias, *, heads
):
    i = pl.program_id(0)
    rows, width = tok.shape
    hp = heads * HEAD_PAD

    @pl.when(i == 0)
    def _():
        tok32[:rows] = tok[...].astype(F32)
        tok32[rows:] = jnp.zeros((tok32.shape[0] - rows, width), F32)
        da32[:rows] = dattn[...].astype(F32)
        da32[rows:] = jnp.zeros((da32.shape[0] - rows, hp), F32)
        vec = w1[:, 3 * width :].astype(F32).T
        bias[0:1, :width] = vec[0:1]
        gw[...] = jnp.zeros(gw.shape, F32)
        gsum[...] = jnp.zeros(gsum.shape, F32)

    start = meta[i]

    def work(length, padded):
        da = load_rows(da32, start, padded)
        if length < padded:
            keep = lax.broadcasted_iota(jnp.int32, (padded, 1), 0) < length
            da = jnp.where(keep, da, 0.0)
        da = da.astype(BF16)
        for h in range(heads):
            at = h * HEAD_PAD
            q = qkv[0, :padded, at : at + HEAD_PAD]
            k = qkv[0, :padded, hp + at : hp + at + HEAD_PAD]
            v = qkv[0, :padded, 2 * hp + at : 2 * hp + at + HEAD_PAD]
            dah = da[:, at : at + HEAD_PAD]
            s = dot_nt(k, q)
            p = jnp.exp2(s * EXP_SCALE - lse[0, h : h + 1, :padded])
            if length < padded:
                key = lax.broadcasted_iota(jnp.int32, s.shape, 0)
                p = jnp.where(key < length, p, 0.0)
            dp = dot_nt(v, dah)
            mean = jnp.sum(p * dp, axis=0, keepdims=True)
            ds = (p * (dp - mean)).astype(BF16)
            dv = dot_nn(p.astype(BF16), dah)
            dk = dot_nn(ds, q) * SCALE
            dqh = dot_tn(ds, k) * SCALE
            gsum[2:3, at : at + HEAD_PAD] += jnp.sum(dqh, axis=0, keepdims=True)
            gsum[2:3, 2 * hp + at : 2 * hp + at + HEAD_PAD] += jnp.sum(dv, axis=0, keepdims=True)
            dq[:padded, at : at + HEAD_PAD] = dqh.astype(BF16)
            dq[:padded, hp + at : hp + at + HEAD_PAD] = dk.astype(BF16)
            dq[:padded, 2 * hp + at : 2 * hp + at + HEAD_PAD] = dv.astype(BF16)
        xhat, inverse = row_norm(load_rows(tok32, start, padded))
        gain = bias[0:1, :width]
        d = dq[:padded, :]
        gw[...] += dot_tn(xhat.astype(BF16), d)
        gsum[3:4, :] += jnp.sum(d.astype(F32), axis=0, keepdims=True)
        dn = dot_nt(d, wpad[...])
        dx = row_norm_back(dn * gain, xhat, inverse)
        base = pl.multiple_of((start // 8) * 8, 8)
        store_rows(da32, start, length, dx, pl.ds(0, width))

    by_group(meta[8 + i], work)

    @pl.when(i == pl.num_programs(0) - 1)
    def _():
        row = lax.broadcasted_iota(jnp.int32, (rows, 1), 0)
        din[...] = jnp.where(row < meta[16], dx1[...] + da32[:rows, :width], 0.0).astype(BF16)
        vec = w1[:, 3 * width :].astype(F32)
        w = wpad[...].astype(F32)
        raw = gw[...]
        col = gsum[3:4, :]
        gain_term = jnp.sum(raw * w, axis=1, keepdims=True)
        bias_term = jnp.sum(col * w, axis=1, keepdims=True)
        g = raw * vec[:, 0:1] + vec[:, 1:2] * col
        grads[:, : 3 * width] = unpad_heads(g).astype(BF16)
        sums = jnp.concatenate(
            [
                unpad_heads(gsum[2:3, :hp]),
                unpad_heads(gsum[2:3, 2 * hp :]),
                jnp.zeros((126, width), F32),
            ],
            axis=0,
        ).T
        lane = lax.broadcasted_iota(jnp.int32, (width, 128), 1)
        moved = pltpu.roll(sums, 2, 1)
        tail = jnp.where(lane == 0, gain_term, jnp.where(lane == 1, bias_term, moved))
        grads[:, 3 * width :] = tail.astype(BF16)


def attn_bwd(meta, tokens, qkv, lse, dattn, dx1, wpad, w1):
    rows, width = tokens.shape
    heads = width // HEAD_DIM
    hp = heads * HEAD_PAD
    slots = (meta.shape[0] - 1) // 2
    whole = lambda a: pl.BlockSpec(a.shape, lambda i, m: (0, 0))
    return pl.pallas_call(
        partial(attn_bwd_kernel, heads=heads),
        grid_spec=pltpu.PrefetchScalarGridSpec(
            num_scalar_prefetch=1,
            grid=(slots,),
            in_specs=[
                whole(tokens),
                pl.BlockSpec((1, SLOT, 3 * hp), lambda i, m: (i, 0, 0)),
                pl.BlockSpec((1, 8, 512), lambda i, m: (i, 0, 0)),
                whole(dattn),
                whole(dx1),
                whole(wpad),
                whole(w1),
            ],
            out_specs=[whole(tokens), whole(w1)],
            scratch_shapes=[
                pltpu.VMEM((rows + ROW_PAD, width), F32),
                pltpu.VMEM((rows + ROW_PAD, hp), F32),
                pltpu.VMEM((width, 3 * hp), F32),
                pltpu.VMEM((8, 3 * hp), F32),
                pltpu.VMEM((SLOT, 3 * hp), BF16),
                pltpu.VMEM((8, 3 * hp), F32),
            ],
        ),
        out_shape=[
            jax.ShapeDtypeStruct((rows, width), BF16),
            jax.ShapeDtypeStruct(w1.shape, BF16),
        ],
        compiler_params=pltpu.CompilerParams(vmem_limit_bytes=VMEM_LIMIT),
        name="attn_bwd",
    )(meta, tokens, qkv, lse, dattn, dx1, wpad, w1)


def swap(value, axis, bit):
    size = lax.axis_size(axis)
    return lax.ppermute(value, axis, [(i, i ^ bit) for i in range(size)])


def bit_of(axis, bit):
    return (lax.axis_index(axis) & bit) != 0


def halves(value, axis, dim):
    size = value.shape[dim] // 2
    low = lax.slice_in_dim(value, 0, size, axis=dim)
    high = lax.slice_in_dim(value, size, 2 * size, axis=dim)
    return low, high


def split_by(value, axis, bit, dim):
    low, high = halves(value, axis, dim)
    mine = bit_of(axis, bit)
    return jnp.where(mine, high, low), jnp.where(mine, low, high)


def join_by(own, other, axis, bit, dim):
    mine = bit_of(axis, bit)
    return jnp.where(
        mine,
        jnp.concatenate([other, own], axis=dim),
        jnp.concatenate([own, other], axis=dim),
    )


def bits_of(axis):
    size = lax.axis_size(axis)
    return [1 << b for b in range(size.bit_length() - 1)]


def gather_rows(shard):
    rows, cols = shard.shape
    part, _ = split_by(shard, "dp", 1, 1)
    part = part[None]
    for bit in bits_of("fsdp")[1:]:
        part = join_by(part, swap(part, "fsdp", bit), "fsdp", bit, 0)
    part = join_by(part[:, None], swap(part, "fsdp", 1)[:, None], "fsdp", 1, 1)
    part = part.reshape(-1, cols // 2)
    return join_by(part, swap(part, "dp", 1), "dp", 1, 1)


def sum_half(value, axis, bit, dim):
    keep, send = split_by(value, axis, bit, dim)
    got = swap(send, axis, bit)
    return (keep.astype(F32) + got.astype(F32)).astype(BF16)


def reduce_rows(value):
    size = lax.axis_size("fsdp")
    rows, cols = value.shape
    part = sum_half(value, "dp", 1, 1)
    part = part.reshape(size, rows // size, cols // 2)
    for bit in bits_of("dp")[1:]:
        part = sum_half(part, "dp", bit, 1)
    part = part.reshape(size // 2, 2, *part.shape[1:])
    part = sum_half(part, "fsdp", 1, 1)
    part = part.reshape(part.shape[0], *part.shape[2:])
    for bit in reversed(bits_of("fsdp")[1:]):
        part = sum_half(part, "fsdp", bit, 0)
    part = part[0]
    for bit in reversed(bits_of("dp")[1:]):
        part = join_by(part, swap(part, "dp", bit), "dp", bit, 0)
    return join_by(part, swap(part, "dp", 1), "dp", 1, 1)


def image_table(size_group, assignment, device, slots):
    owned = assignment == device
    rank = jnp.cumsum(owned.astype(jnp.int32)) - 1
    slot = jnp.arange(slots, dtype=jnp.int32)
    here = owned[None, :] & (rank[None, :] == slot[:, None])
    groups = jnp.sum(jnp.where(here, size_group[None, :], 0), axis=1)
    lengths = jnp.where(groups == 0, LENS[0], jnp.where(groups == 1, LENS[1], LENS[2]))
    ends = jnp.sum(jnp.where(slot[None, :] <= slot[:, None], lengths[None, :], 0), axis=1)
    return jnp.concatenate([ends - lengths, groups, ends[-1:]]).astype(jnp.int32)


def column(vector, size):
    return vector.reshape(-1, size).T


def body(
    tokens,
    cotangent,
    size_group,
    assignment,
    ln1_gain,
    ln1_bias,
    w_qkv,
    q_bias,
    v_bias,
    w_proj,
    proj_bias,
    ln2_gain,
    ln2_bias,
    w_up,
    up_bias,
    w_down,
    down_bias,
):
    width = tokens.shape[1]
    shards = lax.axis_size("fsdp")
    size = width // shards
    ratio = up_bias.shape[0] // size
    hidden = ratio * width
    devices = shards * lax.axis_size("dp")
    device = lax.axis_index("fsdp") * lax.axis_size("dp") + lax.axis_index("dp")
    table = image_table(size_group, assignment, device, size_group.shape[0] // devices)

    first = jnp.concatenate(
        [w_qkv.reshape(size, 3 * width)]
        + [column(v, size) for v in (ln1_gain, ln1_bias, q_bias, v_bias)]
        + [jnp.zeros((size, VEC - 4), BF16)],
        axis=1,
    )
    up = w_up.reshape(size, shards, ratio, size).transpose(0, 2, 1, 3).reshape(size, hidden)
    down = w_down.reshape(ratio, size, width)
    second = jnp.concatenate(
        [w_proj.reshape(size, width), up]
        + [down[c] for c in range(ratio)]
        + [column(v, size) for v in (proj_bias, ln2_gain, ln2_bias, down_bias, up_bias)]
        + [jnp.zeros((size, VEC - 4 - ratio), BF16)],
        axis=1,
    )
    first = gather_rows(first)
    second = gather_rows(second)

    attn, qkv, lse, padded = attn_fwd(table, tokens, first)
    layer_out, dx1, dattn, grad_second = mlp(table, tokens, cotangent, attn, second)
    grad_second = reduce_rows(grad_second).astype(F32)
    grad_input, grad_first = attn_bwd(table, tokens, qkv, lse, dattn, dx1, padded, first)
    grad_first = reduce_rows(grad_first).astype(F32)

    one = lambda r: grad_first[:, 3 * width + r]
    base = width + 2 * hidden
    two = lambda r: grad_second[:, base + r]
    grad_up = grad_second[:, width : width + hidden]
    grad_up = grad_up.reshape(size, ratio, shards, size).transpose(0, 2, 1, 3).reshape(-1)
    grad_down = grad_second[:, width + hidden : base].reshape(size, ratio, width)
    grad_up_bias = grad_second[:, base + 4 : base + 4 + ratio].T.reshape(-1)
    return (
        layer_out,
        grad_input,
        one(0),
        one(1),
        grad_first[:, : 3 * width].reshape(-1),
        one(2),
        one(3),
        grad_second[:, :width].reshape(-1),
        two(0),
        two(1),
        two(2),
        grad_up,
        grad_up_bias,
        grad_down.transpose(1, 0, 2).reshape(-1),
        two(3),
    )


def solution(mesh):
    rows = P(("fsdp", "dp"), None)
    flat = P("fsdp")
    return jax.shard_map(
        body,
        mesh=mesh,
        in_specs=(rows, rows, P(), P()) + (flat,) * 13,
        out_specs=(rows, rows) + (flat,) * 13,
        check_vma=False,
    )
```

```python
from functools import partial
import math

import jax
import jax.numpy as jnp
from jax import lax
from jax.experimental import pallas as pl
from jax.experimental.pallas import tpu as pltpu
from jax.sharding import PartitionSpec as P

HEAD_DIM = 96
HEAD_PAD = 128
LENS = (196, 256, 400)
SLOT = 400
ROW_PAD = 32
PAIR = 2
PAIR_DIM = PAIR * HEAD_DIM
PAIR_PAD = PAIR * HEAD_PAD
QUARTERS = 4
VEC = 128
VEC_PAIR = 64
SCALE = 1.0 / math.sqrt(HEAD_DIM)
EXP_SCALE = SCALE * math.log2(math.e)
MIB = 1024 * 1024
VMEM = {"attn_fwd": 12, "mlp": 21, "attn_bwd": 8, "layer_out": 8, "input_grad": 10}
F32 = jnp.float32
BF16 = jnp.bfloat16


def dot_nn(a, b):
    return lax.dot_general(a, b, (((1,), (0,)), ((), ())), preferred_element_type=F32)


def dot_nt(a, b):
    return lax.dot_general(a, b, (((1,), (1,)), ((), ())), preferred_element_type=F32)


def dot_tn(a, b):
    return lax.dot_general(a, b, (((0,), (0,)), ((), ())), preferred_element_type=F32)


def pad_heads(values):
    rows, cols = values.shape
    gap = jnp.zeros((rows, HEAD_PAD - HEAD_DIM), values.dtype)
    parts = []
    for h in range(cols // HEAD_DIM):
        parts += [values[:, h * HEAD_DIM : (h + 1) * HEAD_DIM], gap]
    return jnp.concatenate(parts, axis=1)


def unpad_heads(values):
    rows, cols = values.shape
    return jnp.concatenate(
        [values[:, h * HEAD_PAD : h * HEAD_PAD + HEAD_DIM] for h in range(cols // HEAD_PAD)], axis=1
    )


def row_norm(x):
    center = x - jnp.mean(x, axis=-1, keepdims=True)
    inverse = lax.rsqrt(jnp.mean(center * center, axis=-1, keepdims=True) + 1e-6)
    return center * inverse, inverse


def row_norm_back(e, xhat, inverse):
    return inverse * (
        e - jnp.mean(e, axis=-1, keepdims=True) - xhat * jnp.mean(e * xhat, axis=-1, keepdims=True)
    )


def load_rows(ref, start, count):
    base = pl.multiple_of((start // 8) * 8, 8)
    window = ref[pl.ds(base, count + 8), :]
    moved = pltpu.roll(window, count + 4, 0)
    return jnp.where(start % 8 == 0, window, moved)[:count]


def store_rows(ref, start, length, values, cols):
    count = -(-length // 8) * 8
    base = pl.multiple_of((start // 8) * 8, 8)
    window = jnp.concatenate([values[:count], jnp.zeros((8, values.shape[1]), values.dtype)], axis=0)
    window = jnp.where(start % 8 == 0, window, pltpu.roll(window, 4, 0))
    row = lax.broadcasted_iota(jnp.int32, window.shape, 0) - start % 8
    held = ref[pl.ds(base, count + 8), cols]
    ref[pl.ds(base, count + 8), cols] = jnp.where((row >= 0) & (row < length), window, held)


def by_group(group, work):
    for g, length in enumerate(LENS):
        pl.when(group == g)(partial(work, length, -(-length // 16) * 16))


def gelu_pair(u):
    cdf = 0.5 + 0.5 * lax.erf(u * (1.0 / math.sqrt(2.0)))
    bell = jnp.exp2((u * u) * (-0.5 * math.log2(math.e)))
    return u * cdf, cdf + u * (bell * (1.0 / math.sqrt(2.0 * math.pi)))


def whole(array):
    at = (0,) * len(array.shape)
    return pl.BlockSpec(array.shape, lambda i, m: at, pipeline_mode=pl.Buffered(1))


def slot_block(cols):
    return pl.BlockSpec((1, SLOT, cols), lambda i, m: (i, 0, 0))


def call(kernel, name, grid, in_specs, out_specs, out_shape, scratch, args, waits=(), carry=(), far=()):
    given, made, passed = len(in_specs) + 1, len(out_shape), len(waits) + len(carry)

    def ordered(*refs):
        kernel(*refs[:given], *refs[given + passed : given + passed + made], *refs[given + passed + made + len(carry) :])

    args = [
        pltpu.with_memory_space_constraint(t, pltpu.HBM) if at in far else t for at, t in enumerate(args)
    ]
    anywhere = pl.BlockSpec(memory_space=pl.ANY)
    outs = pl.pallas_call(
        ordered,
        grid_spec=pltpu.PrefetchScalarGridSpec(
            num_scalar_prefetch=1,
            grid=(grid,),
            in_specs=list(in_specs) + [anywhere] * passed,
            out_specs=list(out_specs) + [anywhere] * len(carry),
            scratch_shapes=scratch,
        ),
        out_shape=list(out_shape) + [jax.ShapeDtypeStruct(t.shape, t.dtype) for t in carry],
        input_output_aliases={given + len(waits) + n: made + n for n in range(len(carry))},
        compiler_params=pltpu.CompilerParams(vmem_limit_bytes=VMEM[name] * MIB),
        name=name,
    )(*args, *waits, *carry)
    return outs


def groups_at(meta):
    return (meta.shape[0] - 2) // 2


def rows_used(meta):
    return meta[meta.shape[0] - 2]


def device_of(meta):
    return meta[meta.shape[0] - 1]


def core_of(meta):
    return device_of(meta) % 2


def attn_fwd_kernel(meta, tok, wf0, wf1, attn0, attn1, qkv0, qkv1, xhat_out, lse0, lse1, wpad0, wpad1,
                    tok32, out32, bias):
    i = pl.program_id(0)
    rows, width = tok.shape
    cols = 3 * PAIR_PAD
    sides = ((wf0, qkv0, lse0, wpad0), (wf1, qkv1, lse1, wpad1))

    @pl.when(i == 0)
    def _():
        tok32[:rows] = tok[...].astype(F32)
        tok32[rows:] = jnp.zeros((tok32.shape[0] - rows, width), F32)
        vec = wf0[:, 3 * PAIR_DIM :].astype(F32).T
        bias[0:2, :width] = vec[0:2]
        for c in range(2):

            @pl.when(core_of(meta) == c)
            def _():
                for p in range(2):
                    at = (p ^ c) * PAIR_DIM
                    parts = [pad_heads(vec[r : r + 1, at : at + PAIR_DIM]) for r in (2, 3)]
                    bias[2 + p : 3 + p, :] = jnp.concatenate(
                        [parts[0], jnp.zeros((1, PAIR_PAD), F32), parts[1]], axis=1
                    )

        for wf, _, _, wpad in sides:
            wpad[...] = pad_heads(wf[:, : 3 * PAIR_DIM].astype(F32)).astype(BF16)

    start = meta[i]

    def work(length, padded):
        xhat, _ = row_norm(load_rows(tok32, start, padded))
        normed = (xhat * bias[0:1, :width] + bias[1:2, :width]).astype(BF16)
        xhat_out[0, :padded, :] = xhat.astype(BF16)
        outs = []
        for p, (_, qkv, lse, wpad) in enumerate(sides):
            qkv[0, :padded, :] = (dot_nn(normed, wpad[...]) + bias[2 + p : 3 + p, :]).astype(BF16)
            for h in range(PAIR):
                at = h * HEAD_PAD
                q = qkv[0, :padded, at : at + HEAD_PAD]
                k = qkv[0, :padded, PAIR_PAD + at : PAIR_PAD + at + HEAD_PAD]
                v = qkv[0, :padded, 2 * PAIR_PAD + at : 2 * PAIR_PAD + at + HEAD_PAD]
                s = dot_nt(k, q)
                if length < padded:
                    key = lax.broadcasted_iota(jnp.int32, s.shape, 0)
                    s = jnp.where(key < length, s, -1e30)
                top = jnp.max(s, axis=0, keepdims=True)
                e = jnp.exp2((s - top) * EXP_SCALE)
                total = jnp.sum(e, axis=0, keepdims=True)
                probs = (e * (1.0 / total)).astype(BF16)
                lse[0, h : h + 1, :padded] = top * EXP_SCALE + jnp.log2(total)
                outs.append(dot_tn(probs, v))
        store_rows(out32, start, length, jnp.concatenate(outs, axis=1), slice(None))

    by_group(meta[groups_at(meta) + i], work)

    @pl.when(i == pl.num_programs(0) - 1)
    def _():
        row = lax.broadcasted_iota(jnp.int32, (rows, 1), 0)
        mixed = jnp.where(row < rows_used(meta), out32[:rows], 0.0).astype(BF16)
        attn0[...] = mixed[:, :PAIR_PAD]
        attn1[...] = mixed[:, PAIR_PAD:]


def attn_fwd(meta, tokens, wf, waits, carry):
    rows, width = tokens.shape
    slots = groups_at(meta)
    cols = 3 * PAIR_PAD
    out_shape = [jax.ShapeDtypeStruct((rows, PAIR_PAD), BF16)] * 2
    out_shape += [jax.ShapeDtypeStruct((slots, SLOT, cols), BF16)] * 2
    out_shape += [jax.ShapeDtypeStruct((slots, SLOT, width), BF16)]
    out_shape += [jax.ShapeDtypeStruct((slots, 8, 512), F32)] * 2
    out_shape += [jax.ShapeDtypeStruct((width, cols), BF16)] * 2
    stats = pl.BlockSpec((1, 8, 512), lambda i, m: (i, 0, 0))
    out_specs = [whole(out_shape[0])] * 2 + [slot_block(cols)] * 2 + [slot_block(width)]
    out_specs += [stats] * 2 + [whole(out_shape[-1])] * 2
    scratch = [
        pltpu.VMEM((rows + ROW_PAD, width), F32),
        pltpu.VMEM((rows + ROW_PAD, 2 * PAIR_PAD), F32),
        pltpu.VMEM((8, cols), F32),
    ]
    in_specs = [whole(tokens), whole(wf[0]), whole(wf[1])]
    args = (meta, tokens, *wf)
    return call(attn_fwd_kernel, "attn_fwd", slots, in_specs, out_specs, out_shape, scratch, args, waits, carry)


def put_blocks(to, value, col, shards, parity=None):
    rows, cols = value.shape
    size = rows // shards
    half = rows // 2
    if size % 16:
        if parity is not None:
            value = value[parity * half : (parity + 1) * half]
        to[:, col : col + cols] = value
        return
    for n, place in enumerate(turned(shards)):
        at = place * size
        if parity is not None:
            if n % 2 != parity:
                continue
            at -= parity * half
        to[at : at + size, col : col + cols] = value[n * size : (n + 1) * size]


def mlp_kernel(meta, tok, cot, attn0, attn1, w0, w1, x1o, acto, dx1, da0, da1,
               keep_a, send_a, keep_b, send_b, wproj, rowvec, gd, gu, gp, gsum, *, shards):
    i = pl.program_id(0)
    rows, width = tok.shape
    parts = (w0, w1)

    def in_order(first, second, use):
        for c in range(2):
            pl.when(core_of(meta) == c)(partial(use, c, *((first, second) if c == 0 else (second, first))))

    @pl.when(i == 0)
    def _():
        def use(c, low, high):
            flat = [ref[x][:, width : width + VEC] for ref in (low, high) for x in range(2)]
            proj = jnp.concatenate(flat[: width // VEC], axis=1)
            wproj[...] = jnp.zeros(wproj.shape, BF16)
            for h in range(2 * PAIR):
                at = (h ^ (PAIR * c)) * HEAD_PAD
                wproj[at : at + HEAD_DIM] = proj[h * HEAD_DIM : (h + 1) * HEAD_DIM]
            vec = flat[-1].astype(F32).T
            for r in range(4):
                rowvec[r : r + 1, :width] = vec[r : r + 1]
                at = (r ^ (2 * c)) * width
                rowvec[4:5, at : at + width] = vec[4 + r : 5 + r]

        in_order(w0, w1, use)
        gd[...] = jnp.zeros(gd.shape, F32)
        gu[...] = jnp.zeros(gu.shape, F32)
        gp[...] = jnp.zeros(gp.shape, F32)
        gsum[...] = jnp.zeros(gsum.shape, F32)

    proj_bias, gain, shift, down_bias = [rowvec[r : r + 1, :width] for r in range(4)]
    row = lax.broadcasted_iota(jnp.int32, (rows, 1), 0) + i * rows
    valid = (row < rows_used(meta)).astype(F32)
    mixed0, mixed1 = attn0[...], attn1[...]
    x1 = tok[...].astype(F32) + dot_nn(mixed0, wproj[:PAIR_PAD]) + dot_nn(mixed1, wproj[PAIR_PAD:])
    x1 = x1 + proj_bias
    x1o[...] = (x1 + down_bias) * valid
    xhat, inverse = row_norm(x1)
    normed = (xhat * gain + shift).astype(BF16)
    dy = cot[...].astype(F32) * valid
    dyb = dy.astype(BF16)
    dn = jnp.zeros((rows, width), F32)
    chunk = 2 * width
    for c in range(2):
        at = c * chunk
        up = jnp.concatenate([parts[c][0][:, :width], parts[c][1][:, :width]], axis=1)
        down = jnp.concatenate([parts[c][x][:, width + VEC :] for x in range(2)], axis=0)
        pre = dot_nn(normed, up) + rowvec[4:5, at : at + chunk]
        act, slope = gelu_pair(pre)
        actb = act.astype(BF16)
        acto[:, at : at + chunk] = actb
        dpre = dot_nt(dyb, down) * slope
        dpreb = dpre.astype(BF16)
        gd[:, at : at + chunk] += dot_tn(dyb, actb)
        gu[:, at : at + chunk] += dot_tn(normed, dpreb)
        gsum[4:5, at : at + chunk] += jnp.sum(dpre, axis=0, keepdims=True)
        dn = dn + dot_nt(dpreb, up)
    dx = dy + row_norm_back(dn * gain, xhat, inverse)
    dx1[...] = dx
    dxb = dx.astype(BF16)
    gp[:, :PAIR_PAD] += dot_tn(dxb, mixed0)
    gp[:, PAIR_PAD:] += dot_tn(dxb, mixed1)
    da0[...] = dot_nt(dxb, wproj[:PAIR_PAD]).astype(BF16)
    da1[...] = dot_nt(dxb, wproj[PAIR_PAD:]).astype(BF16)
    gsum[0:1, :width] += jnp.sum(dx, axis=0, keepdims=True)
    gsum[1:2, :width] += jnp.sum(dn * xhat, axis=0, keepdims=True)
    gsum[2:3, :width] += jnp.sum(dn, axis=0, keepdims=True)
    gsum[3:4, :width] += jnp.sum(dy, axis=0, keepdims=True)

    @pl.when(i == pl.num_programs(0) - 1)
    def _():
        for half, (to_a, to_b) in enumerate(((keep_a, keep_b), (send_a, send_b))):
            for x in range(2):
                at = (2 * half + x) * width
                put_blocks(to_a.at[x], gu[:, at : at + width].astype(BF16), 0, shards)
                part = gd[:, at : at + width].T.astype(BF16)
                for y in range(2):
                    put_blocks(to_b.at[y, x], part, 0, shards, y)

        def use(c, low, high):
            rows_of = [gsum[r : r + 1, :width] for r in range(4)]
            for r in range(4):
                at = (r ^ (2 * c)) * width
                rows_of.append(gsum[4:5, at : at + width])
            vec = jnp.concatenate(rows_of + [jnp.zeros((VEC - 8, width), F32)], axis=0).T
            grad = unpad_heads(gp[...]).T
            first, second = grad[:PAIR_DIM], grad[PAIR_DIM:]
            proj = jnp.concatenate([second, first] if c else [first, second], axis=0)
            flat = jnp.concatenate([proj, vec], axis=1).astype(BF16)
            for k in range(QUARTERS):
                to = (low, high)[k // 2].at[k % 2]
                put_blocks(to, flat[:, k * VEC : (k + 1) * VEC], width, shards)

        in_order(keep_a, send_a, use)


def mlp(meta, tokens, cotangent, attn, w, shards, block=512):
    rows, width = tokens.shape
    hidden = QUARTERS * width
    by_row = lambda cols: pl.BlockSpec((block, cols), lambda i, m: (i, 0))
    out_shape = [
        pltpu.HBM((rows, width), F32),
        pltpu.HBM((rows, hidden), BF16),
        pltpu.HBM((rows, width), F32),
        jax.ShapeDtypeStruct((rows, PAIR_PAD), BF16),
        jax.ShapeDtypeStruct((rows, PAIR_PAD), BF16),
    ]
    out_shape += [jax.ShapeDtypeStruct((2, width, width + VEC), BF16)] * 2
    out_shape += [jax.ShapeDtypeStruct((2, 2, width // 2, width), BF16)] * 2
    out_specs = [by_row(s.shape[1]) for s in out_shape[:5]] + [whole(s) for s in out_shape[5:]]
    in_specs = [by_row(width)] * 2 + [by_row(PAIR_PAD)] * 2 + [whole(t) for t in w]
    scratch = [
        pltpu.VMEM((2 * PAIR_PAD, width), BF16),
        pltpu.VMEM((8, hidden), F32),
        pltpu.VMEM((width, hidden), F32),
        pltpu.VMEM((width, hidden), F32),
        pltpu.VMEM((width, 2 * PAIR_PAD), F32),
        pltpu.VMEM((8, hidden), F32),
    ]
    args = (meta, tokens, cotangent, *attn, *w)
    kernel = partial(mlp_kernel, shards=shards)
    return call(kernel, "mlp", rows // block, in_specs, out_specs, out_shape, scratch, args)


def layer_out_kernel(meta, x1, act, w0, w1, out):
    rows, width = x1.shape
    row = lax.broadcasted_iota(jnp.int32, (rows, 1), 0) + pl.program_id(0) * rows
    valid = (row < rows_used(meta)).astype(F32)
    y = x1[...]
    for c, ref in enumerate((w0, w1)):
        down = jnp.concatenate([ref[x][:, width + VEC :] for x in range(2)], axis=0)
        y = y + dot_nn(act[:, 2 * c * width : 2 * (c + 1) * width], down) * valid
    out[...] = y.astype(BF16)


def layer_output(meta, x1, act, w, waits, carry, block=512):
    rows, width = x1.shape
    by_row = lambda cols: pl.BlockSpec((block, cols), lambda i, m: (i, 0))
    return call(
        layer_out_kernel,
        "layer_out",
        rows // block,
        [by_row(width), by_row(act.shape[1]), whole(w[0]), whole(w[1])],
        [by_row(width)],
        [jax.ShapeDtypeStruct((rows, width), BF16)],
        [],
        (meta, x1, act, *w),
        waits,
        carry,
        (1, 2),
    )


def attn_bwd_kernel(meta, qkv, xhat, lse, dattn, wpad, wf, dqkv, grads, da32, gw, gsum, *, own, shards):
    i = pl.program_id(0)
    rows = dattn.shape[0]
    width = wf.shape[0]

    @pl.when(i == 0)
    def _():
        da32[:rows] = dattn[...].astype(F32)
        da32[rows:] = jnp.zeros((da32.shape[0] - rows, PAIR_PAD), F32)
        gw[...] = jnp.zeros(gw.shape, F32)
        gsum[...] = jnp.zeros(gsum.shape, F32)

    start = meta[i]

    def work(length, padded):
        da = load_rows(da32, start, padded)
        if length < padded:
            keep = lax.broadcasted_iota(jnp.int32, (padded, 1), 0) < length
            da = jnp.where(keep, da, 0.0)
        da = da.astype(BF16)
        for h in range(PAIR):
            at = h * HEAD_PAD
            q = qkv[0, :padded, at : at + HEAD_PAD]
            k = qkv[0, :padded, PAIR_PAD + at : PAIR_PAD + at + HEAD_PAD]
            v = qkv[0, :padded, 2 * PAIR_PAD + at : 2 * PAIR_PAD + at + HEAD_PAD]
            dah = da[:, at : at + HEAD_PAD]
            s = dot_nt(k, q)
            p = jnp.exp2(s * EXP_SCALE - lse[0, h : h + 1, :padded])
            if length < padded:
                key = lax.broadcasted_iota(jnp.int32, s.shape, 0)
                p = jnp.where(key < length, p, 0.0)
            dp = dot_nt(v, dah)
            mean = jnp.sum(p * dp, axis=0, keepdims=True)
            ds = (p * (dp - mean)).astype(BF16)
            dv = dot_nn(p.astype(BF16), dah)
            dk = dot_nn(ds, q) * SCALE
            dq = dot_tn(ds, k) * SCALE
            gsum[0:1, at : at + HEAD_PAD] += jnp.sum(dq, axis=0, keepdims=True)
            gsum[0:1, 2 * PAIR_PAD + at : 2 * PAIR_PAD + at + HEAD_PAD] += jnp.sum(dv, axis=0, keepdims=True)
            dqkv[0, :padded, at : at + HEAD_PAD] = dq.astype(BF16)
            dqkv[0, :padded, PAIR_PAD + at : PAIR_PAD + at + HEAD_PAD] = dk.astype(BF16)
            dqkv[0, :padded, 2 * PAIR_PAD + at : 2 * PAIR_PAD + at + HEAD_PAD] = dv.astype(BF16)
        d = dqkv[0, :padded, :]
        gw[...] += dot_tn(xhat[0, :padded, :], d)
        gsum[1:2, :] += jnp.sum(d.astype(F32), axis=0, keepdims=True)

    by_group(meta[groups_at(meta) + i], work)

    @pl.when(i == pl.num_programs(0) - 1)
    def _():
        w = wpad[...].astype(F32)
        raw = gw[...]
        col = gsum[1:2, :]
        gain_term = jnp.sum(raw * w, axis=1, keepdims=True)
        bias_term = jnp.sum(col * w, axis=1, keepdims=True)
        vec = wf[:, 3 * PAIR_DIM :].astype(F32)
        main = unpad_heads(raw * vec[:, 0:1] + vec[:, 1:2] * col).astype(BF16)
        put_blocks(grads, main, 0, shards)
        q_sum = unpad_heads(gsum[0:1, :PAIR_PAD])
        v_sum = unpad_heads(gsum[0:1, 2 * PAIR_PAD :])
        gap = jnp.zeros((1, width - PAIR_DIM), F32)
        for c in range(2):

            @pl.when(core_of(meta) == (c if own else 1 - c))
            def _():
                rows_of = [jnp.concatenate([gap, t] if c else [t, gap], axis=1) for t in (q_sum, v_sum)]
                rows_of = [jnp.zeros((2, width), F32)] + rows_of + [jnp.zeros((VEC - 4, width), F32)]
                sums = jnp.concatenate(rows_of, axis=0).T
                lane = lax.broadcasted_iota(jnp.int32, sums.shape, 1)
                tail = jnp.where(lane == 0, gain_term, jnp.where(lane == 1, bias_term, sums))
                put_blocks(grads, tail[:, :VEC_PAIR].astype(BF16), 3 * PAIR_DIM, shards)


def attn_bwd(meta, qkv, xhat, lse, dattn, wpad, wf, own, shards, waits, carry):
    rows = dattn.shape[0]
    width = wf.shape[0]
    cols = 3 * PAIR_PAD
    out_shape = [jax.ShapeDtypeStruct(qkv.shape, BF16), jax.ShapeDtypeStruct(wf.shape, BF16)]
    in_specs = [slot_block(cols), slot_block(width), pl.BlockSpec((1, 8, 512), lambda i, m: (i, 0, 0))]
    in_specs += [whole(dattn), whole(wpad), whole(wf)]
    scratch = [
        pltpu.VMEM((rows + ROW_PAD, PAIR_PAD), F32),
        pltpu.VMEM((width, cols), F32),
        pltpu.VMEM((8, cols), F32),
    ]
    args = (meta, qkv, xhat, lse, dattn, wpad, wf)
    kernel = partial(attn_bwd_kernel, own=own, shards=shards)
    out_specs = [slot_block(cols), whole(wf)]
    grid = groups_at(meta)
    return call(kernel, "attn_bwd", grid, in_specs, out_specs, out_shape, scratch, args, waits, carry)


def input_grad_kernel(meta, tok, d0, d1, w0, w1, wf, dx1, out, tok32, bias):
    i = pl.program_id(0)
    rows, width = tok.shape

    @pl.when(i == 0)
    def _():
        tok32[:rows] = tok[...].astype(F32)
        tok32[rows:] = jnp.zeros((tok32.shape[0] - rows, width), F32)
        bias[...] = wf[:, 3 * PAIR_DIM :].astype(F32).T[0:8]

    start = meta[i]

    def work(length, padded):
        dn = dot_nt(d0[0, :padded, :], w0[...]) + dot_nt(d1[0, :padded, :], w1[...])
        xhat, inverse = row_norm(load_rows(tok32, start, padded))
        dx = row_norm_back(dn * bias[0:1, :], xhat, inverse)
        store_rows(tok32, start, length, dx, slice(None))

    by_group(meta[groups_at(meta) + i], work)

    @pl.when(i == pl.num_programs(0) - 1)
    def _():
        row = lax.broadcasted_iota(jnp.int32, (rows, 1), 0)
        total = dx1[...] + tok32[:rows]
        out[...] = jnp.where(row < rows_used(meta), total, 0.0).astype(BF16)


def input_grad(meta, tokens, d, w, wf, dx1, waits, carry):
    rows, width = tokens.shape
    slot = slot_block(d[0].shape[2])
    in_specs = [whole(tokens), slot, slot] + [whole(t) for t in (*w, wf, dx1)]
    scratch = [pltpu.VMEM((rows + ROW_PAD, width), F32), pltpu.VMEM((8, width), F32)]
    out_shape = [jax.ShapeDtypeStruct((rows, width), BF16)]
    args = (meta, tokens, *d, *w, wf, dx1)
    grid, out_specs = groups_at(meta), [whole(tokens)]
    return call(
        input_grad_kernel, "input_grad", grid, in_specs, out_specs, out_shape, scratch, args, waits, carry
    )


def turned(shards):
    count = shards.bit_length() - 1
    return [sum(((n >> b) & 1) << (count - 1 - b) for b in range(count)) for n in range(shards)]


def image_table(size_group, assignment, device, slots):
    owned = assignment == device
    rank = jnp.cumsum(owned.astype(jnp.int32)) - 1
    slot = jnp.arange(slots, dtype=jnp.int32)
    here = owned[None, :] & (rank[None, :] == slot[:, None])
    groups = jnp.sum(jnp.where(here, size_group[None, :], 0), axis=1)
    lengths = jnp.where(groups == 0, LENS[0], jnp.where(groups == 1, LENS[1], LENS[2]))
    ends = jnp.sum(jnp.where(slot[None, :] <= slot[:, None], lengths[None, :], 0), axis=1)
    return jnp.concatenate([ends - lengths, groups, ends[-1:], device[None]]).astype(jnp.int32)


def swap(value, axis, bit):
    size = lax.axis_size(axis)
    return lax.ppermute(value, axis, [(i, i ^ bit) for i in range(size)])


def sides_of(bits):
    table = {}
    for axis, those in bits.items():
        for bit in those:
            mine = (lax.axis_index(axis) & bit) // bit
            table[axis, bit] = (mine.astype(jnp.uint32), (1 - mine).astype(jnp.uint32), mine == 1)
    return table


def pick(sides, value, axis, bit, dim):
    mine, theirs, _ = sides[axis, bit]
    keep = lax.dynamic_index_in_dim(value, mine, dim, keepdims=False)
    send = lax.dynamic_index_in_dim(value, theirs, dim, keepdims=False)
    return keep, send


def join(upper, own, other, dim):
    return jnp.where(upper, jnp.stack([other, own], axis=dim), jnp.stack([own, other], axis=dim))


def added(keep, got):
    return (keep.astype(F32) + got.astype(F32)).astype(BF16)


def after(value, *others):
    return lax.optimization_barrier((value, *others))[0]


class Gather:
    def __init__(self, sides, part, keys):
        self.sides, self.part, self.keys, self.have = sides, part, keys, []

    def grow(self, axis, bit, *others, upper=None):
        if others:
            self.part = after(self.part, *others)
        upper = self.sides[axis, bit][2] if upper is None else upper
        dim = sum(self.keys.index(k) < self.keys.index((axis, bit)) for k in self.have)
        self.part = join(upper, self.part, swap(self.part, axis, bit), dim)
        self.have.append((axis, bit))
        return self


def body(
    tokens,
    cotangent,
    size_group,
    assignment,
    ln1_gain,
    ln1_bias,
    w_qkv,
    q_bias,
    v_bias,
    w_proj,
    proj_bias,
    ln2_gain,
    ln2_bias,
    w_up,
    up_bias,
    w_down,
    down_bias,
):
    rows, width = tokens.shape
    shards = lax.axis_size("fsdp")
    size = width // shards
    devices = shards * lax.axis_size("dp")
    device = lax.axis_index("fsdp") * lax.axis_size("dp") + lax.axis_index("dp")
    table = image_table(size_group, assignment, device, size_group.shape[0] // devices)

    bits = [1 << b for b in range(shards.bit_length() - 1)]
    far, near, y = bits[2:], bits[1:2], bits[0]
    tail_keys = [("fsdp", b) for b in reversed(bits)]
    sides = sides_of({"dp": (1, 2), "fsdp": bits})
    core, column = sides["dp", 1][0], sides["dp", 2][0]

    vectors = jnp.stack([ln1_gain, ln1_bias, q_bias, v_bias]).T
    pair = w_qkv.reshape(size, 3, 2, PAIR_DIM)
    pair = lax.dynamic_index_in_dim(pair, core, 2, keepdims=False).reshape(size, 3 * PAIR_DIM)
    pair = jnp.concatenate([pair, vectors, jnp.zeros((size, VEC_PAIR - 4), BF16)], axis=1)
    quarter = 2 * core + column
    vectors = jnp.stack([proj_bias, ln2_gain, ln2_bias, down_bias]).T
    extra = jnp.concatenate(
        [
            w_proj.reshape(size, width),
            vectors,
            up_bias.reshape(QUARTERS, size).T,
            jnp.zeros((size, VEC - 4 - QUARTERS), BF16),
        ],
        axis=1,
    )
    up = lax.dynamic_index_in_dim(w_up.reshape(size, shards, QUARTERS, size), quarter, 2, False)
    part_a = jnp.concatenate(
        [up.reshape(size, width), lax.dynamic_slice_in_dim(extra, quarter * VEC, VEC, 1)], axis=1
    )
    part_b = lax.dynamic_index_in_dim(w_down.reshape(QUARTERS, size, width), quarter, 0, False)

    f = Gather(sides, pair, tail_keys)
    ab = Gather(sides, jnp.concatenate([part_a, part_b], axis=1), [("dp", 2)] + tail_keys)
    for bit in far:
        ab.grow("fsdp", bit)
    for bit in near:
        f.grow("fsdp", bit)
    ab.grow("dp", 2, f.part)
    for bit in far:
        f.grow("fsdp", bit)
    for bit in near:
        ab.grow("fsdp", bit, f.part)
    f.grow("fsdp", y)
    own = f.part.reshape(width, -1)
    ab.part = after(ab.part, own)
    wf = (own, swap(own, "dp", 1))

    upper = jnp.broadcast_to(sides["fsdp", y][2], (8, ab.part.shape[-1])).astype(jnp.int32)
    table, sides, upper = lax.optimization_barrier((table, sides, upper))
    attn0, attn1, qkv0, qkv1, xhat, lse0, lse1, wpad0, wpad1, upper = attn_fwd(
        table, tokens, wf, (ab.part,), (upper,)
    )
    ab.grow("fsdp", y, upper=upper[0] != 0)
    w = ab.part.reshape(2, width, -1)
    w = (w, swap(w, "dp", 1))
    x1, act, dx1, dattn0, dattn1, keep_a, send_a, keep_b, send_b = mlp(
        table, tokens, cotangent, (attn0, attn1), w, shards
    )

    def by_bits(value, lead):
        if size % 16:
            value = value.reshape(value.shape[:lead] + (2,) * len(bits) + (size, value.shape[-1]))
            order = [lead + b for b in reversed(range(len(bits)))]
            return value.transpose(*range(lead), *order, *range(lead + len(bits), value.ndim))
        return value.reshape(value.shape[:lead] + (2,) * len(bits) + (size, value.shape[-1]))

    def halves_of_b(value):
        if size % 16:
            value = value.swapaxes(0, 1).reshape(2, width, width)
            return by_bits(value, 1).swapaxes(0, 1)
        return value.reshape((2, 2) + (2,) * (len(bits) - 1) + (size, width))

    got_a, got_b = swap(send_a, "dp", 1), swap(send_b, "dp", 1)
    d1, send_g, keep_a, keep_b = attn_bwd(
        table, qkv1, xhat, lse1, dattn1, wpad1, wf[1], False, shards, (send_a, send_b), (keep_a, keep_b)
    )
    got_g = swap(send_g, "dp", 1)
    keep_a, send_a = pick(sides, by_bits(added(keep_a, got_a), 1), "dp", 2, 0)
    keep_b, send_b = pick(sides, halves_of_b(added(keep_b, got_b)), "fsdp", y, 0)
    got_a, got_b = swap(send_a, "dp", 2), swap(send_b, "fsdp", y)
    d0, keep_g, keep_a, keep_b = attn_bwd(
        table, qkv0, xhat, lse0, dattn0, wpad0, wf[0], True, shards, (send_a, send_b, send_g), (keep_a, keep_b)
    )
    keep_g, send_g = pick(sides, by_bits(added(keep_g, got_g), 0), "fsdp", y, 0)
    keep_a, send_a = pick(sides, added(keep_a, got_a), "fsdp", y, 0)
    keep_b, send_b = pick(sides, added(keep_b, got_b), "dp", 2, 0)
    got_g = swap(send_g, "fsdp", y)
    got_a, got_b = swap(send_a, "fsdp", y), swap(send_b, "dp", 2)
    layer_out, keep_g, keep_a, keep_b = layer_output(
        table, x1, act, w, (send_g, send_a, send_b), (keep_g, keep_a, keep_b)
    )
    part_g = added(keep_g, got_g)
    part = jnp.concatenate([added(keep_a, got_a), added(keep_b, got_b)], axis=-1)
    for count, bit in enumerate(bits[1:]):
        keep_g, send_g = pick(sides, part_g, "fsdp", bit, 0)
        keep, send = pick(sides, part, "fsdp", bit, 0)
        got_g, got = swap(send_g, "fsdp", bit), swap(send, "fsdp", bit)
        if count == 0:
            grad_input, keep_g, keep = input_grad(
                table, tokens, (d0, d1), (wpad0, wpad1), wf[0], dx1, (send_g, send), (keep_g, keep)
            )
        part_g, part = added(keep_g, got_g), added(keep, got)
    part_g = added(part_g, swap(part_g, "dp", 2))
    part = join(sides["dp", 2][2], part, swap(part, "dp", 2), 0)
    part_g = join(sides["dp", 1][2], part_g, swap(part_g, "dp", 1), 0).astype(F32)
    part = join(sides["dp", 1][2], part, swap(part, "dp", 1), 0).astype(F32)

    grad_qkv = part_g[:, :, : 3 * PAIR_DIM].reshape(2, size, 3, PAIR_DIM).transpose(1, 2, 0, 3)
    ends = (part_g[0, :, 3 * PAIR_DIM : 3 * PAIR_DIM + 4] + part_g[1, :, 3 * PAIR_DIM : 3 * PAIR_DIM + 4]).T
    part = part.reshape(QUARTERS, size, -1)
    grad_up = part[:, :, :width].reshape(QUARTERS, size, shards, size).transpose(1, 2, 0, 3)
    extra = part[:, :, width : width + VEC].transpose(1, 0, 2).reshape(size, QUARTERS * VEC)
    more = extra[:, width : width + 4 + QUARTERS].T
    return (
        layer_out,
        grad_input,
        ends[0],
        ends[1],
        grad_qkv.reshape(-1),
        ends[2],
        ends[3],
        extra[:, :width].reshape(-1),
        more[0],
        more[1],
        more[2],
        grad_up.reshape(-1),
        more[4:].reshape(-1),
        part[:, :, width + VEC :].reshape(-1),
        more[3],
    )


def solution(mesh):
    rows = P(("fsdp", "dp"), None)
    flat = P("fsdp")
    return jax.shard_map(
        body,
        mesh=mesh,
        in_specs=(rows, rows, P(), P()) + (flat,) * 13,
        out_specs=(rows, rows) + (flat,) * 13,
        check_vma=False,
    )
```

```python
from functools import partial
import math

import jax
import jax.numpy as jnp
from jax import lax
from jax.experimental import pallas as pl
from jax.experimental.pallas import tpu as pltpu
from jax.sharding import PartitionSpec as P

HEAD_DIM = 96
HEAD_PAD = 128
LENS = (196, 256, 400)
SLOT = 400
ROW_PAD = 32
PAIR = 2
PAIR_DIM = PAIR * HEAD_DIM
PAIR_PAD = PAIR * HEAD_PAD
QUARTERS = 4
VEC = 128
VEC_PAIR = 64
SCALE = 1.0 / math.sqrt(HEAD_DIM)
EXP_SCALE = SCALE * math.log2(math.e)
MIB = 1024 * 1024
VMEM = {"attn_fwd": 12, "mlp": 26, "attn_bwd": 8, "layer_out": 8, "input_grad": 10, "finish": 10}
F32 = jnp.float32
BF16 = jnp.bfloat16


def dot_nn(a, b):
    return lax.dot_general(a, b, (((1,), (0,)), ((), ())), preferred_element_type=F32)


def dot_nt(a, b):
    return lax.dot_general(a, b, (((1,), (1,)), ((), ())), preferred_element_type=F32)


def dot_tn(a, b):
    return lax.dot_general(a, b, (((0,), (0,)), ((), ())), preferred_element_type=F32)


def pad_heads(values):
    rows, cols = values.shape
    gap = jnp.zeros((rows, HEAD_PAD - HEAD_DIM), values.dtype)
    parts = []
    for h in range(cols // HEAD_DIM):
        parts += [values[:, h * HEAD_DIM : (h + 1) * HEAD_DIM], gap]
    return jnp.concatenate(parts, axis=1)


def unpad_heads(values):
    rows, cols = values.shape
    return jnp.concatenate(
        [values[:, h * HEAD_PAD : h * HEAD_PAD + HEAD_DIM] for h in range(cols // HEAD_PAD)], axis=1
    )


def row_norm(x):
    center = x - jnp.mean(x, axis=-1, keepdims=True)
    inverse = lax.rsqrt(jnp.mean(center * center, axis=-1, keepdims=True) + 1e-6)
    return center * inverse, inverse


def row_norm_back(e, xhat, inverse):
    return inverse * (
        e - jnp.mean(e, axis=-1, keepdims=True) - xhat * jnp.mean(e * xhat, axis=-1, keepdims=True)
    )


def load_rows(ref, start, count):
    base = pl.multiple_of((start // 8) * 8, 8)
    window = ref[pl.ds(base, count + 8), :]
    moved = pltpu.roll(window, count + 4, 0)
    return jnp.where(start % 8 == 0, window, moved)[:count]


def store_rows(ref, start, length, values, cols):
    count = -(-length // 8) * 8
    base = pl.multiple_of((start // 8) * 8, 8)
    window = jnp.concatenate([values[:count], jnp.zeros((8, values.shape[1]), values.dtype)], axis=0)
    window = jnp.where(start % 8 == 0, window, pltpu.roll(window, 4, 0))
    row = lax.broadcasted_iota(jnp.int32, window.shape, 0) - start % 8
    held = ref[pl.ds(base, count + 8), cols]
    ref[pl.ds(base, count + 8), cols] = jnp.where((row >= 0) & (row < length), window, held)


def by_group(group, work):
    for g, length in enumerate(LENS):
        pl.when(group == g)(partial(work, length, -(-length // 16) * 16))


def gelu_pair(u):
    cdf = 0.5 + 0.5 * lax.erf(u * (1.0 / math.sqrt(2.0)))
    bell = jnp.exp2((u * u) * (-0.5 * math.log2(math.e)))
    return u * cdf, cdf + u * (bell * (1.0 / math.sqrt(2.0 * math.pi)))


def whole(array):
    at = (0,) * len(array.shape)
    return pl.BlockSpec(array.shape, lambda i, m: at, pipeline_mode=pl.Buffered(1))


def slot_block(cols):
    return pl.BlockSpec((1, SLOT, cols), lambda i, m: (i, 0, 0))


def call(kernel, name, grid, in_specs, out_specs, out_shape, scratch, args, waits=(), carry=(), far=()):
    given, made, passed = len(in_specs) + 1, len(out_shape), len(waits) + len(carry)

    def ordered(*refs):
        kernel(*refs[:given], *refs[given + passed : given + passed + made], *refs[given + passed + made + len(carry) :])

    args = [
        pltpu.with_memory_space_constraint(t, pltpu.HBM) if at in far else t for at, t in enumerate(args)
    ]
    anywhere = pl.BlockSpec(memory_space=pl.ANY)
    outs = pl.pallas_call(
        ordered,
        grid_spec=pltpu.PrefetchScalarGridSpec(
            num_scalar_prefetch=1,
            grid=(grid,),
            in_specs=list(in_specs) + [anywhere] * passed,
            out_specs=list(out_specs) + [anywhere] * len(carry),
            scratch_shapes=scratch,
        ),
        out_shape=list(out_shape) + [jax.ShapeDtypeStruct(t.shape, t.dtype) for t in carry],
        input_output_aliases={given + len(waits) + n: made + n for n in range(len(carry))},
        compiler_params=pltpu.CompilerParams(vmem_limit_bytes=VMEM[name] * MIB),
        name=name,
    )(*args, *waits, *carry)
    return outs


def groups_at(meta):
    return (meta.shape[0] - 2) // 2


def rows_used(meta):
    return meta[meta.shape[0] - 2]


def device_of(meta):
    return meta[meta.shape[0] - 1]


def core_of(meta):
    return device_of(meta) % 2


def attn_fwd_kernel(meta, tok, wf0, wf1, attn0, attn1, qkv0, qkv1, xhat_out, lse0, lse1, wpad0, wpad1,
                    tok32, out32, bias):
    i = pl.program_id(0)
    rows, width = tok.shape
    cols = 3 * PAIR_PAD
    sides = ((wf0, qkv0, lse0, wpad0), (wf1, qkv1, lse1, wpad1))

    @pl.when(i == 0)
    def _():
        tok32[:rows] = tok[...].astype(F32)
        tok32[rows:] = jnp.zeros((tok32.shape[0] - rows, width), F32)
        vec = wf0[:, 3 * PAIR_DIM :].astype(F32).T
        bias[0:2, :width] = vec[0:2]
        for c in range(2):

            @pl.when(core_of(meta) == c)
            def _():
                for p in range(2):
                    at = (p ^ c) * PAIR_DIM
                    parts = [pad_heads(vec[r : r + 1, at : at + PAIR_DIM]) for r in (2, 3)]
                    bias[2 + p : 3 + p, :] = jnp.concatenate(
                        [parts[0], jnp.zeros((1, PAIR_PAD), F32), parts[1]], axis=1
                    )

        for wf, _, _, wpad in sides:
            wpad[...] = pad_heads(wf[:, : 3 * PAIR_DIM].astype(F32)).astype(BF16)

    start = meta[i]

    def work(length, padded):
        xhat, _ = row_norm(load_rows(tok32, start, padded))
        normed = (xhat * bias[0:1, :width] + bias[1:2, :width]).astype(BF16)
        xhat_out[0, :padded, :] = xhat.astype(BF16)
        for p, (_, qkv, lse, wpad) in enumerate(sides):
            qkv[0, :padded, :] = (dot_nn(normed, wpad[...]) + bias[2 + p : 3 + p, :]).astype(BF16)
        heads = [(p, h) for p in range(2) for h in range(PAIR)]
        scores = []
        for p, h in heads:
            qkv, at = sides[p][1], h * HEAD_PAD
            q = qkv[0, :padded, at : at + HEAD_PAD]
            k = qkv[0, :padded, PAIR_PAD + at : PAIR_PAD + at + HEAD_PAD]
            scores.append(dot_nt(k, q))
        probs = []
        for (p, h), s in zip(heads, scores):
            if length < padded:
                key = lax.broadcasted_iota(jnp.int32, s.shape, 0)
                s = jnp.where(key < length, s, -1e30)
            top = jnp.max(s, axis=0, keepdims=True)
            e = jnp.exp2((s - top) * EXP_SCALE)
            total = jnp.sum(e, axis=0, keepdims=True)
            probs.append((e * (1.0 / total)).astype(BF16))
            sides[p][2][0, h : h + 1, :padded] = top * EXP_SCALE + jnp.log2(total)
        outs = []
        for (p, h), prob in zip(heads, probs):
            at = 2 * PAIR_PAD + h * HEAD_PAD
            outs.append(dot_tn(prob, sides[p][1][0, :padded, at : at + HEAD_PAD]))
        store_rows(out32, start, length, jnp.concatenate(outs, axis=1), slice(None))

    by_group(meta[groups_at(meta) + i], work)

    @pl.when(i == pl.num_programs(0) - 1)
    def _():
        row = lax.broadcasted_iota(jnp.int32, (rows, 1), 0)
        mixed = jnp.where(row < rows_used(meta), out32[:rows], 0.0).astype(BF16)
        attn0[...] = mixed[:, :PAIR_PAD]
        attn1[...] = mixed[:, PAIR_PAD:]


def attn_fwd(meta, tokens, wf, waits, carry):
    rows, width = tokens.shape
    slots = groups_at(meta)
    cols = 3 * PAIR_PAD
    out_shape = [jax.ShapeDtypeStruct((rows, PAIR_PAD), BF16)] * 2
    out_shape += [jax.ShapeDtypeStruct((slots, SLOT, cols), BF16)] * 2
    out_shape += [jax.ShapeDtypeStruct((slots, SLOT, width), BF16)]
    out_shape += [jax.ShapeDtypeStruct((slots, 8, 512), F32)] * 2
    out_shape += [jax.ShapeDtypeStruct((width, cols), BF16)] * 2
    stats = pl.BlockSpec((1, 8, 512), lambda i, m: (i, 0, 0))
    out_specs = [whole(out_shape[0])] * 2 + [slot_block(cols)] * 2 + [slot_block(width)]
    out_specs += [stats] * 2 + [whole(out_shape[-1])] * 2
    scratch = [
        pltpu.VMEM((rows + ROW_PAD, width), F32),
        pltpu.VMEM((rows + ROW_PAD, 2 * PAIR_PAD), F32),
        pltpu.VMEM((8, cols), F32),
    ]
    in_specs = [whole(tokens), whole(wf[0]), whole(wf[1])]
    args = (meta, tokens, *wf)
    return call(attn_fwd_kernel, "attn_fwd", slots, in_specs, out_specs, out_shape, scratch, args, waits, carry)


def put_blocks(to, value, col, shards, parity=None):
    rows, cols = value.shape
    size = rows // shards
    half = rows // 2
    if size % 16:
        if parity is not None:
            value = value[parity * half : (parity + 1) * half]
        to[:, col : col + cols] = value
        return
    for n, place in enumerate(turned(shards)):
        at = place * size
        if parity is not None:
            if n % 2 != parity:
                continue
            at -= parity * half
        to[at : at + size, col : col + cols] = value[n * size : (n + 1) * size]


def mlp_kernel(meta, tok, cot, attn0, attn1, w0, w1, b0, b1, x1o, acto, dx1, da0, da1,
               keep_a, send_a, keep_b, send_b, wproj, rowvec, gd, gu, gp, gsum, *, shards):
    i = pl.program_id(0)
    rows, width = tok.shape
    parts = (w0, w1)
    lower = (b0, b1)

    def in_order(first, second, use):
        for c in range(2):
            pl.when(core_of(meta) == c)(partial(use, c, *((first, second) if c == 0 else (second, first))))

    @pl.when(i == 0)
    def _():
        def use(c, low, high):
            flat = [ref[x][:, width : width + VEC] for ref in (low, high) for x in range(2)]
            proj = jnp.concatenate(flat[: width // VEC], axis=1)
            wproj[...] = jnp.zeros(wproj.shape, BF16)
            for h in range(2 * PAIR):
                at = (h ^ (PAIR * c)) * HEAD_PAD
                wproj[at : at + HEAD_DIM] = proj[h * HEAD_DIM : (h + 1) * HEAD_DIM]
            vec = flat[-1].astype(F32).T
            for r in range(4):
                rowvec[r : r + 1, :width] = vec[r : r + 1]
                at = (r ^ (2 * c)) * width
                rowvec[4:5, at : at + width] = vec[4 + r : 5 + r]

        in_order(w0, w1, use)
        gd[...] = jnp.zeros(gd.shape, F32)
        gu[...] = jnp.zeros(gu.shape, F32)
        gp[...] = jnp.zeros(gp.shape, F32)
        gsum[...] = jnp.zeros(gsum.shape, F32)

    proj_bias, gain, shift, down_bias = [rowvec[r : r + 1, :width] for r in range(4)]
    row = lax.broadcasted_iota(jnp.int32, (rows, 1), 0) + i * rows
    valid = (row < rows_used(meta)).astype(F32)
    dy = cot[...].astype(F32) * valid
    dyb = dy.astype(BF16)
    chunk = 2 * width
    ups = [jnp.concatenate([parts[c][0][:, :width], parts[c][1][:, :width]], axis=1) for c in range(2)]
    downs = [jnp.concatenate([lower[c][x] for x in range(2)], axis=0) for c in range(2)]
    dacts = [dot_nt(dyb, downs[c]) for c in range(2)]
    mixed0, mixed1 = attn0[...], attn1[...]
    x1 = tok[...].astype(F32) + dot_nn(mixed0, wproj[:PAIR_PAD]) + dot_nn(mixed1, wproj[PAIR_PAD:])
    x1 = x1 + proj_bias
    x1o[...] = (x1 + down_bias) * valid
    xhat, inverse = row_norm(x1)
    normed = (xhat * gain + shift).astype(BF16)
    dn = jnp.zeros((rows, width), F32)
    kept = []
    for c in range(2):
        at = c * chunk
        pre = dot_nn(normed, ups[c]) + rowvec[4:5, at : at + chunk]
        act, slope = gelu_pair(pre)
        actb = act.astype(BF16)
        acto[:, at : at + chunk] = actb
        dpre = dacts[c] * slope
        dpreb = dpre.astype(BF16)
        gsum[4:5, at : at + chunk] += jnp.sum(dpre, axis=0, keepdims=True)
        dn = dn + dot_nt(dpreb, ups[c])
        kept.append(dpreb)
    for c in range(2):
        at = c * chunk
        gd[:, at : at + chunk] += dot_tn(dyb, acto[:, at : at + chunk])
        gu[:, at : at + chunk] += dot_tn(normed, kept[c])
    dx = dy + row_norm_back(dn * gain, xhat, inverse)
    dx1[...] = dx
    dxb = dx.astype(BF16)
    gp[:, :PAIR_PAD] += dot_tn(dxb, mixed0)
    gp[:, PAIR_PAD:] += dot_tn(dxb, mixed1)
    da0[...] = dot_nt(dxb, wproj[:PAIR_PAD]).astype(BF16)
    da1[...] = dot_nt(dxb, wproj[PAIR_PAD:]).astype(BF16)
    gsum[0:1, :width] += jnp.sum(dx, axis=0, keepdims=True)
    gsum[1:2, :width] += jnp.sum(dn * xhat, axis=0, keepdims=True)
    gsum[2:3, :width] += jnp.sum(dn, axis=0, keepdims=True)
    gsum[3:4, :width] += jnp.sum(dy, axis=0, keepdims=True)

    @pl.when(i == pl.num_programs(0) - 1)
    def _():
        for half, (to_a, to_b) in enumerate(((keep_a, keep_b), (send_a, send_b))):
            for x in range(2):
                at = (2 * half + x) * width
                put_blocks(to_a.at[x], gu[:, at : at + width].astype(BF16), 0, shards)
                part = gd[:, at : at + width].T.astype(BF16)
                for y in range(2):
                    put_blocks(to_b.at[y, x], part, 0, shards, y)

        def use(c, low, high):
            rows_of = [gsum[r : r + 1, :width] for r in range(4)]
            for r in range(4):
                at = (r ^ (2 * c)) * width
                rows_of.append(gsum[4:5, at : at + width])
            vec = jnp.concatenate(rows_of + [jnp.zeros((VEC - 8, width), F32)], axis=0).T
            grad = unpad_heads(gp[...]).T
            first, second = grad[:PAIR_DIM], grad[PAIR_DIM:]
            proj = jnp.concatenate([second, first] if c else [first, second], axis=0)
            flat = jnp.concatenate([proj, vec], axis=1).astype(BF16)
            for k in range(QUARTERS):
                to = (low, high)[k // 2].at[k % 2]
                put_blocks(to, flat[:, k * VEC : (k + 1) * VEC], width, shards)

        in_order(keep_a, send_a, use)


def mlp(meta, tokens, cotangent, attn, w, shards, block=512):
    rows, width = tokens.shape
    hidden = QUARTERS * width
    by_row = lambda cols: pl.BlockSpec((block, cols), lambda i, m: (i, 0))
    out_shape = [
        pltpu.HBM((rows, width), F32),
        pltpu.HBM((rows, hidden), BF16),
        pltpu.HBM((rows, width), F32),
        jax.ShapeDtypeStruct((rows, PAIR_PAD), BF16),
        jax.ShapeDtypeStruct((rows, PAIR_PAD), BF16),
    ]
    out_shape += [jax.ShapeDtypeStruct((2, width, width + VEC), BF16)] * 2
    out_shape += [jax.ShapeDtypeStruct((2, 2, width // 2, width), BF16)] * 2
    out_specs = [by_row(s.shape[1]) for s in out_shape[:5]] + [whole(s) for s in out_shape[5:]]
    in_specs = [by_row(width)] * 2 + [by_row(PAIR_PAD)] * 2 + [whole(t) for t in w]
    scratch = [
        pltpu.VMEM((2 * PAIR_PAD, width), BF16),
        pltpu.VMEM((8, hidden), F32),
        pltpu.VMEM((width, hidden), F32),
        pltpu.VMEM((width, hidden), F32),
        pltpu.VMEM((width, 2 * PAIR_PAD), F32),
        pltpu.VMEM((8, hidden), F32),
    ]
    args = (meta, tokens, cotangent, *attn, *w)
    kernel = partial(mlp_kernel, shards=shards)
    return call(kernel, "mlp", rows // block, in_specs, out_specs, out_shape, scratch, args)


def layer_out_kernel(meta, x1, act, b0, b1, out):
    rows, width = x1.shape
    row = lax.broadcasted_iota(jnp.int32, (rows, 1), 0) + pl.program_id(0) * rows
    valid = (row < rows_used(meta)).astype(F32)
    y = x1[...]
    for c, ref in enumerate((b0, b1)):
        down = jnp.concatenate([ref[x] for x in range(2)], axis=0)
        y = y + dot_nn(act[:, 2 * c * width : 2 * (c + 1) * width], down) * valid
    out[...] = y.astype(BF16)


def layer_output(meta, x1, act, w, waits, carry, block=512):
    rows, width = x1.shape
    by_row = lambda cols: pl.BlockSpec((block, cols), lambda i, m: (i, 0))
    return call(
        layer_out_kernel,
        "layer_out",
        rows // block,
        [by_row(width), by_row(act.shape[1]), whole(w[0]), whole(w[1])],
        [by_row(width)],
        [jax.ShapeDtypeStruct((rows, width), BF16)],
        [],
        (meta, x1, act, *w),
        waits,
        carry,
        (1, 2),
    )


def attn_bwd_kernel(meta, qkv, xhat, lse, dattn, wpad, wf, dqkv, grads, da32, gw, gsum, *, own, shards):
    i = pl.program_id(0)
    rows = dattn.shape[0]
    width = wf.shape[0]

    @pl.when(i == 0)
    def _():
        da32[:rows] = dattn[...].astype(F32)
        da32[rows:] = jnp.zeros((da32.shape[0] - rows, PAIR_PAD), F32)
        gw[...] = jnp.zeros(gw.shape, F32)
        gsum[...] = jnp.zeros(gsum.shape, F32)

    start = meta[i]

    def work(length, padded):
        da = load_rows(da32, start, padded)
        if length < padded:
            keep = lax.broadcasted_iota(jnp.int32, (padded, 1), 0) < length
            da = jnp.where(keep, da, 0.0)
        da = da.astype(BF16)
        def cut(ref, part, h):
            at = part * PAIR_PAD + h * HEAD_PAD
            return ref[0, :padded, at : at + HEAD_PAD]

        heads = range(PAIR)
        das = [da[:, h * HEAD_PAD : (h + 1) * HEAD_PAD] for h in heads]
        scores = [dot_nt(cut(qkv, 1, h), cut(qkv, 0, h)) for h in heads]
        dps = [dot_nt(cut(qkv, 2, h), das[h]) for h in heads]
        ps, dss = [], []
        for h in heads:
            p = jnp.exp2(scores[h] * EXP_SCALE - lse[0, h : h + 1, :padded])
            if length < padded:
                key = lax.broadcasted_iota(jnp.int32, p.shape, 0)
                p = jnp.where(key < length, p, 0.0)
            mean = jnp.sum(p * dps[h], axis=0, keepdims=True)
            dss.append((p * (dps[h] - mean)).astype(BF16))
            ps.append(p.astype(BF16))
        parts = [[dot_tn(dss[h], cut(qkv, 1, h)) * SCALE for h in heads]]
        parts += [[dot_nn(dss[h], cut(qkv, 0, h)) * SCALE for h in heads]]
        parts += [[dot_nn(ps[h], das[h]) for h in heads]]
        d = []
        for part in range(3):
            value = jnp.concatenate(parts[part], axis=1)
            at = part * PAIR_PAD
            if part != 1:
                gsum[0:1, at : at + PAIR_PAD] += jnp.sum(value, axis=0, keepdims=True)
            d.append(value.astype(BF16))
        d = jnp.concatenate(d, axis=1)
        dqkv[0, :padded, :] = d
        gw[...] += dot_tn(xhat[0, :padded, :], d)
        gsum[1:2, :] += jnp.sum(d.astype(F32), axis=0, keepdims=True)

    by_group(meta[groups_at(meta) + i], work)

    @pl.when(i == pl.num_programs(0) - 1)
    def _():
        w = wpad[...].astype(F32)
        raw = gw[...]
        col = gsum[1:2, :]
        gain_term = jnp.sum(raw * w, axis=1, keepdims=True)
        bias_term = jnp.sum(col * w, axis=1, keepdims=True)
        vec = wf[:, 3 * PAIR_DIM :].astype(F32)
        main = unpad_heads(raw * vec[:, 0:1] + vec[:, 1:2] * col).astype(BF16)
        put_blocks(grads, main, 0, shards)
        q_sum = unpad_heads(gsum[0:1, :PAIR_PAD])
        v_sum = unpad_heads(gsum[0:1, 2 * PAIR_PAD :])
        gap = jnp.zeros((1, width - PAIR_DIM), F32)
        for c in range(2):

            @pl.when(core_of(meta) == (c if own else 1 - c))
            def _():
                rows_of = [jnp.concatenate([gap, t] if c else [t, gap], axis=1) for t in (q_sum, v_sum)]
                rows_of = [jnp.zeros((2, width), F32)] + rows_of + [jnp.zeros((VEC - 4, width), F32)]
                sums = jnp.concatenate(rows_of, axis=0).T
                lane = lax.broadcasted_iota(jnp.int32, sums.shape, 1)
                tail = jnp.where(lane == 0, gain_term, jnp.where(lane == 1, bias_term, sums))
                put_blocks(grads, tail[:, :VEC_PAIR].astype(BF16), 3 * PAIR_DIM, shards)


def attn_bwd(meta, qkv, xhat, lse, dattn, wpad, wf, own, shards, waits, carry):
    rows = dattn.shape[0]
    width = wf.shape[0]
    cols = 3 * PAIR_PAD
    out_shape = [jax.ShapeDtypeStruct(qkv.shape, BF16), jax.ShapeDtypeStruct(wf.shape, BF16)]
    in_specs = [slot_block(cols), slot_block(width), pl.BlockSpec((1, 8, 512), lambda i, m: (i, 0, 0))]
    in_specs += [whole(dattn), whole(wpad), whole(wf)]
    scratch = [
        pltpu.VMEM((rows + ROW_PAD, PAIR_PAD), F32),
        pltpu.VMEM((width, cols), F32),
        pltpu.VMEM((8, cols), F32),
    ]
    args = (meta, qkv, xhat, lse, dattn, wpad, wf)
    kernel = partial(attn_bwd_kernel, own=own, shards=shards)
    out_specs = [slot_block(cols), whole(wf)]
    grid = groups_at(meta)
    return call(kernel, "attn_bwd", grid, in_specs, out_specs, out_shape, scratch, args, waits, carry)


def input_grad_kernel(meta, tok, d0, d1, w0, w1, wf, dx1, out, tok32, bias):
    i = pl.program_id(0)
    rows, width = tok.shape

    @pl.when(i == 0)
    def _():
        tok32[:rows] = tok[...].astype(F32)
        tok32[rows:] = jnp.zeros((tok32.shape[0] - rows, width), F32)
        bias[...] = wf[:, 3 * PAIR_DIM :].astype(F32).T[0:8]

    start = meta[i]

    def work(length, padded):
        dn = dot_nt(d0[0, :padded, :], w0[...]) + dot_nt(d1[0, :padded, :], w1[...])
        xhat, inverse = row_norm(load_rows(tok32, start, padded))
        dx = row_norm_back(dn * bias[0:1, :], xhat, inverse)
        store_rows(tok32, start, length, dx, slice(None))

    by_group(meta[groups_at(meta) + i], work)

    @pl.when(i == pl.num_programs(0) - 1)
    def _():
        row = lax.broadcasted_iota(jnp.int32, (rows, 1), 0)
        total = dx1[...] + tok32[:rows]
        out[...] = jnp.where(row < rows_used(meta), total, 0.0).astype(BF16)


def input_grad(meta, tokens, d, w, wf, dx1, waits, carry):
    rows, width = tokens.shape
    slot = slot_block(d[0].shape[2])
    in_specs = [whole(tokens), slot, slot] + [whole(t) for t in (*w, wf, dx1)]
    scratch = [pltpu.VMEM((rows + ROW_PAD, width), F32), pltpu.VMEM((8, width), F32)]
    out_shape = [jax.ShapeDtypeStruct((rows, width), BF16)]
    args = (meta, tokens, *d, *w, wf, dx1)
    grid, out_specs = groups_at(meta), [whole(tokens)]
    return call(
        input_grad_kernel, "input_grad", grid, in_specs, out_specs, out_shape, scratch, args, waits, carry
    )


def final_parts(core, own, got, shards):
    size = own.shape[0]
    width = shards * size
    cut = 3 * PAIR_DIM + VEC_PAIR
    low, high = (got, own) if core else (own, got)
    qkv = [t[:, part * PAIR_DIM : (part + 1) * PAIR_DIM] for part in range(3) for t in (low, high)]
    step = (low.shape[1] - cut) // 2
    quarters = [t[:, cut + x * step : cut + (x + 1) * step] for t in (low, high) for x in range(2)]
    extra_at, down_at = width, width + VEC
    extra = [q[:, extra_at:down_at] for q in quarters]
    up = [q[:, n * size : (n + 1) * size] for n in range(shards) for q in quarters]
    down = jnp.concatenate([q[:, down_at:] for q in quarters], axis=0)
    ends = low[:, 3 * PAIR_DIM : cut] + high[:, 3 * PAIR_DIM : cut]
    columns = jnp.concatenate([ends[:, :4], extra[-1][:, : 4 + QUARTERS]], axis=1)
    cat = lambda parts: jnp.concatenate(parts, axis=1)
    return cat(qkv), cat(extra[: width // VEC]), cat(up), down, columns


def finish_kernel(meta, own, got, *outs, shards):
    size = own.shape[0]

    def use(core):
        *mats, columns = final_parts(core, own[...].astype(F32), got[...].astype(F32), shards)
        for mat, out in zip(mats, outs):
            tiles = mat.shape[1] // 128
            for t in range(tiles):
                out[pl.ds(t, mat.shape[0], stride=tiles), :] = mat[:, t * 128 : (t + 1) * 128]
        count = columns.shape[1]
        square = jnp.concatenate([columns, jnp.zeros((size, 128 - count), F32)], axis=1)
        square = jnp.concatenate([square, jnp.zeros((128 - size, 128), F32)], axis=0)
        outs[4][...] = square.T[:16]

    for c in range(2):
        pl.when(core_of(meta) == c)(partial(use, c))


def finish(meta, own, got, shards):
    size = own.shape[0]
    width = shards * size
    if size % 16:
        core = core_of(meta) == 1
        own, got = own.astype(F32), got.astype(F32)
        parts = final_parts(0, jnp.where(core, got, own), jnp.where(core, own, got), shards)
        return [p.reshape(-1) for p in parts[:4]], parts[4].T
    sizes = [size * 3 * width, size * width, size * QUARTERS * width, size * QUARTERS * width]
    out_shape = [jax.ShapeDtypeStruct((n // 128, 128), F32) for n in sizes + [16 * 128]]
    out_specs = [whole(t) for t in out_shape]
    kernel = partial(finish_kernel, shards=shards)
    outs = call(kernel, "finish", 1, [whole(own), whole(got)], out_specs, out_shape, [], (meta, own, got))
    return [t.reshape(-1) for t in outs[:4]], outs[4]


def turned(shards):
    count = shards.bit_length() - 1
    return [sum(((n >> b) & 1) << (count - 1 - b) for b in range(count)) for n in range(shards)]


def image_table(size_group, assignment, device, slots):
    owned = assignment == device
    rank = jnp.cumsum(owned.astype(jnp.int32)) - 1
    slot = jnp.arange(slots, dtype=jnp.int32)
    here = owned[None, :] & (rank[None, :] == slot[:, None])
    groups = jnp.sum(jnp.where(here, size_group[None, :], 0), axis=1)
    lengths = jnp.where(groups == 0, LENS[0], jnp.where(groups == 1, LENS[1], LENS[2]))
    ends = jnp.sum(jnp.where(slot[None, :] <= slot[:, None], lengths[None, :], 0), axis=1)
    return jnp.concatenate([ends - lengths, groups, ends[-1:], device[None]]).astype(jnp.int32)


def swap(value, axis, bit):
    size = lax.axis_size(axis)
    return lax.ppermute(value, axis, [(i, i ^ bit) for i in range(size)])


def sides_of(bits):
    table = {}
    for axis, those in bits.items():
        for bit in those:
            mine = (lax.axis_index(axis) & bit) // bit
            table[axis, bit] = (mine.astype(jnp.uint32), (1 - mine).astype(jnp.uint32), mine == 1)
    return table


def pick(sides, value, axis, bit, dim):
    mine, theirs, _ = sides[axis, bit]
    keep = lax.dynamic_index_in_dim(value, mine, dim, keepdims=False)
    send = lax.dynamic_index_in_dim(value, theirs, dim, keepdims=False)
    return keep, send


def join(upper, own, other, dim):
    return jnp.stack([jnp.where(upper, other, own), jnp.where(upper, own, other)], axis=dim)


def added(keep, got):
    return (keep.astype(F32) + got.astype(F32)).astype(BF16)


def after(value, *others):
    return lax.optimization_barrier((value, *others))[0]


class Gather:
    def __init__(self, sides, part, keys):
        self.sides, self.part, self.keys, self.have = sides, part, keys, []

    def grow(self, axis, bit, *others, upper=None):
        if others:
            self.part = after(self.part, *others)
        upper = self.sides[axis, bit][2] if upper is None else upper
        dim = sum(self.keys.index(k) < self.keys.index((axis, bit)) for k in self.have)
        self.part = join(upper, self.part, swap(self.part, axis, bit), dim)
        self.have.append((axis, bit))
        return self


def body(
    tokens,
    cotangent,
    size_group,
    assignment,
    ln1_gain,
    ln1_bias,
    w_qkv,
    q_bias,
    v_bias,
    w_proj,
    proj_bias,
    ln2_gain,
    ln2_bias,
    w_up,
    up_bias,
    w_down,
    down_bias,
):
    rows, width = tokens.shape
    shards = lax.axis_size("fsdp")
    size = width // shards
    devices = shards * lax.axis_size("dp")
    device = lax.axis_index("fsdp") * lax.axis_size("dp") + lax.axis_index("dp")
    table = image_table(size_group, assignment, device, size_group.shape[0] // devices)

    bits = [1 << b for b in range(shards.bit_length() - 1)]
    far, near, y = bits[2:], bits[1:2], bits[0]
    tail_keys = [("fsdp", b) for b in reversed(bits)]
    sides = sides_of({"dp": (1, 2), "fsdp": bits})
    core, column = sides["dp", 1][0], sides["dp", 2][0]

    vectors = [ln1_gain, ln1_bias, q_bias, v_bias, proj_bias, ln2_gain, ln2_bias, down_bias]
    vectors = jnp.concatenate([jnp.stack(vectors), up_bias.reshape(QUARTERS, size)]).T
    pair = w_qkv.reshape(size, 3, 2, PAIR_DIM)
    pair = lax.dynamic_index_in_dim(pair, core, 2, keepdims=False).reshape(size, 3 * PAIR_DIM)
    pair = jnp.concatenate([pair, vectors[:, :4], jnp.zeros((size, VEC_PAIR - 4), BF16)], axis=1)
    f = Gather(sides, pair, tail_keys)
    w_up, w_down, w_proj, _ = lax.optimization_barrier((w_up, w_down, w_proj, pair))
    quarter = 2 * core + column
    extra = [w_proj.reshape(size, width), vectors[:, 4:], jnp.zeros((size, VEC - 4 - QUARTERS), BF16)]
    extra = lax.dynamic_slice_in_dim(jnp.concatenate(extra, axis=1), quarter * VEC, VEC, 1)
    up = lax.dynamic_index_in_dim(w_up.reshape(size, shards, QUARTERS, size), quarter, 2, False)
    part_a = jnp.concatenate([up.reshape(size, width), extra], axis=1)
    part_b = lax.dynamic_index_in_dim(w_down.reshape(QUARTERS, size, width), quarter, 0, False)
    ab = Gather(sides, jnp.concatenate([part_a, part_b], axis=1), tail_keys)

    for bit in far:
        f.grow("fsdp", bit)
    for bit in far:
        ab.grow("fsdp", bit)
    for bit in near:
        f.grow("fsdp", bit)
    for bit in near:
        ab.grow("fsdp", bit)
    f.grow("fsdp", y)
    own = f.part.reshape(width, -1)
    cut = width + VEC
    keys = [("dp", 2)] + tail_keys
    a, b = Gather(sides, ab.part[..., :cut], keys), Gather(sides, ab.part[..., cut:], keys)
    a.have, b.have = list(ab.have), list(ab.have)
    a.grow("dp", 2)
    b.grow("fsdp", y)
    wf = (own, swap(own, "dp", 1))

    upper = jnp.stack([sides["fsdp", y][2], sides["dp", 2][2]])
    upper = jnp.broadcast_to(upper[:, None, None], (2, 8, cut)).astype(jnp.int32)
    table, sides, upper = lax.optimization_barrier((table, sides, upper))
    attn0, attn1, qkv0, qkv1, xhat, lse0, lse1, wpad0, wpad1, upper = attn_fwd(
        table, tokens, wf, (a.part, b.part), (upper,)
    )
    a.grow("fsdp", y, upper=upper[0, 0] != 0)
    b.grow("dp", 2, upper=upper[1, 0, :width] != 0)
    wa, wb = a.part.reshape(2, width, cut), b.part.reshape(2, width, width)
    w = (wa, swap(wa, "dp", 1), wb, swap(wb, "dp", 1))
    x1, act, dx1, dattn0, dattn1, keep_a, send_a, keep_b, send_b = mlp(
        table, tokens, cotangent, (attn0, attn1), w, shards
    )

    def by_bits(value, lead):
        if size % 16:
            value = value.reshape(value.shape[:lead] + (2,) * len(bits) + (size, value.shape[-1]))
            order = [lead + b for b in reversed(range(len(bits)))]
            return value.transpose(*range(lead), *order, *range(lead + len(bits), value.ndim))
        return value.reshape(value.shape[:lead] + (2,) * len(bits) + (size, value.shape[-1]))

    def halves_of_b(value):
        if size % 16:
            value = value.swapaxes(0, 1).reshape(2, width, width)
            return by_bits(value, 1).swapaxes(0, 1)
        return value.reshape((2, 2) + (2,) * (len(bits) - 1) + (size, width))

    got_a, got_b = swap(send_a, "dp", 1), swap(send_b, "dp", 1)
    d1, send_g, keep_a, keep_b = attn_bwd(
        table, qkv1, xhat, lse1, dattn1, wpad1, wf[1], False, shards, (send_a, send_b), (keep_a, keep_b)
    )
    got_g = swap(send_g, "dp", 1)
    keep_a, send_a = pick(sides, by_bits(added(keep_a, got_a), 1), "dp", 2, 0)
    keep_b, send_b = pick(sides, halves_of_b(added(keep_b, got_b)), "fsdp", y, 0)
    got_a, got_b = swap(send_a, "dp", 2), swap(send_b, "fsdp", y)
    d0, keep_g, keep_a, keep_b = attn_bwd(
        table, qkv0, xhat, lse0, dattn0, wpad0, wf[0], True, shards, (send_a, send_b, send_g), (keep_a, keep_b)
    )
    part = jnp.concatenate([by_bits(added(keep_g, got_g), 0), added(keep_a, got_a)], axis=-1)
    keep, send = pick(sides, part, "fsdp", y, 0)
    keep_b, send_b = pick(sides, added(keep_b, got_b), "dp", 2, 0)
    got, got_b = swap(send, "fsdp", y), swap(send_b, "dp", 2)
    layer_out, keep, keep_b = layer_output(table, x1, act, w[2:], (send, send_b), (keep, keep_b))
    part = jnp.concatenate([added(keep, got), added(keep_b, got_b)], axis=-1)
    for count, bit in enumerate(bits[1:]):
        keep, send = pick(sides, part, "fsdp", bit, 0)
        got = swap(send, "fsdp", bit)
        if count == 0:
            grad_input, keep = input_grad(
                table, tokens, (d0, d1), (wpad0, wpad1), wf[0], dx1, (send,), (keep,)
            )
        part = added(keep, got)
    got = swap(part, "dp", 2)
    cut = keep_g.shape[-1]
    part_g = added(part[:, :cut], got[:, :cut])
    low, high = part[:, cut:], got[:, cut:]
    upper = sides["dp", 2][2]
    part = [part_g, jnp.where(upper, high, low), jnp.where(upper, low, high)]
    part = jnp.concatenate(part, axis=1)
    flat, vectors = finish(table, part, swap(part, "dp", 1), shards)
    g = [vectors[r, :size] for r in range(8)] + [vectors[8 : 8 + QUARTERS, :size].reshape(-1)]
    qkv, proj, up, down = flat
    return (
        layer_out, grad_input, g[0], g[1], qkv, g[2], g[3], proj, g[4], g[5], g[6], up, g[8], down, g[7]
    )


def solution(mesh):
    rows = P(("fsdp", "dp"), None)
    flat = P("fsdp")
    return jax.shard_map(
        body,
        mesh=mesh,
        in_specs=(rows, rows, P(), P()) + (flat,) * 13,
        out_specs=(rows, rows) + (flat,) * 13,
        check_vma=False,
    )
```

```python
from functools import partial
import math

import jax
import jax.numpy as jnp
from jax import lax
from jax.experimental import pallas as pl
from jax.experimental.pallas import tpu as pltpu
from jax.sharding import PartitionSpec as P

HEAD_DIM = 96
HEAD_PAD = 128
LENS = (196, 256, 400)
SLOT = 400
ROW_PAD = 32
PAIR = 2
PAIR_DIM = PAIR * HEAD_DIM
PAIR_PAD = PAIR * HEAD_PAD
QUARTERS = 4
VEC = 128
VEC_PAIR = 64
SCALE = 1.0 / math.sqrt(HEAD_DIM)
EXP_SCALE = SCALE * math.log2(math.e)
MIB = 1024 * 1024
VMEM = {"attn_fwd": 12, "mlp": 24, "attn_bwd": 9, "layer_out": 8, "input_grad": 10, "finish": 10}
F32 = jnp.float32
BF16 = jnp.bfloat16


def dot_nn(a, b):
    return lax.dot_general(a, b, (((1,), (0,)), ((), ())), preferred_element_type=F32)


def dot_nt(a, b):
    return lax.dot_general(a, b, (((1,), (1,)), ((), ())), preferred_element_type=F32)


def dot_tn(a, b):
    return lax.dot_general(a, b, (((0,), (0,)), ((), ())), preferred_element_type=F32)


def pad_heads(values):
    rows, cols = values.shape
    gap = jnp.zeros((rows, HEAD_PAD - HEAD_DIM), values.dtype)
    parts = []
    for h in range(cols // HEAD_DIM):
        parts += [values[:, h * HEAD_DIM : (h + 1) * HEAD_DIM], gap]
    return jnp.concatenate(parts, axis=1)


def unpad_heads(values):
    rows, cols = values.shape
    return jnp.concatenate(
        [values[:, h * HEAD_PAD : h * HEAD_PAD + HEAD_DIM] for h in range(cols // HEAD_PAD)], axis=1
    )


def row_norm(x):
    center = x - jnp.mean(x, axis=-1, keepdims=True)
    inverse = lax.rsqrt(jnp.mean(center * center, axis=-1, keepdims=True) + 1e-6)
    return center * inverse, inverse


def row_norm_back(e, xhat, inverse):
    return inverse * (
        e - jnp.mean(e, axis=-1, keepdims=True) - xhat * jnp.mean(e * xhat, axis=-1, keepdims=True)
    )


def load_rows(ref, start, count):
    base = pl.multiple_of((start // 8) * 8, 8)
    window = ref[pl.ds(base, count + 8), :]
    moved = pltpu.roll(window, count + 4, 0)
    return jnp.where(start % 8 == 0, window, moved)[:count]


def store_rows(ref, start, length, values, cols):
    count = -(-length // 8) * 8
    base = pl.multiple_of((start // 8) * 8, 8)
    window = jnp.concatenate([values[:count], jnp.zeros((8, values.shape[1]), values.dtype)], axis=0)
    window = jnp.where(start % 8 == 0, window, pltpu.roll(window, 4, 0))
    row = lax.broadcasted_iota(jnp.int32, window.shape, 0) - start % 8
    held = ref[pl.ds(base, count + 8), cols]
    ref[pl.ds(base, count + 8), cols] = jnp.where((row >= 0) & (row < length), window, held)


def by_group(group, work):
    for g, length in enumerate(LENS):
        pl.when(group == g)(partial(work, length, -(-length // 16) * 16))


def gelu_pair(u):
    cdf = 0.5 + 0.5 * lax.erf(u * (1.0 / math.sqrt(2.0)))
    bell = jnp.exp2((u * u) * (-0.5 * math.log2(math.e)))
    return u * cdf, cdf + u * (bell * (1.0 / math.sqrt(2.0 * math.pi)))


def whole(array):
    at = (0,) * len(array.shape)
    return pl.BlockSpec(array.shape, lambda i, m: at, pipeline_mode=pl.Buffered(1))


def slot_block(cols):
    return pl.BlockSpec((1, SLOT, cols), lambda i, m: (i, 0, 0))


def call(kernel, name, grid, in_specs, out_specs, out_shape, scratch, args, waits=(), carry=(), far=(), onto=()):
    given, made, passed = len(in_specs) + 1, len(out_shape), len(waits) + len(carry) + len(onto)

    def ordered(*refs):
        kernel(*refs[:given], *refs[given + passed : given + passed + made], *refs[given + passed + made + len(carry) :])

    args = [
        pltpu.with_memory_space_constraint(t, pltpu.HBM) if at in far else t for at, t in enumerate(args)
    ]
    anywhere = pl.BlockSpec(memory_space=pl.ANY)
    outs = pl.pallas_call(
        ordered,
        grid_spec=pltpu.PrefetchScalarGridSpec(
            num_scalar_prefetch=1,
            grid=(grid,),
            in_specs=list(in_specs) + [anywhere] * passed,
            out_specs=list(out_specs) + [anywhere] * len(carry),
            scratch_shapes=scratch,
        ),
        out_shape=list(out_shape) + [jax.ShapeDtypeStruct(t.shape, t.dtype) for t in carry],
        input_output_aliases={given + len(waits) + n: made + n for n in range(len(carry))}
        | {given + len(waits) + len(carry) + n: n for n in range(len(onto))},
        compiler_params=pltpu.CompilerParams(vmem_limit_bytes=VMEM[name] * MIB),
        name=name,
    )(*args, *waits, *carry, *onto)
    return outs


def groups_at(meta):
    return (meta.shape[0] - 2) // 2


def rows_used(meta):
    return meta[meta.shape[0] - 2]


def device_of(meta):
    return meta[meta.shape[0] - 1]


def core_of(meta):
    return device_of(meta) % 2


def attn_fwd_kernel(meta, tok, wf0, wf1, attn0, attn1, qkv0, qkv1, xhat_out, lse0, lse1, wpad0, wpad1,
                    tok32, out32, bias):
    i = pl.program_id(0)
    rows, width = tok.shape
    cols = 3 * PAIR_PAD
    sides = ((wf0, qkv0, lse0, wpad0), (wf1, qkv1, lse1, wpad1))

    @pl.when(i == 0)
    def _():
        tok32[:rows] = tok[...].astype(F32)
        tok32[rows:] = jnp.zeros((tok32.shape[0] - rows, width), F32)
        vec = wf0[:, 3 * PAIR_DIM :].astype(F32).T
        bias[0:2, :width] = vec[0:2]
        for c in range(2):

            @pl.when(core_of(meta) == c)
            def _():
                for p in range(2):
                    at = (p ^ c) * PAIR_DIM
                    parts = [pad_heads(vec[r : r + 1, at : at + PAIR_DIM]) for r in (2, 3)]
                    bias[2 + p : 3 + p, :] = jnp.concatenate(
                        [parts[0], jnp.zeros((1, PAIR_PAD), F32), parts[1]], axis=1
                    )

        for wf, _, _, wpad in sides:
            wpad[...] = pad_heads(wf[:, : 3 * PAIR_DIM].astype(F32)).astype(BF16)

    start = meta[i]

    def work(length, padded):
        xhat, _ = row_norm(load_rows(tok32, start, padded))
        normed = (xhat * bias[0:1, :width] + bias[1:2, :width]).astype(BF16)
        xhat_out[0, :padded, :] = xhat.astype(BF16)
        for p, (_, qkv, lse, wpad) in enumerate(sides):
            qkv[0, :padded, :] = (dot_nn(normed, wpad[...]) + bias[2 + p : 3 + p, :]).astype(BF16)
        heads = [(p, h) for p in range(2) for h in range(PAIR)]
        scores = []
        for p, h in heads:
            qkv, at = sides[p][1], h * HEAD_PAD
            q = qkv[0, :padded, at : at + HEAD_PAD]
            k = qkv[0, :padded, PAIR_PAD + at : PAIR_PAD + at + HEAD_PAD]
            scores.append(dot_nt(k, q))
        probs = []
        for (p, h), s in zip(heads, scores):
            if length < padded:
                key = lax.broadcasted_iota(jnp.int32, s.shape, 0)
                s = jnp.where(key < length, s, -1e30)
            top = jnp.max(s, axis=0, keepdims=True)
            e = jnp.exp2((s - top) * EXP_SCALE)
            total = jnp.sum(e, axis=0, keepdims=True)
            probs.append((e * (1.0 / total)).astype(BF16))
            sides[p][2][0, h : h + 1, :padded] = top * EXP_SCALE + jnp.log2(total)
        outs = []
        for (p, h), prob in zip(heads, probs):
            at = 2 * PAIR_PAD + h * HEAD_PAD
            outs.append(dot_tn(prob, sides[p][1][0, :padded, at : at + HEAD_PAD]))
        store_rows(out32, start, length, jnp.concatenate(outs, axis=1), slice(None))

    by_group(meta[groups_at(meta) + i], work)

    @pl.when(i == pl.num_programs(0) - 1)
    def _():
        row = lax.broadcasted_iota(jnp.int32, (rows, 1), 0)
        mixed = jnp.where(row < rows_used(meta), out32[:rows], 0.0).astype(BF16)
        attn0[...] = mixed[:, :PAIR_PAD]
        attn1[...] = mixed[:, PAIR_PAD:]


def attn_fwd(meta, tokens, wf, waits, carry):
    rows, width = tokens.shape
    slots = groups_at(meta)
    cols = 3 * PAIR_PAD
    out_shape = [jax.ShapeDtypeStruct((rows, PAIR_PAD), BF16)] * 2
    out_shape += [jax.ShapeDtypeStruct((slots, SLOT, cols), BF16)] * 2
    out_shape += [jax.ShapeDtypeStruct((slots, SLOT, width), BF16)]
    out_shape += [jax.ShapeDtypeStruct((slots, 8, 512), F32)] * 2
    out_shape += [jax.ShapeDtypeStruct((width, cols), BF16)] * 2
    stats = pl.BlockSpec((1, 8, 512), lambda i, m: (i, 0, 0))
    out_specs = [whole(out_shape[0])] * 2 + [slot_block(cols)] * 2 + [slot_block(width)]
    out_specs += [stats] * 2 + [whole(out_shape[-1])] * 2
    scratch = [
        pltpu.VMEM((rows + ROW_PAD, width), F32),
        pltpu.VMEM((rows + ROW_PAD, 2 * PAIR_PAD), F32),
        pltpu.VMEM((8, cols), F32),
    ]
    in_specs = [whole(tokens), whole(wf[0]), whole(wf[1])]
    args = (meta, tokens, *wf)
    return call(attn_fwd_kernel, "attn_fwd", slots, in_specs, out_specs, out_shape, scratch, args, waits, carry)


def put_blocks(to, value, col, shards, parity=None):
    rows, cols = value.shape
    size = rows // shards
    half = rows // 2
    if size % 16:
        if parity is not None:
            value = value[parity * half : (parity + 1) * half]
        to[:, col : col + cols] = value
        return
    for n, place in enumerate(turned(shards)):
        at = place * size
        if parity is not None:
            if n % 2 != parity:
                continue
            at -= parity * half
        to[at : at + size, col : col + cols] = value[n * size : (n + 1) * size]


def mlp_kernel(meta, tok, cot, attn0, attn1, w0, w1, b0, b1, x1o, acto, dx1, da0, da1,
               keep_a, send_a, keep_b, send_b, wproj, rowvec, gd, gu, gp, gsum, *, shards):
    i = pl.program_id(0)
    rows, width = tok.shape
    parts = (w0, w1)
    lower = (b0, b1)

    def in_order(first, second, use):
        for c in range(2):
            pl.when(core_of(meta) == c)(partial(use, c, *((first, second) if c == 0 else (second, first))))

    @pl.when(i == 0)
    def _():
        def use(c, low, high):
            flat = [ref[x][:, width : width + VEC] for ref in (low, high) for x in range(2)]
            proj = jnp.concatenate(flat[: width // VEC], axis=1)
            wproj[...] = jnp.zeros(wproj.shape, BF16)
            for h in range(2 * PAIR):
                at = (h ^ (PAIR * c)) * HEAD_PAD
                wproj[at : at + HEAD_DIM] = proj[h * HEAD_DIM : (h + 1) * HEAD_DIM]
            vec = flat[-1].astype(F32).T
            for r in range(4):
                rowvec[r : r + 1, :width] = vec[r : r + 1]
                at = (r ^ (2 * c)) * width
                rowvec[4:5, at : at + width] = vec[4 + r : 5 + r]

        in_order(w0, w1, use)
        gd[...] = jnp.zeros(gd.shape, F32)
        gu[...] = jnp.zeros(gu.shape, F32)
        gp[...] = jnp.zeros(gp.shape, F32)
        gsum[...] = jnp.zeros(gsum.shape, F32)

    proj_bias, gain, shift, down_bias = [rowvec[r : r + 1, :width] for r in range(4)]
    row = lax.broadcasted_iota(jnp.int32, (rows, 1), 0) + i * rows
    valid = (row < rows_used(meta)).astype(F32)
    dy = cot[...].astype(F32) * valid
    dyb = dy.astype(BF16)
    chunk = 2 * width
    ups = [jnp.concatenate([parts[c][0][:, :width], parts[c][1][:, :width]], axis=1) for c in range(2)]
    downs = [jnp.concatenate([lower[c][x] for x in range(2)], axis=0) for c in range(2)]
    dacts = [dot_nt(dyb, downs[c]) for c in range(2)]
    mixed0, mixed1 = attn0[...], attn1[...]
    x1 = tok[...].astype(F32) + dot_nn(mixed0, wproj[:PAIR_PAD]) + dot_nn(mixed1, wproj[PAIR_PAD:])
    x1 = x1 + proj_bias
    x1o[...] = (x1 + down_bias) * valid
    xhat, inverse = row_norm(x1)
    normed = (xhat * gain + shift).astype(BF16)
    dn = jnp.zeros((rows, width), F32)
    kept = []
    for c in range(2):
        at = c * chunk
        pre = dot_nn(normed, ups[c]) + rowvec[4:5, at : at + chunk]
        act, slope = gelu_pair(pre)
        actb = act.astype(BF16)
        acto[:, at : at + chunk] = actb
        dpre = dacts[c] * slope
        dpreb = dpre.astype(BF16)
        gsum[4:5, at : at + chunk] += jnp.sum(dpre, axis=0, keepdims=True)
        dn = dn + dot_nt(dpreb, ups[c])
        kept.append(dpreb)
    for c in range(2):
        at = c * chunk
        gd[:, at : at + chunk] += dot_tn(dyb, acto[:, at : at + chunk])
        gu[:, at : at + chunk] += dot_tn(normed, kept[c])
    dx = dy + row_norm_back(dn * gain, xhat, inverse)
    dx1[...] = dx
    dxb = dx.astype(BF16)
    gp[:, :PAIR_PAD] += dot_tn(dxb, mixed0)
    gp[:, PAIR_PAD:] += dot_tn(dxb, mixed1)
    da0[...] = dot_nt(dxb, wproj[:PAIR_PAD]).astype(BF16)
    da1[...] = dot_nt(dxb, wproj[PAIR_PAD:]).astype(BF16)
    gsum[0:1, :width] += jnp.sum(dx, axis=0, keepdims=True)
    gsum[1:2, :width] += jnp.sum(dn * xhat, axis=0, keepdims=True)
    gsum[2:3, :width] += jnp.sum(dn, axis=0, keepdims=True)
    gsum[3:4, :width] += jnp.sum(dy, axis=0, keepdims=True)

    @pl.when(i == pl.num_programs(0) - 1)
    def _():
        for half, (to_a, to_b) in enumerate(((keep_a, keep_b), (send_a, send_b))):
            for x in range(2):
                at = (2 * half + x) * width
                put_blocks(to_a.at[x], gu[:, at : at + width].astype(BF16), 0, shards)
                part = gd[:, at : at + width].T.astype(BF16)
                for y in range(2):
                    put_blocks(to_b.at[y, x], part, 0, shards, y)

        def use(c, low, high):
            rows_of = [gsum[r : r + 1, :width] for r in range(4)]
            for r in range(4):
                at = (r ^ (2 * c)) * width
                rows_of.append(gsum[4:5, at : at + width])
            vec = jnp.concatenate(rows_of + [jnp.zeros((VEC - 8, width), F32)], axis=0).T
            grad = unpad_heads(gp[...]).T
            first, second = grad[:PAIR_DIM], grad[PAIR_DIM:]
            proj = jnp.concatenate([second, first] if c else [first, second], axis=0)
            flat = jnp.concatenate([proj, vec], axis=1).astype(BF16)
            for k in range(QUARTERS):
                to = (low, high)[k // 2].at[k % 2]
                put_blocks(to, flat[:, k * VEC : (k + 1) * VEC], width, shards)

        in_order(keep_a, send_a, use)


def mlp(meta, tokens, cotangent, attn, w, shards, block=512):
    rows, width = tokens.shape
    hidden = QUARTERS * width
    by_row = lambda cols: pl.BlockSpec((block, cols), lambda i, m: (i, 0))
    out_shape = [
        jax.ShapeDtypeStruct((rows, width), F32),
        jax.ShapeDtypeStruct((rows, hidden), BF16),
        jax.ShapeDtypeStruct((rows, width), F32),
        jax.ShapeDtypeStruct((rows, PAIR_PAD), BF16),
        jax.ShapeDtypeStruct((rows, PAIR_PAD), BF16),
    ]
    out_shape += [jax.ShapeDtypeStruct((2, width, width + VEC), BF16)] * 2
    out_shape += [jax.ShapeDtypeStruct((2, 2, width // 2, width), BF16)] * 2
    out_specs = [by_row(s.shape[1]) for s in out_shape[:5]] + [whole(s) for s in out_shape[5:]]
    in_specs = [by_row(width)] * 2 + [by_row(PAIR_PAD)] * 2 + [whole(t) for t in w]
    scratch = [
        pltpu.VMEM((2 * PAIR_PAD, width), BF16),
        pltpu.VMEM((8, hidden), F32),
        pltpu.VMEM((width, hidden), F32),
        pltpu.VMEM((width, hidden), F32),
        pltpu.VMEM((width, 2 * PAIR_PAD), F32),
        pltpu.VMEM((8, hidden), F32),
    ]
    args = (meta, tokens, cotangent, *attn, *w)
    kernel = partial(mlp_kernel, shards=shards)
    return call(kernel, "mlp", rows // block, in_specs, out_specs, out_shape, scratch, args)


def layer_out_kernel(meta, x1, act, b0, b1, out):
    rows, width = x1.shape
    row = lax.broadcasted_iota(jnp.int32, (rows, 1), 0) + pl.program_id(0) * rows
    valid = (row < rows_used(meta)).astype(F32)
    y = x1[...]
    for c, ref in enumerate((b0, b1)):
        down = jnp.concatenate([ref[x] for x in range(2)], axis=0)
        y = y + dot_nn(act[:, 2 * c * width : 2 * (c + 1) * width], down) * valid
    out[...] = y.astype(BF16)


def layer_output(meta, x1, act, w, waits, carry, block=512):
    rows, width = x1.shape
    by_row = lambda cols: pl.BlockSpec((block, cols), lambda i, m: (i, 0))
    return call(
        layer_out_kernel,
        "layer_out",
        rows // block,
        [by_row(width), by_row(act.shape[1]), whole(w[0]), whole(w[1])],
        [by_row(width)],
        [jax.ShapeDtypeStruct((rows, width), BF16)],
        [],
        (meta, x1, act, *w),
        waits,
        carry,
    )


def attn_bwd_kernel(meta, qkv, xhat, lse, dattn, wpad, wf, *rest, own, shards, half):
    if half:
        gw_in, gsum_in, dqkv, grads, da32, gw, gsum = rest
    else:
        dqkv, gw, gsum, da32 = rest
    i = pl.program_id(0)
    slot = i + half * pl.num_programs(0)
    rows = dattn.shape[0]
    width = wf.shape[0]

    @pl.when(i == 0)
    def _():
        da32[:rows] = dattn[...].astype(F32)
        da32[rows:] = jnp.zeros((da32.shape[0] - rows, PAIR_PAD), F32)
        gw[...] = gw_in[...] if half else jnp.zeros(gw.shape, F32)
        gsum[...] = gsum_in[...] if half else jnp.zeros(gsum.shape, F32)

    start = meta[slot]

    def work(length, padded):
        da = load_rows(da32, start, padded)
        if length < padded:
            keep = lax.broadcasted_iota(jnp.int32, (padded, 1), 0) < length
            da = jnp.where(keep, da, 0.0)
        da = da.astype(BF16)
        def cut(ref, part, h):
            at = part * PAIR_PAD + h * HEAD_PAD
            return ref[0, :padded, at : at + HEAD_PAD]

        heads = range(PAIR)
        das = [da[:, h * HEAD_PAD : (h + 1) * HEAD_PAD] for h in heads]
        scores = [dot_nt(cut(qkv, 1, h), cut(qkv, 0, h)) for h in heads]
        dps = [dot_nt(cut(qkv, 2, h), das[h]) for h in heads]
        ps, dss = [], []
        for h in heads:
            p = jnp.exp2(scores[h] * EXP_SCALE - lse[0, h : h + 1, :padded])
            if length < padded:
                key = lax.broadcasted_iota(jnp.int32, p.shape, 0)
                p = jnp.where(key < length, p, 0.0)
            mean = jnp.sum(p * dps[h], axis=0, keepdims=True)
            dss.append((p * (dps[h] - mean)).astype(BF16))
            ps.append(p.astype(BF16))
        parts = [[dot_tn(dss[h], cut(qkv, 1, h)) * SCALE for h in heads]]
        parts += [[dot_nn(dss[h], cut(qkv, 0, h)) * SCALE for h in heads]]
        parts += [[dot_nn(ps[h], das[h]) for h in heads]]
        d = []
        for part in range(3):
            value = jnp.concatenate(parts[part], axis=1)
            at = part * PAIR_PAD
            if part != 1:
                gsum[0:1, at : at + PAIR_PAD] += jnp.sum(value, axis=0, keepdims=True)
            d.append(value.astype(BF16))
        d = jnp.concatenate(d, axis=1)
        dqkv[0, :padded, :] = d
        gw[...] += dot_tn(xhat[0, :padded, :], d)
        gsum[1:2, :] += jnp.sum(d.astype(F32), axis=0, keepdims=True)

    by_group(meta[groups_at(meta) + slot], work)
    if not half:
        return

    @pl.when(i == pl.num_programs(0) - 1)
    def _():
        w = wpad[...].astype(F32)
        raw = gw[...]
        col = gsum[1:2, :]
        gain_term = jnp.sum(raw * w, axis=1, keepdims=True)
        bias_term = jnp.sum(col * w, axis=1, keepdims=True)
        vec = wf[:, 3 * PAIR_DIM :].astype(F32)
        main = unpad_heads(raw * vec[:, 0:1] + vec[:, 1:2] * col).astype(BF16)
        put_blocks(grads, main, 0, shards)
        q_sum = unpad_heads(gsum[0:1, :PAIR_PAD])
        v_sum = unpad_heads(gsum[0:1, 2 * PAIR_PAD :])
        gap = jnp.zeros((1, width - PAIR_DIM), F32)
        for c in range(2):

            @pl.when(core_of(meta) == (c if own else 1 - c))
            def _():
                rows_of = [jnp.concatenate([gap, t] if c else [t, gap], axis=1) for t in (q_sum, v_sum)]
                rows_of = [jnp.zeros((2, width), F32)] + rows_of + [jnp.zeros((VEC - 4, width), F32)]
                sums = jnp.concatenate(rows_of, axis=0).T
                lane = lax.broadcasted_iota(jnp.int32, sums.shape, 1)
                tail = jnp.where(lane == 0, gain_term, jnp.where(lane == 1, bias_term, sums))
                put_blocks(grads, tail[:, :VEC_PAIR].astype(BF16), 3 * PAIR_DIM, shards)


def attn_bwd(meta, qkv, xhat, lse, dattn, wpad, wf, own, shards, held, waits, carry):
    rows = dattn.shape[0]
    width = wf.shape[0]
    cols = 3 * PAIR_PAD
    half = int(bool(held))
    count = groups_at(meta) // 2
    at = half * count
    slot = lambda c: pl.BlockSpec((1, SLOT, c), lambda i, m: (i + at, 0, 0))
    sums = [jax.ShapeDtypeStruct((width, cols), F32), jax.ShapeDtypeStruct((8, cols), F32)]
    dqkv = jax.ShapeDtypeStruct(qkv.shape, BF16)
    in_specs = [slot(cols), slot(width), pl.BlockSpec((1, 8, 512), lambda i, m: (i + at, 0, 0))]
    in_specs += [whole(dattn), whole(wpad), whole(wf)]
    args = (meta, qkv, xhat, lse, dattn, wpad, wf)
    scratch = [pltpu.VMEM((rows + ROW_PAD, PAIR_PAD), F32)]
    if half:
        in_specs += [whole(t) for t in sums]
        args += tuple(held[1:])
        out_shape = [dqkv, jax.ShapeDtypeStruct(wf.shape, BF16)]
        scratch += [pltpu.VMEM(t.shape, F32) for t in sums]
    else:
        out_shape = [dqkv, *sums]
    out_specs = [slot(cols)] + [whole(t) for t in out_shape[1:]]
    kernel = partial(attn_bwd_kernel, own=own, shards=shards, half=half)
    onto = held[:1] if half else ()
    return call(
        kernel, "attn_bwd", count, in_specs, out_specs, out_shape, scratch, args, waits, carry, (), onto
    )


def input_grad_kernel(meta, tok, d0, d1, w0, w1, wf, dx1, out, tok32, bias):
    i = pl.program_id(0)
    rows, width = tok.shape

    @pl.when(i == 0)
    def _():
        tok32[:rows] = tok[...].astype(F32)
        tok32[rows:] = jnp.zeros((tok32.shape[0] - rows, width), F32)
        bias[...] = wf[:, 3 * PAIR_DIM :].astype(F32).T[0:8]

    start = meta[i]

    def work(length, padded):
        dn = dot_nt(d0[0, :padded, :], w0[...]) + dot_nt(d1[0, :padded, :], w1[...])
        xhat, inverse = row_norm(load_rows(tok32, start, padded))
        dx = row_norm_back(dn * bias[0:1, :], xhat, inverse)
        store_rows(tok32, start, length, dx, slice(None))

    by_group(meta[groups_at(meta) + i], work)

    @pl.when(i == pl.num_programs(0) - 1)
    def _():
        row = lax.broadcasted_iota(jnp.int32, (rows, 1), 0)
        total = dx1[...] + tok32[:rows]
        out[...] = jnp.where(row < rows_used(meta), total, 0.0).astype(BF16)


def input_grad(meta, tokens, d, w, wf, dx1, waits, carry):
    rows, width = tokens.shape
    slot = slot_block(d[0].shape[2])
    in_specs = [whole(tokens), slot, slot] + [whole(t) for t in (*w, wf, dx1)]
    scratch = [pltpu.VMEM((rows + ROW_PAD, width), F32), pltpu.VMEM((8, width), F32)]
    out_shape = [jax.ShapeDtypeStruct((rows, width), BF16)]
    args = (meta, tokens, *d, *w, wf, dx1)
    grid, out_specs = groups_at(meta), [whole(tokens)]
    return call(
        input_grad_kernel, "input_grad", grid, in_specs, out_specs, out_shape, scratch, args, waits, carry
    )


def final_parts(core, own, got, own_q, got_q):
    size = own.shape[0]
    width = own_q.shape[-1] - VEC
    width = width // 2
    cut = 3 * PAIR_DIM + VEC_PAIR
    low, high = (got, own) if core else (own, got)
    qkv = [t[:, part * PAIR_DIM : (part + 1) * PAIR_DIM] for part in range(3) for t in (low, high)]
    quarters = [t[x] for t in ((got_q, own_q) if core else (own_q, got_q)) for x in range(2)]
    extra_at, down_at = width, width + VEC
    extra = [q[:, extra_at:down_at] for q in quarters]
    up = [q[:, n : n + size] for n in range(0, width, size) for q in quarters]
    down = jnp.concatenate([q[:, down_at:] for q in quarters], axis=0)
    ends = low[:, 3 * PAIR_DIM : cut] + high[:, 3 * PAIR_DIM : cut]
    columns = jnp.concatenate([ends[:, :4], extra[-1][:, : 4 + QUARTERS]], axis=1)
    cat = lambda parts: jnp.concatenate(parts, axis=1)
    return cat(qkv), cat(extra[: width // VEC]), cat(up), down, columns


def finish_kernel(meta, own, got, own_q, got_q, *outs):
    size = own.shape[0]

    def use(core):
        parts = [t[...].astype(F32) for t in (own, got, own_q, got_q)]
        *mats, columns = final_parts(core, *parts)
        for mat, out in zip(mats, outs):
            tiles = mat.shape[1] // 128
            for t in range(tiles):
                out[pl.ds(t, mat.shape[0], stride=tiles), :] = mat[:, t * 128 : (t + 1) * 128]
        count = columns.shape[1]
        square = jnp.concatenate([columns, jnp.zeros((size, 128 - count), F32)], axis=1)
        square = jnp.concatenate([square, jnp.zeros((128 - size, 128), F32)], axis=0)
        outs[4][...] = square.T[:16]

    for c in range(2):
        pl.when(core_of(meta) == c)(partial(use, c))


def finish(meta, *parts):
    own, _, own_q, _ = parts
    size = own.shape[0]
    width = (own_q.shape[-1] - VEC) // 2
    if size % 16:
        core = core_of(meta) == 1
        own, got, own_q, got_q = (t.astype(F32) for t in parts)
        pick_two = lambda a, b: (jnp.where(core, b, a), jnp.where(core, a, b))
        outs = final_parts(0, *pick_two(own, got), *pick_two(own_q, got_q))
        return [p.reshape(-1) for p in outs[:4]], outs[4].T
    sizes = [size * 3 * width, size * width, size * QUARTERS * width, size * QUARTERS * width]
    out_shape = [jax.ShapeDtypeStruct((n // 128, 128), F32) for n in sizes + [16 * 128]]
    out_specs = [whole(t) for t in out_shape]
    in_specs = [whole(t) for t in parts]
    outs = call(finish_kernel, "finish", 1, in_specs, out_specs, out_shape, [], (meta, *parts))
    return [t.reshape(-1) for t in outs[:4]], outs[4]


def turned(shards):
    count = shards.bit_length() - 1
    return [sum(((n >> b) & 1) << (count - 1 - b) for b in range(count)) for n in range(shards)]


def image_table(size_group, assignment, device, slots):
    owned = assignment == device
    rank = jnp.cumsum(owned.astype(jnp.int32)) - 1
    slot = jnp.arange(slots, dtype=jnp.int32)
    here = owned[None, :] & (rank[None, :] == slot[:, None])
    groups = jnp.sum(jnp.where(here, size_group[None, :], 0), axis=1)
    lengths = jnp.where(groups == 0, LENS[0], jnp.where(groups == 1, LENS[1], LENS[2]))
    ends = jnp.sum(jnp.where(slot[None, :] <= slot[:, None], lengths[None, :], 0), axis=1)
    return jnp.concatenate([ends - lengths, groups, ends[-1:], device[None]]).astype(jnp.int32)


def swap(value, axis, bit):
    size = lax.axis_size(axis)
    return lax.ppermute(value, axis, [(i, i ^ bit) for i in range(size)])


def sides_of(bits):
    table = {}
    for axis, those in bits.items():
        for bit in those:
            mine = (lax.axis_index(axis) & bit) // bit
            table[axis, bit] = (mine.astype(jnp.uint32), (1 - mine).astype(jnp.uint32), mine == 1)
    return table


def pick(sides, value, axis, bit, dim):
    mine, theirs, _ = sides[axis, bit]
    keep = lax.dynamic_index_in_dim(value, mine, dim, keepdims=False)
    send = lax.dynamic_index_in_dim(value, theirs, dim, keepdims=False)
    return keep, send


def join(upper, own, other, dim):
    return jnp.stack([jnp.where(upper, other, own), jnp.where(upper, own, other)], axis=dim)


def added(keep, got):
    return (keep.astype(F32) + got.astype(F32)).astype(BF16)


def after(value, *others):
    return lax.optimization_barrier((value, *others))[0]


class Gather:
    def __init__(self, sides, part, keys):
        self.sides, self.part, self.keys, self.have = sides, part, keys, []

    def grow(self, axis, bit, *others, upper=None):
        if others:
            self.part = after(self.part, *others)
        upper = self.sides[axis, bit][2] if upper is None else upper
        dim = sum(self.keys.index(k) < self.keys.index((axis, bit)) for k in self.have)
        self.part = join(upper, self.part, swap(self.part, axis, bit), dim)
        self.have.append((axis, bit))
        return self


def body(
    tokens,
    cotangent,
    size_group,
    assignment,
    ln1_gain,
    ln1_bias,
    w_qkv,
    q_bias,
    v_bias,
    w_proj,
    proj_bias,
    ln2_gain,
    ln2_bias,
    w_up,
    up_bias,
    w_down,
    down_bias,
):
    rows, width = tokens.shape
    shards = lax.axis_size("fsdp")
    size = width // shards
    devices = shards * lax.axis_size("dp")
    device = lax.axis_index("fsdp") * lax.axis_size("dp") + lax.axis_index("dp")
    bits = [1 << b for b in range(shards.bit_length() - 1)]
    far, near, y = bits[2:], bits[1:2], bits[0]
    tail_keys = [("fsdp", b) for b in reversed(bits)]
    sides = sides_of({"dp": (1, 2), "fsdp": bits})
    core, column = sides["dp", 1][0], sides["dp", 2][0]

    vectors = [ln1_gain, ln1_bias, q_bias, v_bias, proj_bias, ln2_gain, ln2_bias, down_bias]
    vectors += [up_bias[k * size : (k + 1) * size] for k in range(QUARTERS)]
    vectors = jnp.stack(vectors).T
    pair = w_qkv.reshape(size, 3, 2, PAIR_DIM)
    pair = lax.dynamic_index_in_dim(pair, core, 2, keepdims=False).reshape(size, 3 * PAIR_DIM)
    pair = jnp.concatenate([pair, vectors[:, :4], jnp.zeros((size, VEC_PAIR - 4), BF16)], axis=1)
    f = Gather(sides, pair, tail_keys)
    w_up, w_down, w_proj, _ = lax.optimization_barrier((w_up, w_down, w_proj, pair))
    quarter = 2 * core + column
    extra = [w_proj.reshape(size, width), vectors[:, 4:], jnp.zeros((size, VEC - 4 - QUARTERS), BF16)]
    extra = lax.dynamic_slice_in_dim(jnp.concatenate(extra, axis=1), quarter * VEC, VEC, 1)
    up = lax.dynamic_index_in_dim(w_up.reshape(size, shards, QUARTERS, size), quarter, 2, False)
    part_a = jnp.concatenate([up.reshape(size, width), extra], axis=1)
    part_b = lax.dynamic_index_in_dim(w_down.reshape(QUARTERS, size, width), quarter, 0, False)
    ab = Gather(sides, jnp.concatenate([part_a, part_b], axis=1), tail_keys)

    for bit in far:
        f.grow("fsdp", bit)
    for bit in far:
        ab.grow("fsdp", bit)
    for bit in near:
        f.grow("fsdp", bit)
    for bit in near:
        ab.grow("fsdp", bit)
    size_group, assignment, _ = lax.optimization_barrier((size_group, assignment, f.part))
    table = image_table(size_group, assignment, device, size_group.shape[0] // devices)
    f.grow("fsdp", y)
    own = f.part.reshape(width, -1)
    cut = width + VEC
    keys = [("dp", 2)] + tail_keys
    a, b = Gather(sides, ab.part[..., :cut], keys), Gather(sides, ab.part[..., cut:], keys)
    a.have, b.have = list(ab.have), list(ab.have)
    a.grow("dp", 2)
    b.grow("fsdp", y)
    wf = (own, swap(own, "dp", 1))

    upper = jnp.stack([sides["fsdp", y][2], sides["dp", 2][2]])
    upper = jnp.broadcast_to(upper[:, None, None], (2, 8, cut)).astype(jnp.int32)
    table, sides, upper = lax.optimization_barrier((table, sides, upper))
    attn0, attn1, qkv0, qkv1, xhat, lse0, lse1, wpad0, wpad1, upper = attn_fwd(
        table, tokens, wf, (a.part, b.part), (upper,)
    )
    a.grow("fsdp", y, upper=upper[0, 0] != 0)
    b.grow("dp", 2, upper=upper[1, 0, :width] != 0)
    wa, wb = a.part.reshape(2, width, cut), b.part.reshape(2, width, width)
    w = (wa, swap(wa, "dp", 1), wb, swap(wb, "dp", 1))
    x1, act, dx1, dattn0, dattn1, keep_a, send_a, keep_b, send_b = mlp(
        table, tokens, cotangent, (attn0, attn1), w, shards
    )

    def by_bits(value, lead):
        if size % 16:
            value = value.reshape(value.shape[:lead] + (2,) * len(bits) + (size, value.shape[-1]))
            order = [lead + b for b in reversed(range(len(bits)))]
            return value.transpose(*range(lead), *order, *range(lead + len(bits), value.ndim))
        return value.reshape(value.shape[:lead] + (2,) * len(bits) + (size, value.shape[-1]))

    def halves_of_b(value):
        if size % 16:
            value = value.swapaxes(0, 1).reshape(2, width, width)
            return by_bits(value, 1).swapaxes(0, 1)
        return value.reshape((2, 2) + (2,) * (len(bits) - 1) + (size, width))

    got_a, got_b = swap(send_a, "dp", 1), swap(send_b, "dp", 1)
    back0 = (table, qkv0, xhat, lse0, dattn0, wpad0, wf[0], True, shards)
    back1 = (table, qkv1, xhat, lse1, dattn1, wpad1, wf[1], False, shards)
    *held, keep_a, keep_b = attn_bwd(*back1, (), (send_a, send_b), (keep_a, keep_b))
    keep_a, send_a = pick(sides, by_bits(added(keep_a, got_a), 1), "dp", 2, 0)
    keep_b, send_b = pick(sides, halves_of_b(added(keep_b, got_b)), "fsdp", y, 0)
    got_a, got_b = swap(send_a, "dp", 2), swap(send_b, "fsdp", y)
    d1, send_g = attn_bwd(*back1, held, (send_a, send_b), ())
    got_g = swap(send_g, "dp", 1)
    *held, keep_a, keep_b = attn_bwd(*back0, (), (send_g,), (keep_a, keep_b))
    keep_a, send_a = pick(sides, added(keep_a, got_a), "fsdp", y, 0)
    keep_b, send_b = pick(sides, added(keep_b, got_b), "dp", 2, 0)
    got_a, got_b = swap(send_a, "fsdp", y), swap(send_b, "dp", 2)
    d0, keep_g, keep_a, keep_b = attn_bwd(*back0, held, (send_a, send_b), (keep_a, keep_b))
    part_g = by_bits(added(keep_g, got_g), 0)
    part = jnp.concatenate([added(keep_a, got_a), added(keep_b, got_b)], axis=-1)

    steps = [[("fsdp", b) for b in bits] + [("dp", 2), ("dp", 1)]]
    steps += [[("fsdp", b) for b in bits[1:]] + [("dp", 2), ("dp", 1)]]
    parts = [part_g, part]
    done = [None, None]
    for count in range(len(steps[0])):
        sent, kept = [None, None], [None, None]
        for n in range(2):
            if count < len(steps[n]):
                kept[n] = sent[n] = parts[n]
                if steps[n][count][0] == "fsdp":
                    kept[n], sent[n] = pick(sides, parts[n], *steps[n][count], 0)
        got = [None if sent[n] is None else swap(sent[n], *steps[n][count]) for n in range(2)]
        if count == 0:
            grads_of = (table, tokens, (d0, d1), (wpad0, wpad1), wf[0], dx1)
            grad_input, *kept = input_grad(*grads_of, sent, kept)
        elif count == 1:
            layer_out, *kept = layer_output(table, x1, act, w[2:], sent, kept)
        for n in range(2):
            if sent[n] is None:
                continue
            axis, bit = steps[n][count]
            if axis == "fsdp" or (n == 0 and bit == 2):
                parts[n] = added(kept[n], got[n])
            elif bit == 2:
                parts[n] = join(sides["dp", 2][2], kept[n], got[n], 0)
            else:
                done[n] = (kept[n], got[n])
    flat, vectors = finish(table, *done[0], *done[1])
    g = [vectors[r, :size] for r in range(8)] + [vectors[8 : 8 + QUARTERS, :size].reshape(-1)]
    qkv, proj, up, down = flat
    return (
        layer_out, grad_input, g[0], g[1], qkv, g[2], g[3], proj, g[4], g[5], g[6], up, g[8], down, g[7]
    )


def solution(mesh):
    rows = P(("fsdp", "dp"), None)
    flat = P("fsdp")
    return jax.shard_map(
        body,
        mesh=mesh,
        in_specs=(rows, rows, P(), P()) + (flat,) * 13,
        out_specs=(rows, rows) + (flat,) * 13,
        check_vma=False,
    )
```

```python
from functools import partial
import math

import jax
import jax.numpy as jnp
from jax import lax
from jax.experimental import pallas as pl
from jax.experimental.pallas import tpu as pltpu
from jax.sharding import PartitionSpec as P

HEAD_DIM = 96
HEAD_PAD = 128
LENS = (196, 256, 400)
SLOT = 400
ROW_PAD = 32
PAIR = 2
PAIR_DIM = PAIR * HEAD_DIM
PAIR_PAD = PAIR * HEAD_PAD
QUARTERS = 4
VEC = 128
VEC_PAIR = 64
SCALE = 1.0 / math.sqrt(HEAD_DIM)
EXP_SCALE = SCALE * math.log2(math.e)
MIB = 1024 * 1024
VMEM = {"attn_fwd": 12, "mlp": 24, "attn_bwd": 8, "layer_out": 8, "input_grad": 10, "finish": 10}
F32 = jnp.float32
BF16 = jnp.bfloat16


def dot_nn(a, b):
    return lax.dot_general(a, b, (((1,), (0,)), ((), ())), preferred_element_type=F32)


def dot_nt(a, b):
    return lax.dot_general(a, b, (((1,), (1,)), ((), ())), preferred_element_type=F32)


def dot_tn(a, b):
    return lax.dot_general(a, b, (((0,), (0,)), ((), ())), preferred_element_type=F32)


def pad_heads(values):
    rows, cols = values.shape
    gap = jnp.zeros((rows, HEAD_PAD - HEAD_DIM), values.dtype)
    parts = []
    for h in range(cols // HEAD_DIM):
        parts += [values[:, h * HEAD_DIM : (h + 1) * HEAD_DIM], gap]
    return jnp.concatenate(parts, axis=1)


def unpad_heads(values):
    rows, cols = values.shape
    return jnp.concatenate(
        [values[:, h * HEAD_PAD : h * HEAD_PAD + HEAD_DIM] for h in range(cols // HEAD_PAD)], axis=1
    )


def row_norm(x):
    center = x - jnp.mean(x, axis=-1, keepdims=True)
    inverse = lax.rsqrt(jnp.mean(center * center, axis=-1, keepdims=True) + 1e-6)
    return center * inverse, inverse


def row_norm_back(e, xhat, inverse):
    return inverse * (
        e - jnp.mean(e, axis=-1, keepdims=True) - xhat * jnp.mean(e * xhat, axis=-1, keepdims=True)
    )


def load_rows(ref, start, count):
    base = pl.multiple_of((start // 8) * 8, 8)
    window = ref[pl.ds(base, count + 8), :]
    moved = pltpu.roll(window, count + 4, 0)
    return jnp.where(start % 8 == 0, window, moved)[:count]


def store_rows(ref, start, length, values, cols):
    count = -(-length // 8) * 8
    base = pl.multiple_of((start // 8) * 8, 8)
    window = jnp.concatenate([values[:count], jnp.zeros((8, values.shape[1]), values.dtype)], axis=0)
    window = jnp.where(start % 8 == 0, window, pltpu.roll(window, 4, 0))
    row = lax.broadcasted_iota(jnp.int32, window.shape, 0) - start % 8
    held = ref[pl.ds(base, count + 8), cols]
    ref[pl.ds(base, count + 8), cols] = jnp.where((row >= 0) & (row < length), window, held)


def by_group(group, work):
    for g, length in enumerate(LENS):
        pl.when(group == g)(partial(work, length, -(-length // 16) * 16))


def gelu_pair(u):
    cdf = 0.5 + 0.5 * lax.erf(u * (1.0 / math.sqrt(2.0)))
    bell = jnp.exp2((u * u) * (-0.5 * math.log2(math.e)))
    return u * cdf, cdf + u * (bell * (1.0 / math.sqrt(2.0 * math.pi)))


def whole(array):
    at = (0,) * len(array.shape)
    return pl.BlockSpec(array.shape, lambda i, m: at, pipeline_mode=pl.Buffered(1))


def slot_block(cols):
    return pl.BlockSpec((1, SLOT, cols), lambda i, m: (i, 0, 0))


def call(kernel, name, grid, in_specs, out_specs, out_shape, scratch, args, waits=(), carry=(), far=()):
    given, made, passed = len(in_specs) + 1, len(out_shape), len(waits) + len(carry)

    def ordered(*refs):
        kernel(*refs[:given], *refs[given + passed : given + passed + made], *refs[given + passed + made + len(carry) :])

    args = [
        pltpu.with_memory_space_constraint(t, pltpu.HBM) if at in far else t for at, t in enumerate(args)
    ]
    anywhere = pl.BlockSpec(memory_space=pl.ANY)
    outs = pl.pallas_call(
        ordered,
        grid_spec=pltpu.PrefetchScalarGridSpec(
            num_scalar_prefetch=1,
            grid=(grid,),
            in_specs=list(in_specs) + [anywhere] * passed,
            out_specs=list(out_specs) + [anywhere] * len(carry),
            scratch_shapes=scratch,
        ),
        out_shape=list(out_shape) + [jax.ShapeDtypeStruct(t.shape, t.dtype) for t in carry],
        input_output_aliases={given + len(waits) + n: made + n for n in range(len(carry))},
        compiler_params=pltpu.CompilerParams(vmem_limit_bytes=VMEM[name] * MIB),
        name=name,
    )(*args, *waits, *carry)
    return outs


def groups_at(meta):
    return (meta.shape[0] - 2) // 2


def rows_used(meta):
    return meta[meta.shape[0] - 2]


def device_of(meta):
    return meta[meta.shape[0] - 1]


def core_of(meta):
    return device_of(meta) % 2


def attn_fwd_kernel(meta, tok, wf0, wf1, attn0, attn1, qkv0, qkv1, xhat_out, lse0, lse1, wpad0, wpad1,
                    tok32, out32, bias):
    i = pl.program_id(0)
    rows, width = tok.shape
    cols = 3 * PAIR_PAD
    sides = ((wf0, qkv0, lse0, wpad0), (wf1, qkv1, lse1, wpad1))

    @pl.when(i == 0)
    def _():
        tok32[:rows] = tok[...].astype(F32)
        tok32[rows:] = jnp.zeros((tok32.shape[0] - rows, width), F32)
        vec = wf0[:, 3 * PAIR_DIM :].astype(F32).T
        bias[0:2, :width] = vec[0:2]
        for c in range(2):

            @pl.when(core_of(meta) == c)
            def _():
                for p in range(2):
                    at = (p ^ c) * PAIR_DIM
                    parts = [pad_heads(vec[r : r + 1, at : at + PAIR_DIM]) for r in (2, 3)]
                    bias[2 + p : 3 + p, :] = jnp.concatenate(
                        [parts[0], jnp.zeros((1, PAIR_PAD), F32), parts[1]], axis=1
                    )

        for wf, _, _, wpad in sides:
            wpad[...] = pad_heads(wf[:, : 3 * PAIR_DIM].astype(F32)).astype(BF16)

    start = meta[i]

    def work(length, padded):
        xhat, _ = row_norm(load_rows(tok32, start, padded))
        normed = (xhat * bias[0:1, :width] + bias[1:2, :width]).astype(BF16)
        xhat_out[0, :padded, :] = xhat.astype(BF16)
        for p, (_, qkv, lse, wpad) in enumerate(sides):
            qkv[0, :padded, :] = (dot_nn(normed, wpad[...]) + bias[2 + p : 3 + p, :]).astype(BF16)
        heads = [(p, h) for p in range(2) for h in range(PAIR)]
        scores = []
        for p, h in heads:
            qkv, at = sides[p][1], h * HEAD_PAD
            q = qkv[0, :padded, at : at + HEAD_PAD]
            k = qkv[0, :padded, PAIR_PAD + at : PAIR_PAD + at + HEAD_PAD]
            scores.append(dot_nt(k, q))
        probs = []
        for (p, h), s in zip(heads, scores):
            if length < padded:
                key = lax.broadcasted_iota(jnp.int32, s.shape, 0)
                s = jnp.where(key < length, s, -1e30)
            top = jnp.max(s, axis=0, keepdims=True)
            e = jnp.exp2((s - top) * EXP_SCALE)
            total = jnp.sum(e, axis=0, keepdims=True)
            probs.append((e * (1.0 / total)).astype(BF16))
            sides[p][2][0, h : h + 1, :padded] = top * EXP_SCALE + jnp.log2(total)
        outs = []
        for (p, h), prob in zip(heads, probs):
            at = 2 * PAIR_PAD + h * HEAD_PAD
            outs.append(dot_tn(prob, sides[p][1][0, :padded, at : at + HEAD_PAD]))
        store_rows(out32, start, length, jnp.concatenate(outs, axis=1), slice(None))

    by_group(meta[groups_at(meta) + i], work)

    @pl.when(i == pl.num_programs(0) - 1)
    def _():
        row = lax.broadcasted_iota(jnp.int32, (rows, 1), 0)
        mixed = jnp.where(row < rows_used(meta), out32[:rows], 0.0).astype(BF16)
        attn0[...] = mixed[:, :PAIR_PAD]
        attn1[...] = mixed[:, PAIR_PAD:]


def attn_fwd(meta, tokens, wf, waits, carry):
    rows, width = tokens.shape
    slots = groups_at(meta)
    cols = 3 * PAIR_PAD
    out_shape = [jax.ShapeDtypeStruct((rows, PAIR_PAD), BF16)] * 2
    out_shape += [jax.ShapeDtypeStruct((slots, SLOT, cols), BF16)] * 2
    out_shape += [jax.ShapeDtypeStruct((slots, SLOT, width), BF16)]
    out_shape += [jax.ShapeDtypeStruct((slots, 8, 512), F32)] * 2
    out_shape += [jax.ShapeDtypeStruct((width, cols), BF16)] * 2
    stats = pl.BlockSpec((1, 8, 512), lambda i, m: (i, 0, 0))
    out_specs = [whole(out_shape[0])] * 2 + [slot_block(cols)] * 2 + [slot_block(width)]
    out_specs += [stats] * 2 + [whole(out_shape[-1])] * 2
    scratch = [
        pltpu.VMEM((rows + ROW_PAD, width), F32),
        pltpu.VMEM((rows + ROW_PAD, 2 * PAIR_PAD), F32),
        pltpu.VMEM((8, cols), F32),
    ]
    in_specs = [whole(tokens), whole(wf[0]), whole(wf[1])]
    args = (meta, tokens, *wf)
    return call(attn_fwd_kernel, "attn_fwd", slots, in_specs, out_specs, out_shape, scratch, args, waits, carry)


def put_blocks(to, value, col, shards, parity=None):
    rows, cols = value.shape
    size = rows // shards
    half = rows // 2
    if size % 16:
        if parity is not None:
            value = value[parity * half : (parity + 1) * half]
        to[:, col : col + cols] = value
        return
    for n, place in enumerate(turned(shards)):
        at = place * size
        if parity is not None:
            if n % 2 != parity:
                continue
            at -= parity * half
        to[at : at + size, col : col + cols] = value[n * size : (n + 1) * size]


def mlp_kernel(meta, tok, cot, attn0, attn1, w0, w1, b0, b1, x1o, acto, dx1, da0, da1,
               keep_a, send_a, keep_b, send_b, wproj, rowvec, gd, gu, gp, gsum, *, shards):
    i = pl.program_id(0)
    rows, width = tok.shape
    parts = (w0, w1)
    lower = (b0, b1)

    def in_order(first, second, use):
        for c in range(2):
            pl.when(core_of(meta) == c)(partial(use, c, *((first, second) if c == 0 else (second, first))))

    @pl.when(i == 0)
    def _():
        def use(c, low, high):
            flat = [ref[x][:, width : width + VEC] for ref in (low, high) for x in range(2)]
            proj = jnp.concatenate(flat[: width // VEC], axis=1)
            wproj[...] = jnp.zeros(wproj.shape, BF16)
            for h in range(2 * PAIR):
                at = (h ^ (PAIR * c)) * HEAD_PAD
                wproj[at : at + HEAD_DIM] = proj[h * HEAD_DIM : (h + 1) * HEAD_DIM]
            vec = flat[-1].astype(F32).T
            for r in range(4):
                rowvec[r : r + 1, :width] = vec[r : r + 1]
                at = (r ^ (2 * c)) * width
                rowvec[4:5, at : at + width] = vec[4 + r : 5 + r]

        in_order(w0, w1, use)
        gd[...] = jnp.zeros(gd.shape, F32)
        gu[...] = jnp.zeros(gu.shape, F32)
        gp[...] = jnp.zeros(gp.shape, F32)
        gsum[...] = jnp.zeros(gsum.shape, F32)

    proj_bias, gain, shift, down_bias = [rowvec[r : r + 1, :width] for r in range(4)]
    row = lax.broadcasted_iota(jnp.int32, (rows, 1), 0) + i * rows
    valid = (row < rows_used(meta)).astype(F32)
    dy = cot[...].astype(F32) * valid
    dyb = dy.astype(BF16)
    chunk = 2 * width
    ups = [jnp.concatenate([parts[c][0][:, :width], parts[c][1][:, :width]], axis=1) for c in range(2)]
    downs = [jnp.concatenate([lower[c][x] for x in range(2)], axis=0) for c in range(2)]
    dacts = [dot_nt(dyb, downs[c]) for c in range(2)]
    mixed0, mixed1 = attn0[...], attn1[...]
    x1 = tok[...].astype(F32) + dot_nn(mixed0, wproj[:PAIR_PAD]) + dot_nn(mixed1, wproj[PAIR_PAD:])
    x1 = x1 + proj_bias
    x1o[...] = (x1 + down_bias) * valid
    xhat, inverse = row_norm(x1)
    normed = (xhat * gain + shift).astype(BF16)
    dn = jnp.zeros((rows, width), F32)
    kept = []
    for c in range(2):
        at = c * chunk
        pre = dot_nn(normed, ups[c]) + rowvec[4:5, at : at + chunk]
        act, slope = gelu_pair(pre)
        actb = act.astype(BF16)
        acto[:, at : at + chunk] = actb
        dpre = dacts[c] * slope
        dpreb = dpre.astype(BF16)
        gsum[4:5, at : at + chunk] += jnp.sum(dpre, axis=0, keepdims=True)
        dn = dn + dot_nt(dpreb, ups[c])
        kept.append(dpreb)
    for c in range(2):
        at = c * chunk
        gd[:, at : at + chunk] += dot_tn(dyb, acto[:, at : at + chunk])
        gu[:, at : at + chunk] += dot_tn(normed, kept[c])
    dx = dy + row_norm_back(dn * gain, xhat, inverse)
    dx1[...] = dx
    dxb = dx.astype(BF16)
    gp[:, :PAIR_PAD] += dot_tn(dxb, mixed0)
    gp[:, PAIR_PAD:] += dot_tn(dxb, mixed1)
    da0[...] = dot_nt(dxb, wproj[:PAIR_PAD]).astype(BF16)
    da1[...] = dot_nt(dxb, wproj[PAIR_PAD:]).astype(BF16)
    gsum[0:1, :width] += jnp.sum(dx, axis=0, keepdims=True)
    gsum[1:2, :width] += jnp.sum(dn * xhat, axis=0, keepdims=True)
    gsum[2:3, :width] += jnp.sum(dn, axis=0, keepdims=True)
    gsum[3:4, :width] += jnp.sum(dy, axis=0, keepdims=True)

    @pl.when(i == pl.num_programs(0) - 1)
    def _():
        for half, (to_a, to_b) in enumerate(((keep_a, keep_b), (send_a, send_b))):
            for x in range(2):
                at = (2 * half + x) * width
                put_blocks(to_a.at[x], gu[:, at : at + width].astype(BF16), 0, shards)
                part = gd[:, at : at + width].T.astype(BF16)
                for y in range(2):
                    put_blocks(to_b.at[y, x], part, 0, shards, y)

        def use(c, low, high):
            rows_of = [gsum[r : r + 1, :width] for r in range(4)]
            for r in range(4):
                at = (r ^ (2 * c)) * width
                rows_of.append(gsum[4:5, at : at + width])
            vec = jnp.concatenate(rows_of + [jnp.zeros((VEC - 8, width), F32)], axis=0).T
            grad = unpad_heads(gp[...]).T
            first, second = grad[:PAIR_DIM], grad[PAIR_DIM:]
            proj = jnp.concatenate([second, first] if c else [first, second], axis=0)
            flat = jnp.concatenate([proj, vec], axis=1).astype(BF16)
            for k in range(QUARTERS):
                to = (low, high)[k // 2].at[k % 2]
                put_blocks(to, flat[:, k * VEC : (k + 1) * VEC], width, shards)

        in_order(keep_a, send_a, use)


def mlp(meta, tokens, cotangent, attn, w, shards, block=512):
    rows, width = tokens.shape
    hidden = QUARTERS * width
    by_row = lambda cols: pl.BlockSpec((block, cols), lambda i, m: (i, 0))
    out_shape = [
        jax.ShapeDtypeStruct((rows, width), F32),
        pltpu.HBM((rows, hidden), BF16),
        jax.ShapeDtypeStruct((rows, width), F32),
        jax.ShapeDtypeStruct((rows, PAIR_PAD), BF16),
        jax.ShapeDtypeStruct((rows, PAIR_PAD), BF16),
    ]
    out_shape += [jax.ShapeDtypeStruct((2, width, width + VEC), BF16)] * 2
    out_shape += [jax.ShapeDtypeStruct((2, 2, width // 2, width), BF16)] * 2
    out_specs = [by_row(s.shape[1]) for s in out_shape[:5]] + [whole(s) for s in out_shape[5:]]
    in_specs = [by_row(width)] * 2 + [by_row(PAIR_PAD)] * 2 + [whole(t) for t in w]
    scratch = [
        pltpu.VMEM((2 * PAIR_PAD, width), BF16),
        pltpu.VMEM((8, hidden), F32),
        pltpu.VMEM((width, hidden), F32),
        pltpu.VMEM((width, hidden), F32),
        pltpu.VMEM((width, 2 * PAIR_PAD), F32),
        pltpu.VMEM((8, hidden), F32),
    ]
    args = (meta, tokens, cotangent, *attn, *w)
    kernel = partial(mlp_kernel, shards=shards)
    return call(kernel, "mlp", rows // block, in_specs, out_specs, out_shape, scratch, args)


def layer_out_kernel(meta, x1, act, b0, b1, out):
    rows, width = x1.shape
    row = lax.broadcasted_iota(jnp.int32, (rows, 1), 0) + pl.program_id(0) * rows
    valid = (row < rows_used(meta)).astype(F32)
    y = x1[...]
    for c, ref in enumerate((b0, b1)):
        down = jnp.concatenate([ref[x] for x in range(2)], axis=0)
        y = y + dot_nn(act[:, 2 * c * width : 2 * (c + 1) * width], down) * valid
    out[...] = y.astype(BF16)


def layer_output(meta, x1, act, w, waits, carry, block=512):
    rows, width = x1.shape
    by_row = lambda cols: pl.BlockSpec((block, cols), lambda i, m: (i, 0))
    return call(
        layer_out_kernel,
        "layer_out",
        rows // block,
        [by_row(width), by_row(act.shape[1]), whole(w[0]), whole(w[1])],
        [by_row(width)],
        [jax.ShapeDtypeStruct((rows, width), BF16)],
        [],
        (meta, x1, act, *w),
        waits,
        carry,
    )


def attn_bwd_kernel(meta, qkv, xhat, lse, dattn, wpad, wf, dqkv, grads, da32, gw, gsum, *, own, shards):
    i = pl.program_id(0)
    rows = dattn.shape[0]
    width = wf.shape[0]

    @pl.when(i == 0)
    def _():
        da32[:rows] = dattn[...].astype(F32)
        da32[rows:] = jnp.zeros((da32.shape[0] - rows, PAIR_PAD), F32)
        gw[...] = jnp.zeros(gw.shape, F32)
        gsum[...] = jnp.zeros(gsum.shape, F32)

    start = meta[i]

    def work(length, padded):
        da = load_rows(da32, start, padded)
        if length < padded:
            keep = lax.broadcasted_iota(jnp.int32, (padded, 1), 0) < length
            da = jnp.where(keep, da, 0.0)
        da = da.astype(BF16)
        def cut(ref, part, h):
            at = part * PAIR_PAD + h * HEAD_PAD
            return ref[0, :padded, at : at + HEAD_PAD]

        heads = range(PAIR)
        das = [da[:, h * HEAD_PAD : (h + 1) * HEAD_PAD] for h in heads]
        scores = [dot_nt(cut(qkv, 1, h), cut(qkv, 0, h)) for h in heads]
        dps = [dot_nt(cut(qkv, 2, h), das[h]) for h in heads]
        ps, dss = [], []
        for h in heads:
            p = jnp.exp2(scores[h] * EXP_SCALE - lse[0, h : h + 1, :padded])
            if length < padded:
                key = lax.broadcasted_iota(jnp.int32, p.shape, 0)
                p = jnp.where(key < length, p, 0.0)
            mean = jnp.sum(p * dps[h], axis=0, keepdims=True)
            dss.append((p * (dps[h] - mean)).astype(BF16))
            ps.append(p.astype(BF16))
        parts = [[dot_tn(dss[h], cut(qkv, 1, h)) * SCALE for h in heads]]
        parts += [[dot_nn(dss[h], cut(qkv, 0, h)) * SCALE for h in heads]]
        parts += [[dot_nn(ps[h], das[h]) for h in heads]]
        d = []
        for part in range(3):
            value = jnp.concatenate(parts[part], axis=1)
            at = part * PAIR_PAD
            if part != 1:
                gsum[0:1, at : at + PAIR_PAD] += jnp.sum(value, axis=0, keepdims=True)
            d.append(value.astype(BF16))
        d = jnp.concatenate(d, axis=1)
        dqkv[0, :padded, :] = d
        gw[...] += dot_tn(xhat[0, :padded, :], d)
        gsum[1:2, :] += jnp.sum(d.astype(F32), axis=0, keepdims=True)

    by_group(meta[groups_at(meta) + i], work)

    @pl.when(i == pl.num_programs(0) - 1)
    def _():
        w = wpad[...].astype(F32)
        raw = gw[...]
        col = gsum[1:2, :]
        gain_term = jnp.sum(raw * w, axis=1, keepdims=True)
        bias_term = jnp.sum(col * w, axis=1, keepdims=True)
        vec = wf[:, 3 * PAIR_DIM :].astype(F32)
        main = unpad_heads(raw * vec[:, 0:1] + vec[:, 1:2] * col).astype(BF16)
        put_blocks(grads, main, 0, shards)
        q_sum = unpad_heads(gsum[0:1, :PAIR_PAD])
        v_sum = unpad_heads(gsum[0:1, 2 * PAIR_PAD :])
        gap = jnp.zeros((1, width - PAIR_DIM), F32)
        for c in range(2):

            @pl.when(core_of(meta) == (c if own else 1 - c))
            def _():
                rows_of = [jnp.concatenate([gap, t] if c else [t, gap], axis=1) for t in (q_sum, v_sum)]
                rows_of = [jnp.zeros((2, width), F32)] + rows_of + [jnp.zeros((VEC - 4, width), F32)]
                sums = jnp.concatenate(rows_of, axis=0).T
                lane = lax.broadcasted_iota(jnp.int32, sums.shape, 1)
                tail = jnp.where(lane == 0, gain_term, jnp.where(lane == 1, bias_term, sums))
                put_blocks(grads, tail[:, :VEC_PAIR].astype(BF16), 3 * PAIR_DIM, shards)


def attn_bwd(meta, qkv, xhat, lse, dattn, wpad, wf, own, shards, waits, carry):
    rows = dattn.shape[0]
    width = wf.shape[0]
    cols = 3 * PAIR_PAD
    out_shape = [jax.ShapeDtypeStruct(qkv.shape, BF16), jax.ShapeDtypeStruct(wf.shape, BF16)]
    in_specs = [slot_block(cols), slot_block(width), pl.BlockSpec((1, 8, 512), lambda i, m: (i, 0, 0))]
    in_specs += [whole(dattn), whole(wpad), whole(wf)]
    scratch = [
        pltpu.VMEM((rows + ROW_PAD, PAIR_PAD), F32),
        pltpu.VMEM((width, cols), F32),
        pltpu.VMEM((8, cols), F32),
    ]
    args = (meta, qkv, xhat, lse, dattn, wpad, wf)
    kernel = partial(attn_bwd_kernel, own=own, shards=shards)
    out_specs = [slot_block(cols), whole(wf)]
    grid = groups_at(meta)
    return call(kernel, "attn_bwd", grid, in_specs, out_specs, out_shape, scratch, args, waits, carry)


def input_grad_kernel(meta, tok, d0, d1, w0, w1, wf, dx1, out, tok32, bias):
    i = pl.program_id(0)
    rows, width = tok.shape

    @pl.when(i == 0)
    def _():
        tok32[:rows] = tok[...].astype(F32)
        tok32[rows:] = jnp.zeros((tok32.shape[0] - rows, width), F32)
        bias[...] = wf[:, 3 * PAIR_DIM :].astype(F32).T[0:8]

    start = meta[i]

    def work(length, padded):
        dn = dot_nt(d0[0, :padded, :], w0[...]) + dot_nt(d1[0, :padded, :], w1[...])
        xhat, inverse = row_norm(load_rows(tok32, start, padded))
        dx = row_norm_back(dn * bias[0:1, :], xhat, inverse)
        store_rows(tok32, start, length, dx, slice(None))

    by_group(meta[groups_at(meta) + i], work)

    @pl.when(i == pl.num_programs(0) - 1)
    def _():
        row = lax.broadcasted_iota(jnp.int32, (rows, 1), 0)
        total = dx1[...] + tok32[:rows]
        out[...] = jnp.where(row < rows_used(meta), total, 0.0).astype(BF16)


def input_grad(meta, tokens, d, w, wf, dx1, waits, carry):
    rows, width = tokens.shape
    slot = slot_block(d[0].shape[2])
    in_specs = [whole(tokens), slot, slot] + [whole(t) for t in (*w, wf, dx1)]
    scratch = [pltpu.VMEM((rows + ROW_PAD, width), F32), pltpu.VMEM((8, width), F32)]
    out_shape = [jax.ShapeDtypeStruct((rows, width), BF16)]
    args = (meta, tokens, *d, *w, wf, dx1)
    grid, out_specs = groups_at(meta), [whole(tokens)]
    return call(
        input_grad_kernel, "input_grad", grid, in_specs, out_specs, out_shape, scratch, args, waits, carry
    )


def final_parts(core, own, got, shards):
    size = own.shape[0]
    width = shards * size
    cut = 3 * PAIR_DIM + VEC_PAIR
    low, high = (got, own) if core else (own, got)
    qkv = [t[:, part * PAIR_DIM : (part + 1) * PAIR_DIM] for part in range(3) for t in (low, high)]
    step = (low.shape[1] - cut) // 2
    quarters = [t[:, cut + x * step : cut + (x + 1) * step] for t in (low, high) for x in range(2)]
    extra_at, down_at = width, width + VEC
    extra = [q[:, extra_at:down_at] for q in quarters]
    up = [q[:, n * size : (n + 1) * size] for n in range(shards) for q in quarters]
    down = jnp.concatenate([q[:, down_at:] for q in quarters], axis=0)
    ends = low[:, 3 * PAIR_DIM : cut] + high[:, 3 * PAIR_DIM : cut]
    columns = jnp.concatenate([ends[:, :4], extra[-1][:, : 4 + QUARTERS]], axis=1)
    cat = lambda parts: jnp.concatenate(parts, axis=1)
    return cat(qkv), cat(extra[: width // VEC]), cat(up), down, columns


def finish_kernel(meta, own, got, *outs, shards):
    size = own.shape[0]

    def use(core):
        *mats, columns = final_parts(core, own[...].astype(F32), got[...].astype(F32), shards)
        for mat, out in zip(mats, outs):
            tiles = mat.shape[1] // 128
            for t in range(tiles):
                out[pl.ds(t, mat.shape[0], stride=tiles), :] = mat[:, t * 128 : (t + 1) * 128]
        count = columns.shape[1]
        square = jnp.concatenate([columns, jnp.zeros((size, 128 - count), F32)], axis=1)
        square = jnp.concatenate([square, jnp.zeros((128 - size, 128), F32)], axis=0)
        outs[4][...] = square.T[:16]

    for c in range(2):
        pl.when(core_of(meta) == c)(partial(use, c))


def finish(meta, own, got, shards):
    size = own.shape[0]
    width = shards * size
    if size % 16:
        core = core_of(meta) == 1
        own, got = own.astype(F32), got.astype(F32)
        parts = final_parts(0, jnp.where(core, got, own), jnp.where(core, own, got), shards)
        return [p.reshape(-1) for p in parts[:4]], parts[4].T
    sizes = [size * 3 * width, size * width, size * QUARTERS * width, size * QUARTERS * width]
    out_shape = [jax.ShapeDtypeStruct((n // 128, 128), F32) for n in sizes + [16 * 128]]
    out_specs = [whole(t) for t in out_shape]
    kernel = partial(finish_kernel, shards=shards)
    outs = call(kernel, "finish", 1, [whole(own), whole(got)], out_specs, out_shape, [], (meta, own, got))
    return [t.reshape(-1) for t in outs[:4]], outs[4]


def turned(shards):
    count = shards.bit_length() - 1
    return [sum(((n >> b) & 1) << (count - 1 - b) for b in range(count)) for n in range(shards)]


def image_table(size_group, assignment, device, slots):
    owned = assignment == device
    rank = jnp.cumsum(owned.astype(jnp.int32)) - 1
    slot = jnp.arange(slots, dtype=jnp.int32)
    here = owned[None, :] & (rank[None, :] == slot[:, None])
    groups = jnp.sum(jnp.where(here, size_group[None, :], 0), axis=1)
    lengths = jnp.where(groups == 0, LENS[0], jnp.where(groups == 1, LENS[1], LENS[2]))
    ends = jnp.sum(jnp.where(slot[None, :] <= slot[:, None], lengths[None, :], 0), axis=1)
    return jnp.concatenate([ends - lengths, groups, ends[-1:], device[None]]).astype(jnp.int32)


def swap(value, axis, bit):
    size = lax.axis_size(axis)
    return lax.ppermute(value, axis, [(i, i ^ bit) for i in range(size)])


def sides_of(bits):
    table = {}
    for axis, those in bits.items():
        for bit in those:
            mine = (lax.axis_index(axis) & bit) // bit
            table[axis, bit] = (mine.astype(jnp.uint32), (1 - mine).astype(jnp.uint32), mine == 1)
    return table


def pick(sides, value, axis, bit, dim):
    mine, theirs, _ = sides[axis, bit]
    keep = lax.dynamic_index_in_dim(value, mine, dim, keepdims=False)
    send = lax.dynamic_index_in_dim(value, theirs, dim, keepdims=False)
    return keep, send


def join(upper, own, other, dim):
    return jnp.stack([jnp.where(upper, other, own), jnp.where(upper, own, other)], axis=dim)


def added(keep, got):
    return (keep.astype(F32) + got.astype(F32)).astype(BF16)


def after(value, *others):
    return lax.optimization_barrier((value, *others))[0]


class Gather:
    def __init__(self, sides, part, keys):
        self.sides, self.part, self.keys, self.have = sides, part, keys, []

    def grow(self, axis, bit, *others, upper=None):
        if others:
            self.part = after(self.part, *others)
        upper = self.sides[axis, bit][2] if upper is None else upper
        dim = sum(self.keys.index(k) < self.keys.index((axis, bit)) for k in self.have)
        self.part = join(upper, self.part, swap(self.part, axis, bit), dim)
        self.have.append((axis, bit))
        return self


def body(
    tokens,
    cotangent,
    size_group,
    assignment,
    ln1_gain,
    ln1_bias,
    w_qkv,
    q_bias,
    v_bias,
    w_proj,
    proj_bias,
    ln2_gain,
    ln2_bias,
    w_up,
    up_bias,
    w_down,
    down_bias,
):
    rows, width = tokens.shape
    shards = lax.axis_size("fsdp")
    size = width // shards
    devices = shards * lax.axis_size("dp")
    device = lax.axis_index("fsdp") * lax.axis_size("dp") + lax.axis_index("dp")
    bits = [1 << b for b in range(shards.bit_length() - 1)]
    far, near, y = bits[2:], bits[1:2], bits[0]
    tail_keys = [("fsdp", b) for b in reversed(bits)]
    sides = sides_of({"dp": (1, 2), "fsdp": bits})
    core, column = sides["dp", 1][0], sides["dp", 2][0]

    vectors = [ln1_gain, ln1_bias, q_bias, v_bias, proj_bias, ln2_gain, ln2_bias, down_bias]
    vectors = jnp.concatenate([jnp.stack(vectors), up_bias.reshape(QUARTERS, size)]).T
    pair = w_qkv.reshape(size, 3, 2, PAIR_DIM)
    pair = lax.dynamic_index_in_dim(pair, core, 2, keepdims=False).reshape(size, 3 * PAIR_DIM)
    pair = jnp.concatenate([pair, vectors[:, :4], jnp.zeros((size, VEC_PAIR - 4), BF16)], axis=1)
    f = Gather(sides, pair, tail_keys)
    w_up, w_down, w_proj, _ = lax.optimization_barrier((w_up, w_down, w_proj, pair))
    quarter = 2 * core + column
    extra = [w_proj.reshape(size, width), vectors[:, 4:], jnp.zeros((size, VEC - 4 - QUARTERS), BF16)]
    extra = lax.dynamic_slice_in_dim(jnp.concatenate(extra, axis=1), quarter * VEC, VEC, 1)
    up = lax.dynamic_index_in_dim(w_up.reshape(size, shards, QUARTERS, size), quarter, 2, False)
    part_a = jnp.concatenate([up.reshape(size, width), extra], axis=1)
    part_b = lax.dynamic_index_in_dim(w_down.reshape(QUARTERS, size, width), quarter, 0, False)
    ab = Gather(sides, jnp.concatenate([part_a, part_b], axis=1), tail_keys)

    for bit in far:
        f.grow("fsdp", bit)
    for bit in far:
        ab.grow("fsdp", bit)
    for bit in near:
        f.grow("fsdp", bit)
    for bit in near:
        ab.grow("fsdp", bit)
    size_group, assignment, _ = lax.optimization_barrier((size_group, assignment, f.part))
    table = image_table(size_group, assignment, device, size_group.shape[0] // devices)
    f.grow("fsdp", y)
    own = f.part.reshape(width, -1)
    cut = width + VEC
    keys = [("dp", 2)] + tail_keys
    a, b = Gather(sides, ab.part[..., :cut], keys), Gather(sides, ab.part[..., cut:], keys)
    a.have, b.have = list(ab.have), list(ab.have)
    a.grow("dp", 2)
    b.grow("fsdp", y)
    wf = (own, swap(own, "dp", 1))

    upper = jnp.stack([sides["fsdp", y][2], sides["dp", 2][2]])
    upper = jnp.broadcast_to(upper[:, None, None], (2, 8, cut)).astype(jnp.int32)
    table, sides, upper = lax.optimization_barrier((table, sides, upper))
    attn0, attn1, qkv0, qkv1, xhat, lse0, lse1, wpad0, wpad1, upper = attn_fwd(
        table, tokens, wf, (a.part, b.part), (upper,)
    )
    a.grow("fsdp", y, upper=upper[0, 0] != 0)
    b.grow("dp", 2, upper=upper[1, 0, :width] != 0)
    wa, wb = a.part.reshape(2, width, cut), b.part.reshape(2, width, width)
    w = (wa, swap(wa, "dp", 1), wb, swap(wb, "dp", 1))
    x1, act, dx1, dattn0, dattn1, keep_a, send_a, keep_b, send_b = mlp(
        table, tokens, cotangent, (attn0, attn1), w, shards
    )

    def by_bits(value, lead):
        if size % 16:
            value = value.reshape(value.shape[:lead] + (2,) * len(bits) + (size, value.shape[-1]))
            order = [lead + b for b in reversed(range(len(bits)))]
            return value.transpose(*range(lead), *order, *range(lead + len(bits), value.ndim))
        return value.reshape(value.shape[:lead] + (2,) * len(bits) + (size, value.shape[-1]))

    def halves_of_b(value):
        if size % 16:
            value = value.swapaxes(0, 1).reshape(2, width, width)
            return by_bits(value, 1).swapaxes(0, 1)
        return value.reshape((2, 2) + (2,) * (len(bits) - 1) + (size, width))

    got_a, got_b = swap(send_a, "dp", 1), swap(send_b, "dp", 1)
    d1, send_g, keep_a, keep_b = attn_bwd(
        table, qkv1, xhat, lse1, dattn1, wpad1, wf[1], False, shards, (send_a, send_b), (keep_a, keep_b)
    )
    got_g = swap(send_g, "dp", 1)
    keep_a, send_a = pick(sides, by_bits(added(keep_a, got_a), 1), "dp", 2, 0)
    keep_b, send_b = pick(sides, halves_of_b(added(keep_b, got_b)), "fsdp", y, 0)
    got_a, got_b = swap(send_a, "dp", 2), swap(send_b, "fsdp", y)
    d0, keep_g, keep_a, keep_b = attn_bwd(
        table, qkv0, xhat, lse0, dattn0, wpad0, wf[0], True, shards, (send_a, send_b, send_g), (keep_a, keep_b)
    )
    part = jnp.concatenate([by_bits(added(keep_g, got_g), 0), added(keep_a, got_a)], axis=-1)
    keep, send = pick(sides, part, "fsdp", y, 0)
    keep_b, send_b = pick(sides, added(keep_b, got_b), "dp", 2, 0)
    got, got_b = swap(send, "fsdp", y), swap(send_b, "dp", 2)
    grads_of = (table, tokens, (d0, d1), (wpad0, wpad1), wf[0], dx1)
    grad_input, keep, keep_b = input_grad(*grads_of, (send, send_b), (keep, keep_b))
    part = jnp.concatenate([added(keep, got), added(keep_b, got_b)], axis=-1)
    for count, bit in enumerate(bits[1:]):
        keep, send = pick(sides, part, "fsdp", bit, 0)
        got = swap(send, "fsdp", bit)
        if count == 0:
            layer_out, keep = layer_output(table, x1, act, w[2:], (send,), (keep,))
        part = added(keep, got)
    got = swap(part, "dp", 2)
    cut = keep_g.shape[-1]
    part_g = added(part[:, :cut], got[:, :cut])
    low, high = part[:, cut:], got[:, cut:]
    upper = sides["dp", 2][2]
    part = [part_g, jnp.where(upper, high, low), jnp.where(upper, low, high)]
    part = jnp.concatenate(part, axis=1)
    flat, vectors = finish(table, part, swap(part, "dp", 1), shards)
    g = [vectors[r, :size] for r in range(8)] + [vectors[8 : 8 + QUARTERS, :size].reshape(-1)]
    qkv, proj, up, down = flat
    return (
        layer_out, grad_input, g[0], g[1], qkv, g[2], g[3], proj, g[4], g[5], g[6], up, g[8], down, g[7]
    )


def solution(mesh):
    rows = P(("fsdp", "dp"), None)
    flat = P("fsdp")
    return jax.shard_map(
        body,
        mesh=mesh,
        in_specs=(rows, rows, P(), P()) + (flat,) * 13,
        out_specs=(rows, rows) + (flat,) * 13,
        check_vma=False,
    )
```

```python
from functools import partial
import math

import jax
import jax.numpy as jnp
from jax import lax
from jax.experimental import pallas as pl
from jax.experimental.pallas import tpu as pltpu
from jax.sharding import PartitionSpec as P

HEAD_DIM = 96
HEAD_PAD = 128
LENS = (196, 256, 400)
SLOT = 400
ROW_PAD = 32
PAIR = 2
PAIR_DIM = PAIR * HEAD_DIM
PAIR_PAD = PAIR * HEAD_PAD
QUARTERS = 4
VEC = 128
VEC_PAIR = 64
SCALE = 1.0 / math.sqrt(HEAD_DIM)
EXP_SCALE = SCALE * math.log2(math.e)
MIB = 1024 * 1024
VMEM = {"attn_fwd": 12, "mlp": 21, "attn_bwd": 8, "layer_out": 8, "input_grad": 10, "finish": 10}
F32 = jnp.float32
BF16 = jnp.bfloat16


def dot_nn(a, b):
    return lax.dot_general(a, b, (((1,), (0,)), ((), ())), preferred_element_type=F32)


def dot_nt(a, b):
    return lax.dot_general(a, b, (((1,), (1,)), ((), ())), preferred_element_type=F32)


def dot_tn(a, b):
    return lax.dot_general(a, b, (((0,), (0,)), ((), ())), preferred_element_type=F32)


def pad_heads(values):
    rows, cols = values.shape
    gap = jnp.zeros((rows, HEAD_PAD - HEAD_DIM), values.dtype)
    parts = []
    for h in range(cols // HEAD_DIM):
        parts += [values[:, h * HEAD_DIM : (h + 1) * HEAD_DIM], gap]
    return jnp.concatenate(parts, axis=1)


def unpad_heads(values):
    rows, cols = values.shape
    return jnp.concatenate(
        [values[:, h * HEAD_PAD : h * HEAD_PAD + HEAD_DIM] for h in range(cols // HEAD_PAD)], axis=1
    )


def row_norm(x):
    center = x - jnp.mean(x, axis=-1, keepdims=True)
    inverse = lax.rsqrt(jnp.mean(center * center, axis=-1, keepdims=True) + 1e-6)
    return center * inverse, inverse


def row_norm_back(e, xhat, inverse):
    return inverse * (
        e - jnp.mean(e, axis=-1, keepdims=True) - xhat * jnp.mean(e * xhat, axis=-1, keepdims=True)
    )


def load_rows(ref, start, count):
    base = pl.multiple_of((start // 8) * 8, 8)
    window = ref[pl.ds(base, count + 8), :]
    moved = pltpu.roll(window, count + 4, 0)
    return jnp.where(start % 8 == 0, window, moved)[:count]


def store_rows(ref, start, length, values, cols):
    count = -(-length // 8) * 8
    base = pl.multiple_of((start // 8) * 8, 8)
    window = jnp.concatenate([values[:count], jnp.zeros((8, values.shape[1]), values.dtype)], axis=0)
    window = jnp.where(start % 8 == 0, window, pltpu.roll(window, 4, 0))
    row = lax.broadcasted_iota(jnp.int32, window.shape, 0) - start % 8
    held = ref[pl.ds(base, count + 8), cols]
    ref[pl.ds(base, count + 8), cols] = jnp.where((row >= 0) & (row < length), window, held)


def by_group(group, work):
    for g, length in enumerate(LENS):
        pl.when(group == g)(partial(work, length, -(-length // 16) * 16))


def gelu_pair(u):
    cdf = 0.5 + 0.5 * lax.erf(u * (1.0 / math.sqrt(2.0)))
    bell = jnp.exp2((u * u) * (-0.5 * math.log2(math.e)))
    return u * cdf, cdf + u * (bell * (1.0 / math.sqrt(2.0 * math.pi)))


def whole(array):
    at = (0,) * len(array.shape)
    return pl.BlockSpec(array.shape, lambda i, m: at, pipeline_mode=pl.Buffered(1))


def slot_block(cols):
    return pl.BlockSpec((1, SLOT, cols), lambda i, m: (i, 0, 0))


def call(kernel, name, grid, in_specs, out_specs, out_shape, scratch, args, waits=(), carry=(), far=()):
    given, made, passed = len(in_specs) + 1, len(out_shape), len(waits) + len(carry)

    def ordered(*refs):
        kernel(*refs[:given], *refs[given + passed : given + passed + made], *refs[given + passed + made + len(carry) :])

    args = [
        pltpu.with_memory_space_constraint(t, pltpu.HBM) if at in far else t for at, t in enumerate(args)
    ]
    anywhere = pl.BlockSpec(memory_space=pl.ANY)
    outs = pl.pallas_call(
        ordered,
        grid_spec=pltpu.PrefetchScalarGridSpec(
            num_scalar_prefetch=1,
            grid=(grid,),
            in_specs=list(in_specs) + [anywhere] * passed,
            out_specs=list(out_specs) + [anywhere] * len(carry),
            scratch_shapes=scratch,
        ),
        out_shape=list(out_shape) + [jax.ShapeDtypeStruct(t.shape, t.dtype) for t in carry],
        input_output_aliases={given + len(waits) + n: made + n for n in range(len(carry))},
        compiler_params=pltpu.CompilerParams(vmem_limit_bytes=VMEM[name] * MIB),
        name=name,
    )(*args, *waits, *carry)
    return outs


def groups_at(meta):
    return (meta.shape[0] - 2) // 2


def rows_used(meta):
    return meta[meta.shape[0] - 2]


def device_of(meta):
    return meta[meta.shape[0] - 1]


def core_of(meta):
    return device_of(meta) % 2


def attn_fwd_kernel(meta, tok, wf0, wf1, attn0, attn1, qkv0, qkv1, xhat_out, lse0, lse1, wpad0, wpad1,
                    tok32, out32, bias):
    i = pl.program_id(0)
    rows, width = tok.shape
    cols = 3 * PAIR_PAD
    sides = ((wf0, qkv0, lse0, wpad0), (wf1, qkv1, lse1, wpad1))

    @pl.when(i == 0)
    def _():
        tok32[:rows] = tok[...].astype(F32)
        tok32[rows:] = jnp.zeros((tok32.shape[0] - rows, width), F32)
        vec = wf0[:, 3 * PAIR_DIM :].astype(F32).T
        bias[0:2, :width] = vec[0:2]
        for c in range(2):

            @pl.when(core_of(meta) == c)
            def _():
                for p in range(2):
                    at = (p ^ c) * PAIR_DIM
                    parts = [pad_heads(vec[r : r + 1, at : at + PAIR_DIM]) for r in (2, 3)]
                    bias[2 + p : 3 + p, :] = jnp.concatenate(
                        [parts[0], jnp.zeros((1, PAIR_PAD), F32), parts[1]], axis=1
                    )

        for wf, _, _, wpad in sides:
            wpad[...] = pad_heads(wf[:, : 3 * PAIR_DIM].astype(F32)).astype(BF16)

    start = meta[i]

    def work(length, padded):
        xhat, _ = row_norm(load_rows(tok32, start, padded))
        normed = (xhat * bias[0:1, :width] + bias[1:2, :width]).astype(BF16)
        xhat_out[0, :padded, :] = xhat.astype(BF16)
        for p, (_, qkv, lse, wpad) in enumerate(sides):
            qkv[0, :padded, :] = (dot_nn(normed, wpad[...]) + bias[2 + p : 3 + p, :]).astype(BF16)
        heads = [(p, h) for p in range(2) for h in range(PAIR)]
        scores = []
        for p, h in heads:
            qkv, at = sides[p][1], h * HEAD_PAD
            q = qkv[0, :padded, at : at + HEAD_PAD]
            k = qkv[0, :padded, PAIR_PAD + at : PAIR_PAD + at + HEAD_PAD]
            scores.append(dot_nt(k, q))
        probs = []
        for (p, h), s in zip(heads, scores):
            if length < padded:
                key = lax.broadcasted_iota(jnp.int32, s.shape, 0)
                s = jnp.where(key < length, s, -1e30)
            top = jnp.max(s, axis=0, keepdims=True)
            e = jnp.exp2((s - top) * EXP_SCALE)
            total = jnp.sum(e, axis=0, keepdims=True)
            probs.append((e * (1.0 / total)).astype(BF16))
            sides[p][2][0, h : h + 1, :padded] = top * EXP_SCALE + jnp.log2(total)
        outs = []
        for (p, h), prob in zip(heads, probs):
            at = 2 * PAIR_PAD + h * HEAD_PAD
            outs.append(dot_tn(prob, sides[p][1][0, :padded, at : at + HEAD_PAD]))
        store_rows(out32, start, length, jnp.concatenate(outs, axis=1), slice(None))

    by_group(meta[groups_at(meta) + i], work)

    @pl.when(i == pl.num_programs(0) - 1)
    def _():
        row = lax.broadcasted_iota(jnp.int32, (rows, 1), 0)
        mixed = jnp.where(row < rows_used(meta), out32[:rows], 0.0).astype(BF16)
        attn0[...] = mixed[:, :PAIR_PAD]
        attn1[...] = mixed[:, PAIR_PAD:]


def attn_fwd(meta, tokens, wf, waits, carry):
    rows, width = tokens.shape
    slots = groups_at(meta)
    cols = 3 * PAIR_PAD
    out_shape = [jax.ShapeDtypeStruct((rows, PAIR_PAD), BF16)] * 2
    out_shape += [jax.ShapeDtypeStruct((slots, SLOT, cols), BF16)] * 2
    out_shape += [jax.ShapeDtypeStruct((slots, SLOT, width), BF16)]
    out_shape += [jax.ShapeDtypeStruct((slots, 8, 512), F32)] * 2
    out_shape += [jax.ShapeDtypeStruct((width, cols), BF16)] * 2
    stats = pl.BlockSpec((1, 8, 512), lambda i, m: (i, 0, 0))
    out_specs = [whole(out_shape[0])] * 2 + [slot_block(cols)] * 2 + [slot_block(width)]
    out_specs += [stats] * 2 + [whole(out_shape[-1])] * 2
    scratch = [
        pltpu.VMEM((rows + ROW_PAD, width), F32),
        pltpu.VMEM((rows + ROW_PAD, 2 * PAIR_PAD), F32),
        pltpu.VMEM((8, cols), F32),
    ]
    in_specs = [whole(tokens), whole(wf[0]), whole(wf[1])]
    args = (meta, tokens, *wf)
    return call(attn_fwd_kernel, "attn_fwd", slots, in_specs, out_specs, out_shape, scratch, args, waits, carry)


def put_blocks(to, value, col, shards, parity=None):
    rows, cols = value.shape
    size = rows // shards
    half = rows // 2
    if size % 16:
        if parity is not None:
            value = value[parity * half : (parity + 1) * half]
        to[:, col : col + cols] = value
        return
    for n, place in enumerate(turned(shards)):
        at = place * size
        if parity is not None:
            if n % 2 != parity:
                continue
            at -= parity * half
        to[at : at + size, col : col + cols] = value[n * size : (n + 1) * size]


def mlp_kernel(meta, tok, cot, attn0, attn1, w0, w1, b0, b1, x1o, acto, dx1, da0, da1,
               keep_a, send_a, keep_b, send_b, wproj, rowvec, gd, gu, gp, gsum, *, shards):
    i = pl.program_id(0)
    rows, width = tok.shape
    parts = (w0, w1)
    lower = (b0, b1)

    def in_order(first, second, use):
        for c in range(2):
            pl.when(core_of(meta) == c)(partial(use, c, *((first, second) if c == 0 else (second, first))))

    @pl.when(i == 0)
    def _():
        def use(c, low, high):
            flat = [ref[x][:, width : width + VEC] for ref in (low, high) for x in range(2)]
            proj = jnp.concatenate(flat[: width // VEC], axis=1)
            wproj[...] = jnp.zeros(wproj.shape, BF16)
            for h in range(2 * PAIR):
                at = (h ^ (PAIR * c)) * HEAD_PAD
                wproj[at : at + HEAD_DIM] = proj[h * HEAD_DIM : (h + 1) * HEAD_DIM]
            vec = flat[-1].astype(F32).T
            for r in range(4):
                rowvec[r : r + 1, :width] = vec[r : r + 1]
                at = (r ^ (2 * c)) * width
                rowvec[4:5, at : at + width] = vec[4 + r : 5 + r]

        in_order(w0, w1, use)
        gd[...] = jnp.zeros(gd.shape, F32)
        gu[...] = jnp.zeros(gu.shape, F32)
        gp[...] = jnp.zeros(gp.shape, F32)
        gsum[...] = jnp.zeros(gsum.shape, F32)

    proj_bias, gain, shift, down_bias = [rowvec[r : r + 1, :width] for r in range(4)]
    row = lax.broadcasted_iota(jnp.int32, (rows, 1), 0) + i * rows
    valid = (row < rows_used(meta)).astype(F32)
    dy = cot[...].astype(F32) * valid
    dyb = dy.astype(BF16)
    chunk = 2 * width
    ups = [jnp.concatenate([parts[c][0][:, :width], parts[c][1][:, :width]], axis=1) for c in range(2)]
    downs = [jnp.concatenate([lower[c][x] for x in range(2)], axis=0) for c in range(2)]
    dacts = [dot_nt(dyb, downs[c]) for c in range(2)]
    mixed0, mixed1 = attn0[...], attn1[...]
    x1 = tok[...].astype(F32) + dot_nn(mixed0, wproj[:PAIR_PAD]) + dot_nn(mixed1, wproj[PAIR_PAD:])
    x1 = x1 + proj_bias
    x1o[...] = (x1 + down_bias) * valid
    xhat, inverse = row_norm(x1)
    normed = (xhat * gain + shift).astype(BF16)
    dn = jnp.zeros((rows, width), F32)
    kept = []
    for c in range(2):
        at = c * chunk
        pre = dot_nn(normed, ups[c]) + rowvec[4:5, at : at + chunk]
        act, slope = gelu_pair(pre)
        actb = act.astype(BF16)
        acto[:, at : at + chunk] = actb
        dpre = dacts[c] * slope
        dpreb = dpre.astype(BF16)
        gsum[4:5, at : at + chunk] += jnp.sum(dpre, axis=0, keepdims=True)
        dn = dn + dot_nt(dpreb, ups[c])
        kept.append(dpreb)
    for c in range(2):
        at = c * chunk
        gd[:, at : at + chunk] += dot_tn(dyb, acto[:, at : at + chunk])
        gu[:, at : at + chunk] += dot_tn(normed, kept[c])
    dx = dy + row_norm_back(dn * gain, xhat, inverse)
    dx1[...] = dx
    dxb = dx.astype(BF16)
    gp[:, :PAIR_PAD] += dot_tn(dxb, mixed0)
    gp[:, PAIR_PAD:] += dot_tn(dxb, mixed1)
    da0[...] = dot_nt(dxb, wproj[:PAIR_PAD]).astype(BF16)
    da1[...] = dot_nt(dxb, wproj[PAIR_PAD:]).astype(BF16)
    gsum[0:1, :width] += jnp.sum(dx, axis=0, keepdims=True)
    gsum[1:2, :width] += jnp.sum(dn * xhat, axis=0, keepdims=True)
    gsum[2:3, :width] += jnp.sum(dn, axis=0, keepdims=True)
    gsum[3:4, :width] += jnp.sum(dy, axis=0, keepdims=True)

    @pl.when(i == pl.num_programs(0) - 1)
    def _():
        for half, (to_a, to_b) in enumerate(((keep_a, keep_b), (send_a, send_b))):
            for x in range(2):
                at = (2 * half + x) * width
                put_blocks(to_a.at[x], gu[:, at : at + width].astype(BF16), 0, shards)
                part = gd[:, at : at + width].T.astype(BF16)
                for y in range(2):
                    put_blocks(to_b.at[y, x], part, 0, shards, y)

        def use(c, low, high):
            rows_of = [gsum[r : r + 1, :width] for r in range(4)]
            for r in range(4):
                at = (r ^ (2 * c)) * width
                rows_of.append(gsum[4:5, at : at + width])
            vec = jnp.concatenate(rows_of + [jnp.zeros((VEC - 8, width), F32)], axis=0).T
            grad = unpad_heads(gp[...]).T
            first, second = grad[:PAIR_DIM], grad[PAIR_DIM:]
            proj = jnp.concatenate([second, first] if c else [first, second], axis=0)
            flat = jnp.concatenate([proj, vec], axis=1).astype(BF16)
            for k in range(QUARTERS):
                to = (low, high)[k // 2].at[k % 2]
                put_blocks(to, flat[:, k * VEC : (k + 1) * VEC], width, shards)

        in_order(keep_a, send_a, use)


def mlp(meta, tokens, cotangent, attn, w, shards, block=512):
    rows, width = tokens.shape
    hidden = QUARTERS * width
    by_row = lambda cols: pl.BlockSpec((block, cols), lambda i, m: (i, 0))
    out_shape = [
        jax.ShapeDtypeStruct((rows, width), F32),
        jax.ShapeDtypeStruct((rows, hidden), BF16),
        jax.ShapeDtypeStruct((rows, width), F32),
        jax.ShapeDtypeStruct((rows, PAIR_PAD), BF16),
        jax.ShapeDtypeStruct((rows, PAIR_PAD), BF16),
    ]
    out_shape += [jax.ShapeDtypeStruct((2, width, width + VEC), BF16)] * 2
    out_shape += [jax.ShapeDtypeStruct((2, 2, width // 2, width), BF16)] * 2
    out_specs = [by_row(s.shape[1]) for s in out_shape[:5]] + [whole(s) for s in out_shape[5:]]
    in_specs = [by_row(width)] * 2 + [by_row(PAIR_PAD)] * 2 + [whole(t) for t in w]
    scratch = [
        pltpu.VMEM((2 * PAIR_PAD, width), BF16),
        pltpu.VMEM((8, hidden), F32),
        pltpu.VMEM((width, hidden), F32),
        pltpu.VMEM((width, hidden), F32),
        pltpu.VMEM((width, 2 * PAIR_PAD), F32),
        pltpu.VMEM((8, hidden), F32),
    ]
    args = (meta, tokens, cotangent, *attn, *w)
    kernel = partial(mlp_kernel, shards=shards)
    return call(kernel, "mlp", rows // block, in_specs, out_specs, out_shape, scratch, args)


def layer_out_kernel(meta, x1, act, b0, b1, out):
    rows, width = x1.shape
    row = lax.broadcasted_iota(jnp.int32, (rows, 1), 0) + pl.program_id(0) * rows
    valid = (row < rows_used(meta)).astype(F32)
    y = x1[...]
    for c, ref in enumerate((b0, b1)):
        down = jnp.concatenate([ref[x] for x in range(2)], axis=0)
        y = y + dot_nn(act[:, 2 * c * width : 2 * (c + 1) * width], down) * valid
    out[...] = y.astype(BF16)


def layer_output(meta, x1, act, w, waits, carry, block=512):
    rows, width = x1.shape
    by_row = lambda cols: pl.BlockSpec((block, cols), lambda i, m: (i, 0))
    return call(
        layer_out_kernel,
        "layer_out",
        rows // block,
        [by_row(width), by_row(act.shape[1]), whole(w[0]), whole(w[1])],
        [by_row(width)],
        [jax.ShapeDtypeStruct((rows, width), BF16)],
        [],
        (meta, x1, act, *w),
        waits,
        carry,
    )


def attn_bwd_kernel(meta, qkv, xhat, lse, dattn, wpad, wf, dqkv, grads, da32, gw, gsum, *, own, shards):
    i = pl.program_id(0)
    rows = dattn.shape[0]
    width = wf.shape[0]

    @pl.when(i == 0)
    def _():
        da32[:rows] = dattn[...].astype(F32)
        da32[rows:] = jnp.zeros((da32.shape[0] - rows, PAIR_PAD), F32)
        gw[...] = jnp.zeros(gw.shape, F32)
        gsum[...] = jnp.zeros(gsum.shape, F32)

    start = meta[i]

    def work(length, padded):
        da = load_rows(da32, start, padded)
        if length < padded:
            keep = lax.broadcasted_iota(jnp.int32, (padded, 1), 0) < length
            da = jnp.where(keep, da, 0.0)
        da = da.astype(BF16)
        def cut(ref, part, h):
            at = part * PAIR_PAD + h * HEAD_PAD
            return ref[0, :padded, at : at + HEAD_PAD]

        heads = range(PAIR)
        das = [da[:, h * HEAD_PAD : (h + 1) * HEAD_PAD] for h in heads]
        scores = [dot_nt(cut(qkv, 1, h), cut(qkv, 0, h)) for h in heads]
        dps = [dot_nt(cut(qkv, 2, h), das[h]) for h in heads]
        ps, dss = [], []
        for h in heads:
            p = jnp.exp2(scores[h] * EXP_SCALE - lse[0, h : h + 1, :padded])
            if length < padded:
                key = lax.broadcasted_iota(jnp.int32, p.shape, 0)
                p = jnp.where(key < length, p, 0.0)
            mean = jnp.sum(p * dps[h], axis=0, keepdims=True)
            dss.append((p * (dps[h] - mean)).astype(BF16))
            ps.append(p.astype(BF16))
        parts = [[dot_tn(dss[h], cut(qkv, 1, h)) * SCALE for h in heads]]
        parts += [[dot_nn(dss[h], cut(qkv, 0, h)) * SCALE for h in heads]]
        parts += [[dot_nn(ps[h], das[h]) for h in heads]]
        d = []
        for part in range(3):
            value = jnp.concatenate(parts[part], axis=1)
            at = part * PAIR_PAD
            if part != 1:
                gsum[0:1, at : at + PAIR_PAD] += jnp.sum(value, axis=0, keepdims=True)
            d.append(value.astype(BF16))
        d = jnp.concatenate(d, axis=1)
        dqkv[0, :padded, :] = d
        gw[...] += dot_tn(xhat[0, :padded, :], d)
        gsum[1:2, :] += jnp.sum(d.astype(F32), axis=0, keepdims=True)

    by_group(meta[groups_at(meta) + i], work)

    @pl.when(i == pl.num_programs(0) - 1)
    def _():
        w = wpad[...].astype(F32)
        raw = gw[...]
        col = gsum[1:2, :]
        gain_term = jnp.sum(raw * w, axis=1, keepdims=True)
        bias_term = jnp.sum(col * w, axis=1, keepdims=True)
        vec = wf[:, 3 * PAIR_DIM :].astype(F32)
        main = unpad_heads(raw * vec[:, 0:1] + vec[:, 1:2] * col).astype(BF16)
        put_blocks(grads, main, 0, shards)
        q_sum = unpad_heads(gsum[0:1, :PAIR_PAD])
        v_sum = unpad_heads(gsum[0:1, 2 * PAIR_PAD :])
        gap = jnp.zeros((1, width - PAIR_DIM), F32)
        for c in range(2):

            @pl.when(core_of(meta) == (c if own else 1 - c))
            def _():
                rows_of = [jnp.concatenate([gap, t] if c else [t, gap], axis=1) for t in (q_sum, v_sum)]
                rows_of = [jnp.zeros((2, width), F32)] + rows_of + [jnp.zeros((VEC - 4, width), F32)]
                sums = jnp.concatenate(rows_of, axis=0).T
                lane = lax.broadcasted_iota(jnp.int32, sums.shape, 1)
                tail = jnp.where(lane == 0, gain_term, jnp.where(lane == 1, bias_term, sums))
                put_blocks(grads, tail[:, :VEC_PAIR].astype(BF16), 3 * PAIR_DIM, shards)


def attn_bwd(meta, qkv, xhat, lse, dattn, wpad, wf, own, shards, waits, carry):
    rows = dattn.shape[0]
    width = wf.shape[0]
    cols = 3 * PAIR_PAD
    out_shape = [jax.ShapeDtypeStruct(qkv.shape, BF16), jax.ShapeDtypeStruct(wf.shape, BF16)]
    in_specs = [slot_block(cols), slot_block(width), pl.BlockSpec((1, 8, 512), lambda i, m: (i, 0, 0))]
    in_specs += [whole(dattn), whole(wpad), whole(wf)]
    scratch = [
        pltpu.VMEM((rows + ROW_PAD, PAIR_PAD), F32),
        pltpu.VMEM((width, cols), F32),
        pltpu.VMEM((8, cols), F32),
    ]
    args = (meta, qkv, xhat, lse, dattn, wpad, wf)
    kernel = partial(attn_bwd_kernel, own=own, shards=shards)
    out_specs = [slot_block(cols), whole(wf)]
    grid = groups_at(meta)
    return call(kernel, "attn_bwd", grid, in_specs, out_specs, out_shape, scratch, args, waits, carry)


def input_grad_kernel(meta, tok, d0, d1, w0, w1, wf, dx1, out, tok32, bias):
    i = pl.program_id(0)
    rows, width = tok.shape

    @pl.when(i == 0)
    def _():
        tok32[:rows] = tok[...].astype(F32)
        tok32[rows:] = jnp.zeros((tok32.shape[0] - rows, width), F32)
        bias[...] = wf[:, 3 * PAIR_DIM :].astype(F32).T[0:8]

    start = meta[i]

    def work(length, padded):
        dn = dot_nt(d0[0, :padded, :], w0[...]) + dot_nt(d1[0, :padded, :], w1[...])
        xhat, inverse = row_norm(load_rows(tok32, start, padded))
        dx = row_norm_back(dn * bias[0:1, :], xhat, inverse)
        store_rows(tok32, start, length, dx, slice(None))

    by_group(meta[groups_at(meta) + i], work)

    @pl.when(i == pl.num_programs(0) - 1)
    def _():
        row = lax.broadcasted_iota(jnp.int32, (rows, 1), 0)
        total = dx1[...] + tok32[:rows]
        out[...] = jnp.where(row < rows_used(meta), total, 0.0).astype(BF16)


def input_grad(meta, tokens, d, w, wf, dx1, waits, carry):
    rows, width = tokens.shape
    slot = slot_block(d[0].shape[2])
    in_specs = [whole(tokens), slot, slot] + [whole(t) for t in (*w, wf, dx1)]
    scratch = [pltpu.VMEM((rows + ROW_PAD, width), F32), pltpu.VMEM((8, width), F32)]
    out_shape = [jax.ShapeDtypeStruct((rows, width), BF16)]
    args = (meta, tokens, *d, *w, wf, dx1)
    grid, out_specs = groups_at(meta), [whole(tokens)]
    return call(
        input_grad_kernel, "input_grad", grid, in_specs, out_specs, out_shape, scratch, args, waits, carry
    )


def final_parts(core, own, got, shards):
    size = own.shape[0]
    width = shards * size
    cut = 3 * PAIR_DIM + VEC_PAIR
    low, high = (got, own) if core else (own, got)
    qkv = [t[:, part * PAIR_DIM : (part + 1) * PAIR_DIM] for part in range(3) for t in (low, high)]
    step = (low.shape[1] - cut) // 2
    quarters = [t[:, cut + x * step : cut + (x + 1) * step] for t in (low, high) for x in range(2)]
    extra_at, down_at = width, width + VEC
    extra = [q[:, extra_at:down_at] for q in quarters]
    up = [q[:, n * size : (n + 1) * size] for n in range(shards) for q in quarters]
    down = jnp.concatenate([q[:, down_at:] for q in quarters], axis=0)
    ends = low[:, 3 * PAIR_DIM : cut] + high[:, 3 * PAIR_DIM : cut]
    columns = jnp.concatenate([ends[:, :4], extra[-1][:, : 4 + QUARTERS]], axis=1)
    cat = lambda parts: jnp.concatenate(parts, axis=1)
    return cat(qkv), cat(extra[: width // VEC]), cat(up), down, columns


def finish_kernel(meta, own, got, *outs, shards):
    size = own.shape[0]

    def use(core):
        *mats, columns = final_parts(core, own[...].astype(F32), got[...].astype(F32), shards)
        for mat, out in zip(mats, outs):
            tiles = mat.shape[1] // 128
            for t in range(tiles):
                out[pl.ds(t, mat.shape[0], stride=tiles), :] = mat[:, t * 128 : (t + 1) * 128]
        count = columns.shape[1]
        square = jnp.concatenate([columns, jnp.zeros((size, 128 - count), F32)], axis=1)
        square = jnp.concatenate([square, jnp.zeros((128 - size, 128), F32)], axis=0)
        rows = square.T[:16]
        flat = jnp.concatenate([rows[r : r + 1, :size] for r in range(8, 8 + QUARTERS)], axis=1)
        outs[4][...] = rows
        for n, at in enumerate(range(0, flat.shape[1], 128)):
            piece = flat[:, at : at + 128]
            outs[4][8 + n : 9 + n, : piece.shape[1]] = piece

    for c in range(2):
        pl.when(core_of(meta) == c)(partial(use, c))


def finish(meta, own, got, shards):
    size = own.shape[0]
    width = shards * size
    if size % 16:
        core = core_of(meta) == 1
        own, got = own.astype(F32), got.astype(F32)
        parts = final_parts(0, jnp.where(core, got, own), jnp.where(core, own, got), shards)
        rows = parts[4].T
        return [p.reshape(-1) for p in parts[:4]], rows, rows[8 : 8 + QUARTERS].reshape(-1)
    sizes = [size * 3 * width, size * width, size * QUARTERS * width, size * QUARTERS * width]
    out_shape = [jax.ShapeDtypeStruct((n // 128, 128), F32) for n in sizes + [16 * 128]]
    out_specs = [whole(t) for t in out_shape]
    kernel = partial(finish_kernel, shards=shards)
    outs = call(kernel, "finish", 1, [whole(own), whole(got)], out_specs, out_shape, [], (meta, own, got))
    count = QUARTERS * size
    pieces = [outs[4][8 + n, : min(128, count - at)] for n, at in enumerate(range(0, count, 128))]
    return [t.reshape(-1) for t in outs[:4]], outs[4], jnp.concatenate(pieces)


def turned(shards):
    count = shards.bit_length() - 1
    return [sum(((n >> b) & 1) << (count - 1 - b) for b in range(count)) for n in range(shards)]


def image_table(size_group, assignment, device, slots):
    owned = assignment == device
    rank = jnp.cumsum(owned.astype(jnp.int32)) - 1
    slot = jnp.arange(slots, dtype=jnp.int32)
    here = owned[None, :] & (rank[None, :] == slot[:, None])
    groups = jnp.sum(jnp.where(here, size_group[None, :], 0), axis=1)
    lengths = jnp.where(groups == 0, LENS[0], jnp.where(groups == 1, LENS[1], LENS[2]))
    ends = jnp.sum(jnp.where(slot[None, :] <= slot[:, None], lengths[None, :], 0), axis=1)
    return jnp.concatenate([ends - lengths, groups, ends[-1:], device[None]]).astype(jnp.int32)


def swap(value, axis, bit):
    size = lax.axis_size(axis)
    return lax.ppermute(value, axis, [(i, i ^ bit) for i in range(size)])


def sides_of(bits):
    table = {}
    for axis, those in bits.items():
        for bit in those:
            mine = (lax.axis_index(axis) & bit) // bit
            table[axis, bit] = (mine.astype(jnp.uint32), (1 - mine).astype(jnp.uint32), mine == 1)
    return table


def pick(sides, value, axis, bit, dim):
    mine, theirs, _ = sides[axis, bit]
    keep = lax.dynamic_index_in_dim(value, mine, dim, keepdims=False)
    send = lax.dynamic_index_in_dim(value, theirs, dim, keepdims=False)
    return keep, send


def join(upper, own, other, dim):
    return jnp.stack([jnp.where(upper, other, own), jnp.where(upper, own, other)], axis=dim)


def added(keep, got):
    return (keep.astype(F32) + got.astype(F32)).astype(BF16)


def after(value, *others):
    return lax.optimization_barrier((value, *others))[0]


class Gather:
    def __init__(self, sides, part, keys):
        self.sides, self.part, self.keys, self.have = sides, part, keys, []

    def grow(self, axis, bit, *others, upper=None):
        if others:
            self.part = after(self.part, *others)
        upper = self.sides[axis, bit][2] if upper is None else upper
        dim = sum(self.keys.index(k) < self.keys.index((axis, bit)) for k in self.have)
        self.part = join(upper, self.part, swap(self.part, axis, bit), dim)
        self.have.append((axis, bit))
        return self


def body(
    tokens,
    cotangent,
    size_group,
    assignment,
    ln1_gain,
    ln1_bias,
    w_qkv,
    q_bias,
    v_bias,
    w_proj,
    proj_bias,
    ln2_gain,
    ln2_bias,
    w_up,
    up_bias,
    w_down,
    down_bias,
):
    rows, width = tokens.shape
    shards = lax.axis_size("fsdp")
    size = width // shards
    devices = shards * lax.axis_size("dp")
    device = lax.axis_index("fsdp") * lax.axis_size("dp") + lax.axis_index("dp")
    bits = [1 << b for b in range(shards.bit_length() - 1)]
    far, near, y = bits[2:], bits[1:2], bits[0]
    tail_keys = [("fsdp", b) for b in reversed(bits)]
    sides = sides_of({"dp": (1, 2), "fsdp": bits})
    core, column = sides["dp", 1][0], sides["dp", 2][0]

    vectors = [ln1_gain, ln1_bias, q_bias, v_bias, proj_bias, ln2_gain, ln2_bias, down_bias]
    vectors = jnp.concatenate([jnp.stack(vectors), up_bias.reshape(QUARTERS, size)]).T
    pair = w_qkv.reshape(size, 3, 2, PAIR_DIM)
    pair = lax.dynamic_index_in_dim(pair, core, 2, keepdims=False).reshape(size, 3 * PAIR_DIM)
    pair = jnp.concatenate([pair, vectors[:, :4], jnp.zeros((size, VEC_PAIR - 4), BF16)], axis=1)
    f = Gather(sides, pair, tail_keys)
    w_up, w_down, w_proj, _ = lax.optimization_barrier((w_up, w_down, w_proj, pair))
    quarter = 2 * core + column
    extra = [w_proj.reshape(size, width), vectors[:, 4:], jnp.zeros((size, VEC - 4 - QUARTERS), BF16)]
    extra = lax.dynamic_slice_in_dim(jnp.concatenate(extra, axis=1), quarter * VEC, VEC, 1)
    up = lax.dynamic_index_in_dim(w_up.reshape(size, shards, QUARTERS, size), quarter, 2, False)
    part_a = jnp.concatenate([up.reshape(size, width), extra], axis=1)
    part_b = lax.dynamic_index_in_dim(w_down.reshape(QUARTERS, size, width), quarter, 0, False)
    ab = Gather(sides, jnp.concatenate([part_a, part_b], axis=1), tail_keys)

    for bit in far:
        f.grow("fsdp", bit)
    for bit in far:
        ab.grow("fsdp", bit)
    for bit in near:
        f.grow("fsdp", bit)
    for bit in near:
        ab.grow("fsdp", bit)
    size_group, assignment, _ = lax.optimization_barrier((size_group, assignment, f.part))
    table = image_table(size_group, assignment, device, size_group.shape[0] // devices)
    f.grow("fsdp", y)
    own = f.part.reshape(width, -1)
    cut = width + VEC
    keys = [("dp", 2)] + tail_keys
    a, b = Gather(sides, ab.part[..., :cut], keys), Gather(sides, ab.part[..., cut:], keys)
    a.have, b.have = list(ab.have), list(ab.have)
    a.grow("dp", 2)
    b.grow("fsdp", y)
    wf = (own, swap(own, "dp", 1))

    upper = jnp.stack([sides["fsdp", y][2], sides["dp", 2][2]])
    upper = jnp.broadcast_to(upper[:, None, None], (2, 8, cut)).astype(jnp.int32)
    table, sides, upper = lax.optimization_barrier((table, sides, upper))
    attn0, attn1, qkv0, qkv1, xhat, lse0, lse1, wpad0, wpad1, upper = attn_fwd(
        table, tokens, wf, (), (upper,)
    )
    a.grow("fsdp", y, upper=upper[0, 0] != 0)
    b.grow("dp", 2, upper=upper[1, 0, :width] != 0)
    wa, wb = a.part.reshape(2, width, cut), b.part.reshape(2, width, width)
    w = (wa, swap(wa, "dp", 1), wb, swap(wb, "dp", 1))
    x1, act, dx1, dattn0, dattn1, keep_a, send_a, keep_b, send_b = mlp(
        table, tokens, cotangent, (attn0, attn1), w, shards
    )

    def by_bits(value, lead):
        if size % 16:
            value = value.reshape(value.shape[:lead] + (2,) * len(bits) + (size, value.shape[-1]))
            order = [lead + b for b in reversed(range(len(bits)))]
            return value.transpose(*range(lead), *order, *range(lead + len(bits), value.ndim))
        return value.reshape(value.shape[:lead] + (2,) * len(bits) + (size, value.shape[-1]))

    def halves_of_b(value):
        if size % 16:
            value = value.swapaxes(0, 1).reshape(2, width, width)
            return by_bits(value, 1).swapaxes(0, 1)
        return value.reshape((2, 2) + (2,) * (len(bits) - 1) + (size, width))

    got_a, got_b = swap(send_a, "dp", 1), swap(send_b, "dp", 1)
    d1, send_g, keep_a, keep_b = attn_bwd(
        table, qkv1, xhat, lse1, dattn1, wpad1, wf[1], False, shards, (send_a, send_b), (keep_a, keep_b)
    )
    got_g = swap(send_g, "dp", 1)
    keep_a, send_a = pick(sides, by_bits(added(keep_a, got_a), 1), "dp", 2, 0)
    keep_b, send_b = pick(sides, halves_of_b(added(keep_b, got_b)), "fsdp", y, 0)
    got_a, got_b = swap(send_a, "dp", 2), swap(send_b, "fsdp", y)
    d0, keep_g, keep_a, keep_b = attn_bwd(
        table, qkv0, xhat, lse0, dattn0, wpad0, wf[0], True, shards, (send_a, send_b, send_g), (keep_a, keep_b)
    )
    part = jnp.concatenate([by_bits(added(keep_g, got_g), 0), added(keep_a, got_a)], axis=-1)
    keep, send = pick(sides, part, "fsdp", y, 0)
    keep_b, send_b = pick(sides, added(keep_b, got_b), "dp", 2, 0)
    got, got_b = swap(send, "fsdp", y), swap(send_b, "dp", 2)
    grads_of = (table, tokens, (d0, d1), (wpad0, wpad1), wf[0], dx1)
    grad_input, keep, keep_b = input_grad(*grads_of, (send, send_b), (keep, keep_b))
    part = jnp.concatenate([added(keep, got), added(keep_b, got_b)], axis=-1)
    for count, bit in enumerate(bits[1:]):
        keep, send = pick(sides, part, "fsdp", bit, 0)
        got = swap(send, "fsdp", bit)
        if count == 0:
            layer_out, keep = layer_output(table, x1, act, w[2:], (send,), (keep,))
        part = added(keep, got)
    got = swap(part, "dp", 2)
    cut = keep_g.shape[-1]
    part_g = added(part[:, :cut], got[:, :cut])
    low, high = part[:, cut:], got[:, cut:]
    upper = sides["dp", 2][2]
    part = [part_g, jnp.where(upper, high, low), jnp.where(upper, low, high)]
    part = jnp.concatenate(part, axis=1)
    flat, vectors, up_bias = finish(table, part, swap(part, "dp", 1), shards)
    g = [vectors[r, :size] for r in range(8)] + [up_bias]
    qkv, proj, up, down = flat
    return (
        layer_out, grad_input, g[0], g[1], qkv, g[2], g[3], proj, g[4], g[5], g[6], up, g[8], down, g[7]
    )


def solution(mesh):
    rows = P(("fsdp", "dp"), None)
    flat = P("fsdp")
    return jax.shard_map(
        body,
        mesh=mesh,
        in_specs=(rows, rows, P(), P()) + (flat,) * 13,
        out_specs=(rows, rows) + (flat,) * 13,
        check_vma=False,
    )
```

```python
from functools import partial
import math

import jax
import jax.numpy as jnp
from jax import lax
from jax.experimental import pallas as pl
from jax.experimental.pallas import tpu as pltpu
from jax.sharding import PartitionSpec as P

HEAD_DIM = 96
HEAD_PAD = 128
LENS = (196, 256, 400)
SLOT = 400
ROW_PAD = 32
PAIR = 2
PAIR_DIM = PAIR * HEAD_DIM
PAIR_PAD = PAIR * HEAD_PAD
QUARTERS = 4
VEC = 128
VEC_PAIR = 64
SCALE = 1.0 / math.sqrt(HEAD_DIM)
EXP_SCALE = SCALE * math.log2(math.e)
MIB = 1024 * 1024
VMEM = {"attn_fwd": 12, "mlp": 21, "attn_bwd": 8, "layer_out": 8, "input_grad": 10, "finish": 10}
F32 = jnp.float32
BF16 = jnp.bfloat16


def dot_nn(a, b):
    return lax.dot_general(a, b, (((1,), (0,)), ((), ())), preferred_element_type=F32)


def dot_nt(a, b):
    return lax.dot_general(a, b, (((1,), (1,)), ((), ())), preferred_element_type=F32)


def dot_tn(a, b):
    return lax.dot_general(a, b, (((0,), (0,)), ((), ())), preferred_element_type=F32)


def pad_heads(values):
    rows, cols = values.shape
    gap = jnp.zeros((rows, HEAD_PAD - HEAD_DIM), values.dtype)
    parts = []
    for h in range(cols // HEAD_DIM):
        parts += [values[:, h * HEAD_DIM : (h + 1) * HEAD_DIM], gap]
    return jnp.concatenate(parts, axis=1)


def unpad_heads(values):
    rows, cols = values.shape
    return jnp.concatenate(
        [values[:, h * HEAD_PAD : h * HEAD_PAD + HEAD_DIM] for h in range(cols // HEAD_PAD)], axis=1
    )


def row_norm(x):
    center = x - jnp.mean(x, axis=-1, keepdims=True)
    inverse = lax.rsqrt(jnp.mean(center * center, axis=-1, keepdims=True) + 1e-6)
    return center * inverse, inverse


def row_norm_back(e, xhat, inverse):
    return inverse * (
        e - jnp.mean(e, axis=-1, keepdims=True) - xhat * jnp.mean(e * xhat, axis=-1, keepdims=True)
    )


def load_rows(ref, start, count):
    base = pl.multiple_of((start // 8) * 8, 8)
    window = ref[pl.ds(base, count + 8), :]
    moved = pltpu.roll(window, count + 4, 0)
    return jnp.where(start % 8 == 0, window, moved)[:count]


def store_rows(ref, start, length, values, cols):
    count = -(-length // 8) * 8
    base = pl.multiple_of((start // 8) * 8, 8)
    window = jnp.concatenate([values[:count], jnp.zeros((8, values.shape[1]), values.dtype)], axis=0)
    window = jnp.where(start % 8 == 0, window, pltpu.roll(window, 4, 0))
    row = lax.broadcasted_iota(jnp.int32, window.shape, 0) - start % 8
    held = ref[pl.ds(base, count + 8), cols]
    ref[pl.ds(base, count + 8), cols] = jnp.where((row >= 0) & (row < length), window, held)


def by_group(group, work):
    for g, length in enumerate(LENS):
        pl.when(group == g)(partial(work, length, -(-length // 16) * 16))


def gelu_pair(u):
    cdf = 0.5 + 0.5 * lax.erf(u * (1.0 / math.sqrt(2.0)))
    bell = jnp.exp2((u * u) * (-0.5 * math.log2(math.e)))
    return u * cdf, cdf + u * (bell * (1.0 / math.sqrt(2.0 * math.pi)))


def whole(array):
    at = (0,) * len(array.shape)
    return pl.BlockSpec(array.shape, lambda i, m: at, pipeline_mode=pl.Buffered(1))


def slot_block(cols):
    return pl.BlockSpec((1, SLOT, cols), lambda i, m: (i, 0, 0))


def call(kernel, name, grid, in_specs, out_specs, out_shape, scratch, args, waits=(), carry=(), far=()):
    given, made, passed = len(in_specs) + 1, len(out_shape), len(waits) + len(carry)

    def ordered(*refs):
        kernel(*refs[:given], *refs[given + passed : given + passed + made], *refs[given + passed + made + len(carry) :])

    args = [
        pltpu.with_memory_space_constraint(t, pltpu.HBM) if at in far else t for at, t in enumerate(args)
    ]
    anywhere = pl.BlockSpec(memory_space=pl.ANY)
    outs = pl.pallas_call(
        ordered,
        grid_spec=pltpu.PrefetchScalarGridSpec(
            num_scalar_prefetch=1,
            grid=(grid,),
            in_specs=list(in_specs) + [anywhere] * passed,
            out_specs=list(out_specs) + [anywhere] * len(carry),
            scratch_shapes=scratch,
        ),
        out_shape=list(out_shape) + [jax.ShapeDtypeStruct(t.shape, t.dtype) for t in carry],
        input_output_aliases={given + len(waits) + n: made + n for n in range(len(carry))},
        compiler_params=pltpu.CompilerParams(vmem_limit_bytes=VMEM[name] * MIB),
        name=name,
    )(*args, *waits, *carry)
    return outs


def groups_at(meta):
    return (meta.shape[0] - 2) // 2


def rows_used(meta):
    return meta[meta.shape[0] - 2]


def device_of(meta):
    return meta[meta.shape[0] - 1]


def core_of(meta):
    return device_of(meta) % 2


def attn_fwd_kernel(meta, tok, wf0, wf1, attn0, attn1, qkv0, qkv1, xhat_out, lse0, lse1, wpad0, wpad1,
                    tok32, out32, bias):
    i = pl.program_id(0)
    rows, width = tok.shape
    cols = 3 * PAIR_PAD
    sides = ((wf0, qkv0, lse0, wpad0), (wf1, qkv1, lse1, wpad1))

    @pl.when(i == 0)
    def _():
        tok32[:rows] = tok[...].astype(F32)
        tok32[rows:] = jnp.zeros((tok32.shape[0] - rows, width), F32)
        vec = wf0[:, 3 * PAIR_DIM :].astype(F32).T
        bias[0:2, :width] = vec[0:2]
        for c in range(2):

            @pl.when(core_of(meta) == c)
            def _():
                for p in range(2):
                    at = (p ^ c) * PAIR_DIM
                    parts = [pad_heads(vec[r : r + 1, at : at + PAIR_DIM]) for r in (2, 3)]
                    bias[2 + p : 3 + p, :] = jnp.concatenate(
                        [parts[0], jnp.zeros((1, PAIR_PAD), F32), parts[1]], axis=1
                    )

        for wf, _, _, wpad in sides:
            wpad[...] = pad_heads(wf[:, : 3 * PAIR_DIM].astype(F32)).astype(BF16)

    start = meta[i]

    def work(length, padded):
        xhat, _ = row_norm(load_rows(tok32, start, padded))
        normed = (xhat * bias[0:1, :width] + bias[1:2, :width]).astype(BF16)
        xhat_out[0, :padded, :] = xhat.astype(BF16)
        for p, (_, qkv, lse, wpad) in enumerate(sides):
            qkv[0, :padded, :] = (dot_nn(normed, wpad[...]) + bias[2 + p : 3 + p, :]).astype(BF16)
        heads = [(p, h) for p in range(2) for h in range(PAIR)]
        scores = []
        for p, h in heads:
            qkv, at = sides[p][1], h * HEAD_PAD
            q = qkv[0, :padded, at : at + HEAD_PAD]
            k = qkv[0, :padded, PAIR_PAD + at : PAIR_PAD + at + HEAD_PAD]
            scores.append(dot_nt(k, q))
        probs = []
        for (p, h), s in zip(heads, scores):
            if length < padded:
                key = lax.broadcasted_iota(jnp.int32, s.shape, 0)
                s = jnp.where(key < length, s, -1e30)
            top = jnp.max(s, axis=0, keepdims=True)
            e = jnp.exp2((s - top) * EXP_SCALE)
            total = jnp.sum(e, axis=0, keepdims=True)
            probs.append((e * (1.0 / total)).astype(BF16))
            sides[p][2][0, h : h + 1, :padded] = top * EXP_SCALE + jnp.log2(total)
        outs = []
        for (p, h), prob in zip(heads, probs):
            at = 2 * PAIR_PAD + h * HEAD_PAD
            outs.append(dot_tn(prob, sides[p][1][0, :padded, at : at + HEAD_PAD]))
        store_rows(out32, start, length, jnp.concatenate(outs, axis=1), slice(None))

    by_group(meta[groups_at(meta) + i], work)

    @pl.when(i == pl.num_programs(0) - 1)
    def _():
        row = lax.broadcasted_iota(jnp.int32, (rows, 1), 0)
        mixed = jnp.where(row < rows_used(meta), out32[:rows], 0.0).astype(BF16)
        attn0[...] = mixed[:, :PAIR_PAD]
        attn1[...] = mixed[:, PAIR_PAD:]


def attn_fwd(meta, tokens, wf, waits, carry):
    rows, width = tokens.shape
    slots = groups_at(meta)
    cols = 3 * PAIR_PAD
    out_shape = [jax.ShapeDtypeStruct((rows, PAIR_PAD), BF16)] * 2
    out_shape += [jax.ShapeDtypeStruct((slots, SLOT, cols), BF16)] * 2
    out_shape += [jax.ShapeDtypeStruct((slots, SLOT, width), BF16)]
    out_shape += [jax.ShapeDtypeStruct((slots, 8, 512), F32)] * 2
    out_shape += [jax.ShapeDtypeStruct((width, cols), BF16)] * 2
    stats = pl.BlockSpec((1, 8, 512), lambda i, m: (i, 0, 0))
    out_specs = [whole(out_shape[0])] * 2 + [slot_block(cols)] * 2 + [slot_block(width)]
    out_specs += [stats] * 2 + [whole(out_shape[-1])] * 2
    scratch = [
        pltpu.VMEM((rows + ROW_PAD, width), F32),
        pltpu.VMEM((rows + ROW_PAD, 2 * PAIR_PAD), F32),
        pltpu.VMEM((8, cols), F32),
    ]
    in_specs = [whole(tokens), whole(wf[0]), whole(wf[1])]
    args = (meta, tokens, *wf)
    return call(attn_fwd_kernel, "attn_fwd", slots, in_specs, out_specs, out_shape, scratch, args, waits, carry)


def put_blocks(to, value, col, shards, parity=None):
    rows, cols = value.shape
    size = rows // shards
    half = rows // 2
    if size % 16:
        if parity is not None:
            value = value[parity * half : (parity + 1) * half]
        to[:, col : col + cols] = value
        return
    for n, place in enumerate(turned(shards)):
        at = place * size
        if parity is not None:
            if n % 2 != parity:
                continue
            at -= parity * half
        to[at : at + size, col : col + cols] = value[n * size : (n + 1) * size]


def mlp_kernel(meta, tok, cot, attn0, attn1, w0, w1, b0, b1, x1o, acto, dx1, da0, da1,
               keep_a, send_a, keep_b, send_b, wproj, rowvec, gd, gu, gp, gsum, *, shards):
    i = pl.program_id(0)
    rows, width = tok.shape
    parts = (w0, w1)
    lower = (b0, b1)

    def in_order(first, second, use):
        for c in range(2):
            pl.when(core_of(meta) == c)(partial(use, c, *((first, second) if c == 0 else (second, first))))

    @pl.when(i == 0)
    def _():
        def use(c, low, high):
            flat = [ref[x][:, width : width + VEC] for ref in (low, high) for x in range(2)]
            proj = jnp.concatenate(flat[: width // VEC], axis=1)
            wproj[...] = jnp.zeros(wproj.shape, BF16)
            for h in range(2 * PAIR):
                at = (h ^ (PAIR * c)) * HEAD_PAD
                wproj[at : at + HEAD_DIM] = proj[h * HEAD_DIM : (h + 1) * HEAD_DIM]
            vec = flat[-1].astype(F32).T
            for r in range(4):
                rowvec[r : r + 1, :width] = vec[r : r + 1]
                at = (r ^ (2 * c)) * width
                rowvec[4:5, at : at + width] = vec[4 + r : 5 + r]

        in_order(w0, w1, use)
        gd[...] = jnp.zeros(gd.shape, F32)
        gu[...] = jnp.zeros(gu.shape, F32)
        gp[...] = jnp.zeros(gp.shape, F32)
        gsum[...] = jnp.zeros(gsum.shape, F32)

    proj_bias, gain, shift, down_bias = [rowvec[r : r + 1, :width] for r in range(4)]
    row = lax.broadcasted_iota(jnp.int32, (rows, 1), 0) + i * rows
    valid = (row < rows_used(meta)).astype(F32)
    dy = cot[...].astype(F32) * valid
    dyb = dy.astype(BF16)
    chunk = 2 * width
    ups = [jnp.concatenate([parts[c][0][:, :width], parts[c][1][:, :width]], axis=1) for c in range(2)]
    downs = [jnp.concatenate([lower[c][x] for x in range(2)], axis=0) for c in range(2)]
    dacts = [dot_nt(dyb, downs[c]) for c in range(2)]
    mixed0, mixed1 = attn0[...], attn1[...]
    x1 = tok[...].astype(F32) + dot_nn(mixed0, wproj[:PAIR_PAD]) + dot_nn(mixed1, wproj[PAIR_PAD:])
    x1 = x1 + proj_bias
    x1o[...] = (x1 + down_bias) * valid
    xhat, inverse = row_norm(x1)
    normed = (xhat * gain + shift).astype(BF16)
    dn = jnp.zeros((rows, width), F32)
    kept = []
    for c in range(2):
        at = c * chunk
        pre = dot_nn(normed, ups[c]) + rowvec[4:5, at : at + chunk]
        act, slope = gelu_pair(pre)
        actb = act.astype(BF16)
        acto[:, at : at + chunk] = actb
        dpre = dacts[c] * slope
        dpreb = dpre.astype(BF16)
        gsum[4:5, at : at + chunk] += jnp.sum(dpre, axis=0, keepdims=True)
        dn = dn + dot_nt(dpreb, ups[c])
        kept.append(dpreb)
    for c in range(2):
        at = c * chunk
        gd[:, at : at + chunk] += dot_tn(dyb, acto[:, at : at + chunk])
        gu[:, at : at + chunk] += dot_tn(normed, kept[c])
    dx = dy + row_norm_back(dn * gain, xhat, inverse)
    dx1[...] = dx
    dxb = dx.astype(BF16)
    gp[:, :PAIR_PAD] += dot_tn(dxb, mixed0)
    gp[:, PAIR_PAD:] += dot_tn(dxb, mixed1)
    da0[...] = dot_nt(dxb, wproj[:PAIR_PAD]).astype(BF16)
    da1[...] = dot_nt(dxb, wproj[PAIR_PAD:]).astype(BF16)
    gsum[0:1, :width] += jnp.sum(dx, axis=0, keepdims=True)
    gsum[1:2, :width] += jnp.sum(dn * xhat, axis=0, keepdims=True)
    gsum[2:3, :width] += jnp.sum(dn, axis=0, keepdims=True)
    gsum[3:4, :width] += jnp.sum(dy, axis=0, keepdims=True)

    @pl.when(i == pl.num_programs(0) - 1)
    def _():
        for half, (to_a, to_b) in enumerate(((keep_a, keep_b), (send_a, send_b))):
            for x in range(2):
                at = (2 * half + x) * width
                put_blocks(to_a.at[x], gu[:, at : at + width].astype(BF16), 0, shards)
                part = gd[:, at : at + width].astype(BF16).T
                for y in range(2):
                    put_blocks(to_b.at[y, x], part, 0, shards, y)

        def use(c, low, high):
            rows_of = [gsum[r : r + 1, :width] for r in range(4)]
            for r in range(4):
                at = (r ^ (2 * c)) * width
                rows_of.append(gsum[4:5, at : at + width])
            vec = jnp.concatenate(rows_of + [jnp.zeros((VEC - 8, width), F32)], axis=0).T
            grad = unpad_heads(gp[...].astype(BF16)).T
            first, second = grad[:PAIR_DIM], grad[PAIR_DIM:]
            proj = jnp.concatenate([second, first] if c else [first, second], axis=0)
            flat = jnp.concatenate([proj, vec.astype(BF16)], axis=1)
            for k in range(QUARTERS):
                to = (low, high)[k // 2].at[k % 2]
                put_blocks(to, flat[:, k * VEC : (k + 1) * VEC], width, shards)

        in_order(keep_a, send_a, use)


def mlp(meta, tokens, cotangent, attn, w, shards, block=512):
    rows, width = tokens.shape
    hidden = QUARTERS * width
    by_row = lambda cols: pl.BlockSpec((block, cols), lambda i, m: (i, 0))
    out_shape = [
        jax.ShapeDtypeStruct((rows, width), F32),
        jax.ShapeDtypeStruct((rows, hidden), BF16),
        jax.ShapeDtypeStruct((rows, width), F32),
        jax.ShapeDtypeStruct((rows, PAIR_PAD), BF16),
        jax.ShapeDtypeStruct((rows, PAIR_PAD), BF16),
    ]
    out_shape += [jax.ShapeDtypeStruct((2, width, width + VEC), BF16)] * 2
    out_shape += [jax.ShapeDtypeStruct((2, 2, width // 2, width), BF16)] * 2
    out_specs = [by_row(s.shape[1]) for s in out_shape[:5]] + [whole(s) for s in out_shape[5:]]
    in_specs = [by_row(width)] * 2 + [by_row(PAIR_PAD)] * 2 + [whole(t) for t in w]
    scratch = [
        pltpu.VMEM((2 * PAIR_PAD, width), BF16),
        pltpu.VMEM((8, hidden), F32),
        pltpu.VMEM((width, hidden), F32),
        pltpu.VMEM((width, hidden), F32),
        pltpu.VMEM((width, 2 * PAIR_PAD), F32),
        pltpu.VMEM((8, hidden), F32),
    ]
    args = (meta, tokens, cotangent, *attn, *w)
    kernel = partial(mlp_kernel, shards=shards)
    return call(kernel, "mlp", rows // block, in_specs, out_specs, out_shape, scratch, args)


def layer_out_kernel(meta, x1, act, b0, b1, out):
    rows, width = x1.shape
    row = lax.broadcasted_iota(jnp.int32, (rows, 1), 0) + pl.program_id(0) * rows
    valid = (row < rows_used(meta)).astype(F32)
    y = x1[...]
    for c, ref in enumerate((b0, b1)):
        down = jnp.concatenate([ref[x] for x in range(2)], axis=0)
        y = y + dot_nn(act[:, 2 * c * width : 2 * (c + 1) * width], down) * valid
    out[...] = y.astype(BF16)


def layer_output(meta, x1, act, w, waits, carry, block=512):
    rows, width = x1.shape
    by_row = lambda cols: pl.BlockSpec((block, cols), lambda i, m: (i, 0))
    return call(
        layer_out_kernel,
        "layer_out",
        rows // block,
        [by_row(width), by_row(act.shape[1]), whole(w[0]), whole(w[1])],
        [by_row(width)],
        [jax.ShapeDtypeStruct((rows, width), BF16)],
        [],
        (meta, x1, act, *w),
        waits,
        carry,
    )


def attn_bwd_kernel(meta, qkv, xhat, lse, dattn, wpad, wf, dqkv, grads, da32, gw, gsum, *, own, shards):
    i = pl.program_id(0)
    rows = dattn.shape[0]
    width = wf.shape[0]

    @pl.when(i == 0)
    def _():
        da32[:rows] = dattn[...].astype(F32)
        da32[rows:] = jnp.zeros((da32.shape[0] - rows, PAIR_PAD), F32)
        gw[...] = jnp.zeros(gw.shape, F32)
        gsum[...] = jnp.zeros(gsum.shape, F32)

    start = meta[i]

    def work(length, padded):
        da = load_rows(da32, start, padded)
        if length < padded:
            keep = lax.broadcasted_iota(jnp.int32, (padded, 1), 0) < length
            da = jnp.where(keep, da, 0.0)
        da = da.astype(BF16)
        def cut(ref, part, h):
            at = part * PAIR_PAD + h * HEAD_PAD
            return ref[0, :padded, at : at + HEAD_PAD]

        heads = range(PAIR)
        das = [da[:, h * HEAD_PAD : (h + 1) * HEAD_PAD] for h in heads]
        scores = [dot_nt(cut(qkv, 1, h), cut(qkv, 0, h)) for h in heads]
        dps = [dot_nt(cut(qkv, 2, h), das[h]) for h in heads]
        ps, dss = [], []
        for h in heads:
            p = jnp.exp2(scores[h] * EXP_SCALE - lse[0, h : h + 1, :padded])
            if length < padded:
                key = lax.broadcasted_iota(jnp.int32, p.shape, 0)
                p = jnp.where(key < length, p, 0.0)
            mean = jnp.sum(p * dps[h], axis=0, keepdims=True)
            dss.append((p * (dps[h] - mean)).astype(BF16))
            ps.append(p.astype(BF16))
        parts = [[dot_tn(dss[h], cut(qkv, 1, h)) * SCALE for h in heads]]
        parts += [[dot_nn(dss[h], cut(qkv, 0, h)) * SCALE for h in heads]]
        parts += [[dot_nn(ps[h], das[h]) for h in heads]]
        d = []
        for part in range(3):
            value = jnp.concatenate(parts[part], axis=1)
            at = part * PAIR_PAD
            if part != 1:
                gsum[0:1, at : at + PAIR_PAD] += jnp.sum(value, axis=0, keepdims=True)
            d.append(value.astype(BF16))
        d = jnp.concatenate(d, axis=1)
        dqkv[0, :padded, :] = d
        gw[...] += dot_tn(xhat[0, :padded, :], d)
        gsum[1:2, :] += jnp.sum(d.astype(F32), axis=0, keepdims=True)

    by_group(meta[groups_at(meta) + i], work)

    @pl.when(i == pl.num_programs(0) - 1)
    def _():
        w = wpad[...].astype(F32)
        raw = gw[...]
        col = gsum[1:2, :]
        gain_term = jnp.sum(raw * w, axis=1, keepdims=True)
        bias_term = jnp.sum(col * w, axis=1, keepdims=True)
        vec = wf[:, 3 * PAIR_DIM :].astype(F32)
        main = unpad_heads((raw * vec[:, 0:1] + vec[:, 1:2] * col).astype(BF16))
        put_blocks(grads, main, 0, shards)
        q_sum = unpad_heads(gsum[0:1, :PAIR_PAD])
        v_sum = unpad_heads(gsum[0:1, 2 * PAIR_PAD :])
        gap = jnp.zeros((1, width - PAIR_DIM), F32)
        for c in range(2):

            @pl.when(core_of(meta) == (c if own else 1 - c))
            def _():
                rows_of = [jnp.concatenate([gap, t] if c else [t, gap], axis=1) for t in (q_sum, v_sum)]
                rows_of = [jnp.zeros((2, width), F32)] + rows_of + [jnp.zeros((VEC - 4, width), F32)]
                sums = jnp.concatenate(rows_of, axis=0).T
                lane = lax.broadcasted_iota(jnp.int32, sums.shape, 1)
                tail = jnp.where(lane == 0, gain_term, jnp.where(lane == 1, bias_term, sums))
                put_blocks(grads, tail[:, :VEC_PAIR].astype(BF16), 3 * PAIR_DIM, shards)


def attn_bwd(meta, qkv, xhat, lse, dattn, wpad, wf, own, shards, waits, carry):
    rows = dattn.shape[0]
    width = wf.shape[0]
    cols = 3 * PAIR_PAD
    out_shape = [jax.ShapeDtypeStruct(qkv.shape, BF16), jax.ShapeDtypeStruct(wf.shape, BF16)]
    in_specs = [slot_block(cols), slot_block(width), pl.BlockSpec((1, 8, 512), lambda i, m: (i, 0, 0))]
    in_specs += [whole(dattn), whole(wpad), whole(wf)]
    scratch = [
        pltpu.VMEM((rows + ROW_PAD, PAIR_PAD), F32),
        pltpu.VMEM((width, cols), F32),
        pltpu.VMEM((8, cols), F32),
    ]
    args = (meta, qkv, xhat, lse, dattn, wpad, wf)
    kernel = partial(attn_bwd_kernel, own=own, shards=shards)
    out_specs = [slot_block(cols), whole(wf)]
    grid = groups_at(meta)
    return call(kernel, "attn_bwd", grid, in_specs, out_specs, out_shape, scratch, args, waits, carry)


def input_grad_kernel(meta, tok, d0, d1, w0, w1, wf, dx1, out, tok32, bias):
    i = pl.program_id(0)
    rows, width = tok.shape

    @pl.when(i == 0)
    def _():
        tok32[:rows] = tok[...].astype(F32)
        tok32[rows:] = jnp.zeros((tok32.shape[0] - rows, width), F32)
        bias[...] = wf[:, 3 * PAIR_DIM :].astype(F32).T[0:8]

    start = meta[i]

    def work(length, padded):
        dn = dot_nt(d0[0, :padded, :], w0[...]) + dot_nt(d1[0, :padded, :], w1[...])
        xhat, inverse = row_norm(load_rows(tok32, start, padded))
        dx = row_norm_back(dn * bias[0:1, :], xhat, inverse)
        store_rows(tok32, start, length, dx, slice(None))

    by_group(meta[groups_at(meta) + i], work)

    @pl.when(i == pl.num_programs(0) - 1)
    def _():
        row = lax.broadcasted_iota(jnp.int32, (rows, 1), 0)
        total = dx1[...] + tok32[:rows]
        out[...] = jnp.where(row < rows_used(meta), total, 0.0).astype(BF16)


def input_grad(meta, tokens, d, w, wf, dx1, waits, carry):
    rows, width = tokens.shape
    slot = slot_block(d[0].shape[2])
    in_specs = [whole(tokens), slot, slot] + [whole(t) for t in (*w, wf, dx1)]
    scratch = [pltpu.VMEM((rows + ROW_PAD, width), F32), pltpu.VMEM((8, width), F32)]
    out_shape = [jax.ShapeDtypeStruct((rows, width), BF16)]
    args = (meta, tokens, *d, *w, wf, dx1)
    grid, out_specs = groups_at(meta), [whole(tokens)]
    return call(
        input_grad_kernel, "input_grad", grid, in_specs, out_specs, out_shape, scratch, args, waits, carry
    )


def final_parts(core, own, got, shards):
    size = own.shape[0]
    width = shards * size
    cut = 3 * PAIR_DIM + VEC_PAIR
    low, high = (got, own) if core else (own, got)
    qkv = [t[:, part * PAIR_DIM : (part + 1) * PAIR_DIM] for part in range(3) for t in (low, high)]
    step = (low.shape[1] - cut) // 2
    quarters = [t[:, cut + x * step : cut + (x + 1) * step] for t in (low, high) for x in range(2)]
    extra_at, down_at = width, width + VEC
    extra = [q[:, extra_at:down_at] for q in quarters]
    up = [q[:, n * size : (n + 1) * size] for n in range(shards) for q in quarters]
    down = jnp.concatenate([q[:, down_at:] for q in quarters], axis=0)
    ends = low[:, 3 * PAIR_DIM : cut] + high[:, 3 * PAIR_DIM : cut]
    columns = jnp.concatenate([ends[:, :4], extra[-1][:, : 4 + QUARTERS]], axis=1)
    cat = lambda parts: jnp.concatenate(parts, axis=1)
    return cat(qkv), cat(extra[: width // VEC]), cat(up), down, columns


def finish_kernel(meta, own, got, *outs, shards):
    size = own.shape[0]

    def use(core):
        *mats, columns = final_parts(core, own[...].astype(F32), got[...].astype(F32), shards)
        for mat, out in zip(mats, outs):
            tiles = mat.shape[1] // 128
            for t in range(tiles):
                out[pl.ds(t, mat.shape[0], stride=tiles), :] = mat[:, t * 128 : (t + 1) * 128]
        count = columns.shape[1]
        square = jnp.concatenate([columns, jnp.zeros((size, 128 - count), F32)], axis=1)
        square = jnp.concatenate([square, jnp.zeros((128 - size, 128), F32)], axis=0)
        rows = square.T[:16]
        flat = jnp.concatenate([rows[r : r + 1, :size] for r in range(8, 8 + QUARTERS)], axis=1)
        outs[4][...] = rows
        for n, at in enumerate(range(0, flat.shape[1], 128)):
            piece = flat[:, at : at + 128]
            outs[4][8 + n : 9 + n, : piece.shape[1]] = piece

    for c in range(2):
        pl.when(core_of(meta) == c)(partial(use, c))


def finish(meta, own, got, shards):
    size = own.shape[0]
    width = shards * size
    if size % 16:
        core = core_of(meta) == 1
        own, got = own.astype(F32), got.astype(F32)
        parts = final_parts(0, jnp.where(core, got, own), jnp.where(core, own, got), shards)
        rows = parts[4].T
        return [p.reshape(-1) for p in parts[:4]], rows, rows[8 : 8 + QUARTERS].reshape(-1)
    sizes = [size * 3 * width, size * width, size * QUARTERS * width, size * QUARTERS * width]
    out_shape = [jax.ShapeDtypeStruct((n // 128, 128), F32) for n in sizes + [16 * 128]]
    out_specs = [whole(t) for t in out_shape]
    kernel = partial(finish_kernel, shards=shards)
    outs = call(kernel, "finish", 1, [whole(own), whole(got)], out_specs, out_shape, [], (meta, own, got))
    count = QUARTERS * size
    pieces = [outs[4][8 + n, : min(128, count - at)] for n, at in enumerate(range(0, count, 128))]
    return [t.reshape(-1) for t in outs[:4]], outs[4], jnp.concatenate(pieces)


def turned(shards):
    count = shards.bit_length() - 1
    return [sum(((n >> b) & 1) << (count - 1 - b) for b in range(count)) for n in range(shards)]


def image_table(size_group, assignment, device, slots):
    owned = assignment == device
    rank = jnp.cumsum(owned.astype(jnp.int32)) - 1
    slot = jnp.arange(slots, dtype=jnp.int32)
    here = owned[None, :] & (rank[None, :] == slot[:, None])
    groups = jnp.sum(jnp.where(here, size_group[None, :], 0), axis=1)
    lengths = jnp.where(groups == 0, LENS[0], jnp.where(groups == 1, LENS[1], LENS[2]))
    ends = jnp.sum(jnp.where(slot[None, :] <= slot[:, None], lengths[None, :], 0), axis=1)
    return jnp.concatenate([ends - lengths, groups, ends[-1:], device[None]]).astype(jnp.int32)


def swap(value, axis, bit):
    size = lax.axis_size(axis)
    return lax.ppermute(value, axis, [(i, i ^ bit) for i in range(size)])


def sides_of(bits):
    table = {}
    for axis, those in bits.items():
        for bit in those:
            mine = (lax.axis_index(axis) & bit) // bit
            table[axis, bit] = (mine.astype(jnp.uint32), (1 - mine).astype(jnp.uint32), mine == 1)
    return table


def pick(sides, value, axis, bit, dim):
    mine, theirs, _ = sides[axis, bit]
    keep = lax.dynamic_index_in_dim(value, mine, dim, keepdims=False)
    send = lax.dynamic_index_in_dim(value, theirs, dim, keepdims=False)
    return keep, send


def join(upper, own, other, dim):
    return jnp.stack([jnp.where(upper, other, own), jnp.where(upper, own, other)], axis=dim)


def added(keep, got):
    return (keep.astype(F32) + got.astype(F32)).astype(BF16)


def after(value, *others):
    return lax.optimization_barrier((value, *others))[0]


class Gather:
    def __init__(self, sides, part, keys):
        self.sides, self.part, self.keys, self.have = sides, part, keys, []

    def grow(self, axis, bit, *others, upper=None):
        if others:
            self.part = after(self.part, *others)
        upper = self.sides[axis, bit][2] if upper is None else upper
        dim = sum(self.keys.index(k) < self.keys.index((axis, bit)) for k in self.have)
        self.part = join(upper, self.part, swap(self.part, axis, bit), dim)
        self.have.append((axis, bit))
        return self


def body(
    tokens,
    cotangent,
    size_group,
    assignment,
    ln1_gain,
    ln1_bias,
    w_qkv,
    q_bias,
    v_bias,
    w_proj,
    proj_bias,
    ln2_gain,
    ln2_bias,
    w_up,
    up_bias,
    w_down,
    down_bias,
):
    rows, width = tokens.shape
    shards = lax.axis_size("fsdp")
    size = width // shards
    devices = shards * lax.axis_size("dp")
    device = lax.axis_index("fsdp") * lax.axis_size("dp") + lax.axis_index("dp")
    bits = [1 << b for b in range(shards.bit_length() - 1)]
    far, near, y = bits[2:], bits[1:2], bits[0]
    tail_keys = [("fsdp", b) for b in reversed(bits)]
    sides = sides_of({"dp": (1, 2), "fsdp": bits})
    core, column = sides["dp", 1][0], sides["dp", 2][0]

    vectors = [ln1_gain, ln1_bias, q_bias, v_bias, proj_bias, ln2_gain, ln2_bias, down_bias]
    vectors = jnp.concatenate([jnp.stack(vectors), up_bias.reshape(QUARTERS, size)]).T
    pair = w_qkv.reshape(size, 3, 2, PAIR_DIM)
    pair = lax.dynamic_index_in_dim(pair, core, 2, keepdims=False).reshape(size, 3 * PAIR_DIM)
    pair = jnp.concatenate([pair, vectors[:, :4], jnp.zeros((size, VEC_PAIR - 4), BF16)], axis=1)
    f = Gather(sides, pair, tail_keys)
    w_up, w_down, w_proj, _ = lax.optimization_barrier((w_up, w_down, w_proj, pair))
    quarter = 2 * core + column
    extra = [w_proj.reshape(size, width), vectors[:, 4:], jnp.zeros((size, VEC - 4 - QUARTERS), BF16)]
    extra = lax.dynamic_slice_in_dim(jnp.concatenate(extra, axis=1), quarter * VEC, VEC, 1)
    up = lax.dynamic_index_in_dim(w_up.reshape(size, shards, QUARTERS, size), quarter, 2, False)
    part_a = jnp.concatenate([up.reshape(size, width), extra], axis=1)
    part_b = lax.dynamic_index_in_dim(w_down.reshape(QUARTERS, size, width), quarter, 0, False)
    ab = Gather(sides, jnp.concatenate([part_a, part_b], axis=1), tail_keys)

    for bit in far:
        f.grow("fsdp", bit)
    for bit in far:
        ab.grow("fsdp", bit)
    for bit in near:
        f.grow("fsdp", bit)
    for bit in near:
        ab.grow("fsdp", bit)
    size_group, assignment, _ = lax.optimization_barrier((size_group, assignment, f.part))
    table = image_table(size_group, assignment, device, size_group.shape[0] // devices)
    f.grow("fsdp", y)
    own = f.part.reshape(width, -1)
    cut = width + VEC
    keys = [("dp", 2)] + tail_keys
    a, b = Gather(sides, ab.part[..., :cut], keys), Gather(sides, ab.part[..., cut:], keys)
    a.have, b.have = list(ab.have), list(ab.have)
    a.grow("dp", 2)
    b.grow("fsdp", y)
    wf = (own, swap(own, "dp", 1))

    upper = jnp.stack([sides["fsdp", y][2], sides["dp", 2][2]])
    upper = jnp.broadcast_to(upper[:, None, None], (2, 8, cut)).astype(jnp.int32)
    table, sides, upper = lax.optimization_barrier((table, sides, upper))
    attn0, attn1, qkv0, qkv1, xhat, lse0, lse1, wpad0, wpad1, upper = attn_fwd(
        table, tokens, wf, (), (upper,)
    )
    a.grow("fsdp", y, upper=upper[0, 0] != 0)
    b.grow("dp", 2, upper=upper[1, 0, :width] != 0)
    wa, wb = a.part.reshape(2, width, cut), b.part.reshape(2, width, width)
    w = (wa, swap(wa, "dp", 1), wb, swap(wb, "dp", 1))
    x1, act, dx1, dattn0, dattn1, keep_a, send_a, keep_b, send_b = mlp(
        table, tokens, cotangent, (attn0, attn1), w, shards
    )

    def by_bits(value, lead):
        if size % 16:
            value = value.reshape(value.shape[:lead] + (2,) * len(bits) + (size, value.shape[-1]))
            order = [lead + b for b in reversed(range(len(bits)))]
            return value.transpose(*range(lead), *order, *range(lead + len(bits), value.ndim))
        return value.reshape(value.shape[:lead] + (2,) * len(bits) + (size, value.shape[-1]))

    def halves_of_b(value):
        if size % 16:
            value = value.swapaxes(0, 1).reshape(2, width, width)
            return by_bits(value, 1).swapaxes(0, 1)
        return value.reshape((2, 2) + (2,) * (len(bits) - 1) + (size, width))

    got_a, got_b = swap(send_a, "dp", 1), swap(send_b, "dp", 1)
    d1, send_g, keep_a, keep_b = attn_bwd(
        table, qkv1, xhat, lse1, dattn1, wpad1, wf[1], False, shards, (send_a, send_b), (keep_a, keep_b)
    )
    got_g = swap(send_g, "dp", 1)
    keep_a, send_a = pick(sides, by_bits(added(keep_a, got_a), 1), "dp", 2, 0)
    keep_b, send_b = pick(sides, halves_of_b(added(keep_b, got_b)), "fsdp", y, 0)
    got_a, got_b = swap(send_a, "dp", 2), swap(send_b, "fsdp", y)
    d0, keep_g, keep_a, keep_b = attn_bwd(
        table, qkv0, xhat, lse0, dattn0, wpad0, wf[0], True, shards, (send_a, send_b, send_g), (keep_a, keep_b)
    )
    part = jnp.concatenate([by_bits(added(keep_g, got_g), 0), added(keep_a, got_a)], axis=-1)
    keep, send = pick(sides, part, "fsdp", y, 0)
    keep_b, send_b = pick(sides, added(keep_b, got_b), "dp", 2, 0)
    got, got_b = swap(send, "fsdp", y), swap(send_b, "dp", 2)
    grads_of = (table, tokens, (d0, d1), (wpad0, wpad1), wf[0], dx1)
    grad_input, keep, keep_b = input_grad(*grads_of, (send, send_b), (keep, keep_b))
    part = jnp.concatenate([added(keep, got), added(keep_b, got_b)], axis=-1)
    for count, bit in enumerate(bits[1:]):
        keep, send = pick(sides, part, "fsdp", bit, 0)
        got = swap(send, "fsdp", bit)
        if count == 0:
            layer_out, keep = layer_output(table, x1, act, w[2:], (send,), (keep,))
        part = added(keep, got)
    got = swap(part, "dp", 2)
    cut = keep_g.shape[-1]
    part_g = added(part[:, :cut], got[:, :cut])
    low, high = part[:, cut:], got[:, cut:]
    upper = sides["dp", 2][2]
    part = [part_g, jnp.where(upper, high, low), jnp.where(upper, low, high)]
    part = jnp.concatenate(part, axis=1)
    flat, vectors, up_bias = finish(table, part, swap(part, "dp", 1), shards)
    g = [vectors[r, :size] for r in range(8)] + [up_bias]
    qkv, proj, up, down = flat
    return (
        layer_out, grad_input, g[0], g[1], qkv, g[2], g[3], proj, g[4], g[5], g[6], up, g[8], down, g[7]
    )


def solution(mesh):
    rows = P(("fsdp", "dp"), None)
    flat = P("fsdp")
    return jax.shard_map(
        body,
        mesh=mesh,
        in_specs=(rows, rows, P(), P()) + (flat,) * 13,
        out_specs=(rows, rows) + (flat,) * 13,
        check_vma=False,
    )
```
